32 devices in a mesh: dp: 8 (over z, y), tensor: 4 (over x, core).
Axes of the slice: x: 2, y: 2, z: 4, core: 2. Of those that a mesh axis runs over, the one named last changes fastest.
Arguments:
- questions: bfloat16 [96, 64, 768], P(('dp', 'tensor')), may hold values from -6 to 6
- passages: bfloat16 [96, 256, 768], P(('dp', 'tensor')), may hold values from -6 to 6
- question_cotangent: bfloat16 [96, 64, 768], P(('dp', 'tensor')), may hold values from -6 to 6
- passage_cotangent: bfloat16 [96, 256, 768], P(('dp', 'tensor')), may hold values from -6 to 6
- positives: int32 [96, 4], P(('dp', 'tensor')), may hold values from 0 to 95, as said below
- positive_counts: int32 [96], P(('dp', 'tensor')), may hold values from 1 to 4, as said below
- attention_in: bfloat16 [2, 3, 768, 768], P(None, None, None, 'tensor'), may hold values from -0.21875 to 0.21875
- attention_bias: bfloat16 [2, 2, 768], P(None, None, 'tensor'), may hold values from -2 to 2
- attention_out: bfloat16 [2, 768, 768], P(None, 'tensor'), may hold values from -1.75 to 1.75
- branch_biases: bfloat16 [2, 2, 768], replicated, may hold values from -2 to 2
- norm_gains: bfloat16 [2, 2, 768], replicated, may hold values from 0.5 to 1.5
- norm_shifts: bfloat16 [2, 2, 768], replicated, may hold values from -2 to 2
- up_weight: bfloat16 [2, 768, 3072], P(None, None, 'tensor'), may hold values from -0.21875 to 0.21875
- up_bias: bfloat16 [2, 3072], P(None, 'tensor'), may hold values from -2 to 2
- down_weight: bfloat16 [2, 3072, 768], P(None, 'tensor'), may hold values from -0.15625 to 0.15625
Outputs:
- question_out: bfloat16 [96, 64, 768], P(('dp', 'tensor'))
- passage_out: bfloat16 [96, 256, 768], P(('dp', 'tensor'))
- question_losses: float32 [96], P(('dp', 'tensor'))
- question_gradient: bfloat16 [96, 64, 768], P(('dp', 'tensor'))
- passage_gradient: bfloat16 [96, 256, 768], P(('dp', 'tensor'))
- attention_in_gradient: float32 [2, 3, 768, 768], P(None, None, None, 'tensor')
- attention_bias_gradient: float32 [2, 2, 768], P(None, None, 'tensor')
- attention_out_gradient: float32 [2, 768, 768], P(None, 'tensor')
- branch_biases_gradient: float32 [2, 2, 768], replicated
- norm_gains_gradient: float32 [2, 2, 768], replicated
- norm_shifts_gradient: float32 [2, 2, 768], replicated
- up_weight_gradient: float32 [2, 768, 3072], P(None, None, 'tensor')
- up_bias_gradient: float32 [2, 3072], P(None, 'tensor')
- down_weight_gradient: float32 [2, 3072, 768], P(None, 'tensor')
The draws below stay inside these ranges and needn't reach their ends.
Inputs may be any that keep to these rules, and one draw needn't show every extreme that they name: `positive_counts`: some question has 4 positives and another has 1. `positives`: the first positive_counts[i] entries of row i are distinct passage numbers; the remaining entries are 0 and name nothing.
All inputs are finite; a program needn't handle non-finite values.
Results may differ from the reference program's by a relative error of at most 0.02.
Values may be sent and summed in bfloat16 or wider, within the bound.
A program may use at most 192 MiB of HBM per device.

```python
import jax
import jax.numpy as jnp
from jax import lax

D = 768
HEADS = 12
FF = 3072
HD = 64
LQ = 64
LP = 256
MAXPOS = 4
QSH = 3
PSH = 3
NQ = 96
NP = 96


def count_draw(base_key):
    live_counts = jax.random.randint(base_key, (NQ,), 1, MAXPOS + 1)
    chosen = jax.random.randint(jax.random.fold_in(base_key, 101), (), 0, NQ)
    offset = jax.random.randint(jax.random.fold_in(base_key, 102), (), 1, NQ)
    single = (chosen + offset) % NQ
    row_index = jnp.arange(NQ)
    live_counts = jnp.where(row_index == chosen, MAXPOS, live_counts)
    live_counts = jnp.where(row_index == single, 1, live_counts)
    return live_counts.astype(jnp.int32)


def draw_positive_counts(key, part):
    live_counts = count_draw(key)
    return live_counts


def draw_positives(key, part):
    live_counts = count_draw(key)
    key = jax.random.fold_in(key, 7)
    rank_keys = jax.random.randint(key, (NQ, NP), 0, 1 << 18) * NP + jnp.arange(NP)[None, :]
    device_total = NQ // QSH
    owner = jnp.arange(NQ) // QSH
    far_owner = (owner + device_total // 2) % device_total
    far_pick = far_owner * PSH + jax.random.randint(jax.random.fold_in(key, 11), (NQ,), 0, PSH)
    use_far = jax.random.randint(jax.random.fold_in(key, 13), (NQ,), 0, 2) == 1
    boosted = (jnp.arange(NP)[None, :] == far_pick[:, None]) & use_far[:, None]
    rank_keys = jnp.where(boosted, (1 << 18) * NP + NP, rank_keys)
    chosen = lax.top_k(rank_keys, MAXPOS)[1]
    slot_live = jnp.arange(MAXPOS)[None, :] < live_counts[:, None]
    return jnp.where(slot_live, chosen, 0).astype(jnp.int32)


def levels(own_key, extent, cuts, low, high):
    factor_of = 1.0
    for axis_at, shards_of in cuts:
        steps = jax.random.uniform(jax.random.fold_in(jax.random.fold_in(own_key, 6), axis_at), (shards_of,), jnp.float32, low / len(cuts), high / len(cuts))
        factor_of = factor_of * jnp.repeat(jnp.exp(steps), extent[axis_at] // shards_of).reshape((-1,) + (1,) * (len(extent) - 1 - axis_at))
    return factor_of


def scatter_about(rng, shape, scale, most, cuts=(), kind=jnp.bfloat16):
    factor_of = levels(rng, shape, cuts, -0.22, 0.18) if cuts else 1.0
    result = jax.random.normal(rng, shape, jnp.float32) * scale * factor_of
    return jnp.minimum(jnp.maximum(result, -most), most).astype(kind)


def setup_inputs(seed: int = 0) -> dict:
    splits = jax.random.split(jax.random.key(seed), 16)
    questions = scatter_about(splits[0], (NQ, LQ, D), 1.0, 6.0, ((0, 32),))
    passages = scatter_about(splits[1], (NP, LP, D), 1.0, 6.0, ((0, 32),))
    question_cotangent = scatter_about(splits[2], (NQ, LQ, D), 1.0, 6.0, ((0, 32),))
    passage_cotangent = scatter_about(splits[3], (NP, LP, D), 1.0, 6.0, ((0, 32),))
    positives = draw_positives(jax.random.fold_in(splits[15], 71), 0)
    positive_counts = draw_positive_counts(jax.random.fold_in(splits[15], 71), 0)
    attention_in = scatter_about(splits[6], (2, 3, D, D), D ** -0.5, 0.21875, ((3, 4),))
    attention_bias = scatter_about(splits[7], (2, 2, D), 0.3, 2.0, ((2, 4),))
    attention_out = scatter_about(splits[8], (2, D, D), (max(D // 64, 4)) ** -0.5, 1.75, ((1, 4),))
    branch_biases = scatter_about(splits[9], (2, 2, D), 0.3, 2.0)
    norm_gains = jnp.clip(1.0 + 0.1 * jax.random.normal(splits[10], (2, 2, D), jnp.float32), 0.5, 1.5).astype(jnp.bfloat16)
    norm_shifts = scatter_about(splits[11], (2, 2, D), 0.3, 2.0)
    up_weight = scatter_about(splits[12], (2, D, FF), D ** -0.5, 0.21875, ((2, 4),))
    up_bias = scatter_about(splits[13], (2, FF), 0.3, 2.0, ((1, 4),))
    down_weight = scatter_about(splits[14], (2, FF, D), (FF // 2) ** -0.5, 0.15625, ((1, 4),))
    return dict(questions=questions, passages=passages, question_cotangent=question_cotangent, passage_cotangent=passage_cotangent, positives=positives, positive_counts=positive_counts, attention_in=attention_in, attention_bias=attention_bias, attention_out=attention_out, branch_biases=branch_biases, norm_gains=norm_gains, norm_shifts=norm_shifts, up_weight=up_weight, up_bias=up_bias, down_weight=down_weight)


@jax.custom_vjp
def low(v):
    return lax.optimization_barrier(v.astype(jnp.bfloat16)).astype(jnp.float32)

@jax.custom_vjp
def low_back(v):
    return v

def low_keep(v):
    return (low(v), None)

def low_pass(kept, grad):
    return (grad,)

def back_keep(v):
    return (v, None)

def back_low(kept, grad):
    return (low(grad),)
low.defvjp(low_keep, low_pass)
low_back.defvjp(back_keep, back_low)
highest = lax.Precision.HIGHEST
norm_epsilon = 1e-12
block_sequences = 16

def layer_norm(summed, gain_row, shift_row):
    centered = summed - lax.optimization_barrier(jnp.mean(summed, axis=-1, keepdims=True))
    spread = lax.optimization_barrier(jnp.mean(centered * centered, axis=-1, keepdims=True))
    return centered * lax.rsqrt(spread + norm_epsilon) * gain_row + shift_row

def encode_block(params, tokens):
    attention_in, attention_bias, attention_out, branch_biases, norm_gains, norm_shifts, up_weight, up_bias, down_weight = params
    batch, length, model_width = tokens.shape
    projected = jnp.einsum('bld,cde->cble', tokens, attention_in, precision=highest)
    queries = low_back(low(projected[0] + attention_bias[0])).reshape(batch, length, HEADS, HD)
    key_rows = low_back(low(projected[1])).reshape(batch, length, HEADS, HD)
    values = low_back(low(projected[2] + attention_bias[1])).reshape(batch, length, HEADS, HD)
    scores = low_back(jnp.einsum('bqhe,bkhe->bhqk', queries, key_rows, precision=highest) * HD ** (-0.5))
    attention_weights = low(jax.nn.softmax(scores, axis=-1))
    mixed_rows = jnp.einsum('bhqk,bkhe->bqhe', attention_weights, values, precision=highest)
    mixed_rows = low_back(low(mixed_rows.reshape(batch, length, model_width)))
    attended = low_back(jnp.einsum('ble,ed->bld', mixed_rows, attention_out, precision=highest) + branch_biases[0])
    normed = layer_norm(tokens + attended, norm_gains[0], norm_shifts[0])
    pre_active = low_back(jnp.einsum('bld,df->blf', low(normed), up_weight, precision=highest) + up_bias)
    active = low(jax.nn.gelu(pre_active, approximate=False))
    fed_rows = low_back(jnp.einsum('blf,fd->bld', active, down_weight, precision=highest) + branch_biases[1])
    return layer_norm(normed + fed_rows, norm_gains[1], norm_shifts[1])

def encode(params, tokens):
    count_all, length, model_width = tokens.shape
    blocks = tokens.reshape(count_all // block_sequences, block_sequences, length, model_width)
    checked = jax.checkpoint(encode_block)
    outputs = lax.map(lambda block_in: checked(params, block_in), blocks)
    return outputs.reshape(tokens.shape)

def contrast(question_cls, passage_cls, positives, positive_counts):
    score_scale = 2.7 * D ** (-0.5)
    scores = low_back(jnp.dot(low(question_cls), low(passage_cls).T, precision=highest) * score_scale)
    slot_live = jnp.arange(MAXPOS)[None, :] < positive_counts[:, None]
    matches = (positives[:, :, None] == jnp.arange(NP)[None, None, :]) & slot_live[:, :, None]
    positive_marks = lax.optimization_barrier(jnp.sum(matches.astype(jnp.float32), axis=1))
    return jax.nn.logsumexp(scores, axis=1) - jax.nn.logsumexp(scores, axis=1, b=positive_marks)

def reference(questions, passages, question_cotangent, passage_cotangent, positives, positive_counts, attention_in, attention_bias, attention_out, branch_biases, norm_gains, norm_shifts, up_weight, up_bias, down_weight):
    parameters = tuple((array_item.astype(jnp.float32) for array_item in (attention_in, attention_bias, attention_out, branch_biases, norm_gains, norm_shifts, up_weight, up_bias, down_weight)))

    def forward(parameters, question_in, passage_in):
        question_params = tuple((array_item[0] for array_item in parameters))
        passage_params = tuple((array_item[1] for array_item in parameters))
        question_out = encode(question_params, question_in)
        passage_out = encode(passage_params, passage_in)
        losses = contrast(question_out[:, 0], passage_out[:, 0], positives, positive_counts)
        return (question_out, passage_out, losses)
    (question_out, passage_out, losses), pullback = jax.vjp(forward, parameters, questions.astype(jnp.float32), passages.astype(jnp.float32))
    gradients, question_gradient, passage_gradient = pullback((question_cotangent.astype(jnp.float32), passage_cotangent.astype(jnp.float32), jnp.ones_like(losses)))
    return (question_out.astype(jnp.bfloat16), passage_out.astype(jnp.bfloat16), losses, question_gradient.astype(jnp.bfloat16), passage_gradient.astype(jnp.bfloat16), gradients[0], gradients[1], gradients[2], gradients[3], gradients[4], gradients[5], gradients[6], gradients[7], gradients[8])
```

```python
import functools

import jax
import jax.numpy as jnp
from jax import lax
from jax.experimental import pallas as pl
from jax.experimental.pallas import tpu as pltpu
from jax.sharding import PartitionSpec as P

D = 768
MESH = pl.DeviceIdType.MESH
bf16, f32 = jnp.bfloat16, jnp.float32
VM = pl.BlockSpec(memory_space=pltpu.VMEM)
ANY = pl.BlockSpec(memory_space=pl.ANY)
SDS = jax.ShapeDtypeStruct


def place():
    dp, t = lax.axis_index("dp"), lax.axis_index("tensor")
    return dict(dp=dp, t=t, x=lax.div(t, 2), c=lax.rem(t, 2), y=lax.rem(dp, 2),
                z=lax.rem(lax.div(dp, 2), 4), o=lax.div(dp, 8))


def device(p, c=None, x=None, y=None, z=None, o=None):
    g = lambda v, k: p[k] if v is None else v
    return (g(o, "o") * 8 + g(z, "z") * 2 + g(y, "y"), g(x, "x") * 2 + g(c, "c"))


def greet(peers):
    bar = pltpu.get_barrier_semaphore()
    for q in peers:
        pl.semaphore_signal(bar, inc=1, device_id=q, device_id_type=MESH)
    pl.semaphore_wait(bar, len(peers))


def remote(src, dst, ssem, rsem, dev):
    return pltpu.make_async_remote_copy(src, dst, ssem, rsem, device_id=dev, device_id_type=MESH)


R = 64
MACRO = 256
HALF = D // 2
MACROS = 18
STEPS = MACROS * 4 + 1
LAG = dict(c=2, x=2, y=2, z=2, a=2)


def sum_kernel(outer, *refs):
    ops, refs = refs[:17], refs[17:]
    (out_ref, small_ref, made, crecv, xsend, xkeep, xrecv, ysend, ykeep, yrecv, zsend, zrecv, fin, osend, orecv,
     c_ss, c_rs, x_ss, x_rs, y_ss, y_rs, z_ss, z_rs, a_ss, a_rs, o_ss, o_rs, w_ss, w_rs, l_sem, t_ss, t_rs) = refs
    first_ref, per_encoder = ops[0], (ops[9:17], ops[1:9])
    p = place()
    sib, xp, yp = device(p, c=1 - p["c"]), device(p, x=1 - p["x"]), device(p, y=1 - p["y"])
    zs = [lax.rem(p["z"] + j, 4) for j in (1, 2, 3)]
    zp = [device(p, z=v) for v in zs]
    op = [device(p, o=lax.rem(p["o"] + j, outer)) for j in range(1, outer)]
    diag = device(p, x=1 - p["x"], c=1 - p["c"])
    greet([sib, xp, yp, diag] + zp + op)
    dc, dx, dy, dz, da = (LAG[k] for k in "cxyza")
    lx = dc
    ly = lx + dx
    lz = ly + dy
    la = lz + dz
    lf = la + da
    m16 = lambda v, n: pl.ds(pl.multiple_of(v, 16), n)

    def made_at(u, c):
        return made.at[lax.rem(lax.div(u, 4), 2), :, c, m16(lax.rem(u, 4) * R, R)]

    def c_copy(u):
        k = lax.rem(u, 2 * dc)
        return remote(made_at(u, 1 - p["c"]), crecv.at[k], c_ss.at[k], c_rs.at[k], sib)

    def x_copy(u):
        k = lax.rem(u, 2 * dx)
        return remote(xsend.at[k], xrecv.at[k], x_ss.at[k], x_rs.at[k], xp)

    def y_copy(u):
        k = lax.rem(u, 2 * dy)
        return remote(ysend.at[k], yrecv.at[k], y_ss.at[k], y_rs.at[k], yp)

    def z_copy(u, j):
        k = lax.rem(u, 2 * dz)
        return remote(zsend.at[k, m16(zs[j] * 16, 16)], zrecv.at[k, 2 - j], z_ss.at[k, j], z_rs.at[k, 2 - j], zp[j])

    def z_wait(u):
        k = lax.rem(u, 2 * dz)
        for j in range(3):
            c = remote(zsend.at[k, m16(0, 16)], zrecv.at[k, j], z_ss.at[k, j], z_rs.at[k, j], zp[j])
            c.wait_send()
            c.wait_recv()

    def a_copy(u, j):
        k = lax.rem(u, 3 * da)
        a = fin.at[k, m16(p["z"] * 16, 16)]
        return remote(a, a, a_ss.at[k, j], a_rs.at[k, 2 - j], zp[j])

    def a_wait(u):
        k = lax.rem(u, 3 * da)
        for j in range(3):
            a = fin.at[k, m16(0, 16)]
            c = remote(a, a, a_ss.at[k, j], a_rs.at[k, j], zp[j])
            c.wait_send()
            c.wait_recv()

    def target(u):
        m = lax.div(u, 4)
        g = lax.div(m, 3)
        spot_ = jnp.where(m == MACROS, MACROS, (lax.rem(g, 3) * 2 + 1 - lax.div(g, 3)) * 3 + lax.rem(m, 3))
        return out_ref.at[spot_, m16(lax.rem(u, 4) * R, R), pl.ds(pl.multiple_of(p["y"] * HALF, 128), HALF)]

    def w_remote(u):
        k = lax.rem(u, 3 * da)
        return remote(fin.at[k], target(u), w_ss.at[k], w_rs.at[k], yp)

    def w_local(u):
        k = lax.rem(u, 3 * da)
        return pltpu.make_async_copy(fin.at[k], target(u), l_sem.at[k])

    def when(u, fn):
        @pl.when(jnp.logical_and(u >= 0, u < STEPS))
        def _():
            fn(u)

    def finish(u):
        a_wait(u)
        w_remote(u).start()
        w_local(u).start()

    def finished(u):
        c = w_remote(u)
        c.wait_send()
        c.wait_recv()
        w_local(u).wait()

    def take_z(u):
        z_wait(u)
        k = lax.rem(u, 2 * dz)
        mine = m16(p["z"] * 16, 16)
        v = zsend[k, mine].astype(f32)
        for j in range(3):
            v = v + zrecv[k, j].astype(f32)
        if outer > 1:
            osend[...] = v.astype(bf16)
            for j in range(outer - 1):
                remote(osend, orecv.at[outer - 2 - j], o_ss.at[j], o_rs.at[outer - 2 - j], op[j]).start()
            for j in range(outer - 1):
                c = remote(osend, orecv.at[j], o_ss.at[j], o_rs.at[j], op[j])
                c.wait_send()
                c.wait_recv()
            v = osend[...].astype(f32)
            for j in range(outer - 1):
                v = v + orecv[j].astype(f32)
        fin[lax.rem(u, 3 * da), mine] = v.astype(bf16)
        for j in range(3):
            a_copy(u, j).start()

    def take_y(u):
        c = y_copy(u)
        c.wait_send()
        c.wait_recv()
        k = lax.rem(u, 2 * dy)
        zsend[lax.rem(u, 2 * dz)] = (ykeep[k] + yrecv[k].astype(f32)).astype(bf16)
        for j in range(3):
            z_copy(u, j).start()

    def take_x(u):
        c = x_copy(u)
        c.wait_send()
        c.wait_recv()
        k = lax.rem(u, 2 * dx)
        ky = lax.rem(u, 2 * dy)
        ysend[ky] = (xkeep[k, 1 - p["y"]] + xrecv[k, 1 - p["y"]].astype(f32)).astype(bf16)
        y_copy(u).start()
        ykeep[ky] = xkeep[k, p["y"]] + xrecv[k, p["y"]].astype(f32)

    def take_c(u):
        c = c_copy(u)
        c.wait_send()
        c.wait_recv()
        k = lax.rem(u, 2 * dc)
        kx = lax.rem(u, 2 * dx)
        o = 1 - p["x"]
        own = lambda x: made[lax.rem(lax.div(u, 4), 2), x, p["c"], m16(lax.rem(u, 4) * R, R)].astype(f32)
        v = (own(o) + crecv[k, o].astype(f32)).astype(bf16)
        xsend[kx, 0] = v[:, :HALF]
        xsend[kx, 1] = v[:, HALF:]
        x_copy(u).start()
        v = own(p["x"]) + crecv[k, p["x"]].astype(f32)
        xkeep[kx, 0] = v[:, :HALF]
        xkeep[kx, 1] = v[:, HALF:]

    def make(m):
        slot = lax.rem(m, 2)
        g = lax.div(m, 3)
        r = lax.rem(m, 3)
        for e in (0, 1):
            gate_, df, hb, du, o, da_, dqkv, x_ = per_encoder[e]

            @pl.when(g == (1 - e) * 3)
            def _():
                cols = pl.ds(pl.multiple_of(r * MACRO, 128), MACRO)
                for t in range(4):
                    made[slot, t // 2, t % 2] = dot(gate_[t, :, cols], df[...], 0, 0).astype(bf16)

            @pl.when(g == (1 - e) * 3 + 1)
            def _():
                cols = pl.ds(pl.multiple_of(r * MACRO, 128), MACRO)
                for t in range(4):
                    made[slot, t // 2, t % 2] = dot(hb[:, cols], du[t], 0, 0).astype(bf16)

            for rr in range(3):
                @pl.when(m == ((1 - e) * 3 + 2) * 3 + rr)
                def _():
                    for t in range(4):
                        at = rr * MACRO
                        while at < (rr + 1) * MACRO:
                            j, off = at // 192, at % 192
                            n = min(192 - off, (rr + 1) * MACRO - at)
                            src = dqkv[j * D + t * 192 + off : j * D + t * 192 + off + n, :] if j < 3 else o[t * 192 + off : t * 192 + off + n, :]
                            made[slot, t // 2, t % 2, at - rr * MACRO : at - rr * MACRO + n] = dot(
                                src, x_[...] if j < 3 else da_[...], 1, 0).astype(bf16)
                            at += n

        @pl.when(m == MACROS)
        def _():
            made[slot, :, :, 0:R] = first_ref[...]

    def fetch(u):
        @pl.when(lax.rem(u, 4) == 0)
        def _():
            make(lax.div(u, 4))

        c_copy(u).start()

    def step(s, _):
        when(s - lf - da, finished)
        when(s - lf, finish)
        when(s - la, take_z)
        when(s - lz, take_y)
        when(s - ly, take_x)
        when(s - lx, take_c)
        when(s, fetch)
        return _

    lax.fori_loop(0, STEPS + lf + da, step, 0)
    x, c = p["x"], p["c"]
    own = out_ref.at[MACROS, pl.ds(0, 16)]
    sends = [remote(own, small_ref.at[x, c], t_ss.at[i], t_rs.at[i], dev) for i, dev in enumerate((sib, xp, diag))]
    for cp in sends:
        cp.start()
    mine = pltpu.make_async_copy(own, small_ref.at[x, c], l_sem.at[0])
    mine.start()
    mine.wait()
    for i, (a, b) in enumerate(((x, 1 - c), (1 - x, c), (1 - x, 1 - c))):
        sends[i].wait_send()
        remote(own, small_ref.at[a, b], t_ss.at[i], t_rs.at[i], sib).wait_recv()


def grad_sum(first, per_encoder, dp, cid=3):
    outer = dp // 8
    dma = pltpu.SemaphoreType.DMA
    dc, dx, dy, dz, da = (LAG[k] for k in "cxyza")
    no = max(outer - 1, 1)
    vm = pltpu.VMEM
    args = [first.reshape(2, 2, R, D)] + list(per_encoder[1]) + list(per_encoder[0])
    return pl.pallas_call(
        functools.partial(sum_kernel, outer),
        out_shape=(SDS((MACROS + 1, MACRO, D), bf16), SDS((2, 2, 16, D), bf16)),
        in_specs=[VM] * len(args),
        out_specs=(ANY, VM),
        scratch_shapes=[
            vm((2, 2, 2, MACRO, D), bf16), vm((2 * dc, 2, R, D), bf16),
            vm((2 * dx, 2, R, HALF), bf16), vm((2 * dx, 2, R, HALF), f32), vm((2 * dx, 2, R, HALF), bf16),
            vm((2 * dy, R, HALF), bf16), vm((2 * dy, R, HALF), f32), vm((2 * dy, R, HALF), bf16),
            vm((2 * dz, R, HALF), bf16), vm((2 * dz, 3, 16, HALF), bf16),
            vm((3 * da, R, HALF), bf16),
            vm((16, HALF), bf16), vm((no, 16, HALF), bf16),
            dma((2 * dc,)), dma((2 * dc,)), dma((2 * dx,)), dma((2 * dx,)),
            dma((2 * dy,)), dma((2 * dy,)), dma((2 * dz, 3)), dma((2 * dz, 3)),
            dma((3 * da, 3)), dma((3 * da, 3)), dma((no,)), dma((no,)),
            dma((3 * da,)), dma((3 * da,)), dma((3 * da,)), dma((3,)), dma((3,)),
        ],
        compiler_params=pltpu.CompilerParams(collective_id=cid, has_side_effects=True, vmem_limit_bytes=60 * 2**20),
    )(*args)


CH = 6
PLAN = ((0, 1), (1, 1), (2, 1), (0, 0), (1, 0), (2, 0))


def gather_kernel(io_ref, up_ref, down_ref, b_ref, out_ref, bias_ref, held, *sems):
    (x_ss, x_rs, y_ss, y_rs, z_ss, z_rs, y2_ss, y2_rs, z2_ss, z2_rs, sib_ss, sib_rs, f_ss, f_rs, b_ss, b_rs, in_sem, back_sem) = sems
    p = place()
    zb = lax.rem(p["z"], 2)
    sib, xp, yp = device(p, c=1 - p["c"]), device(p, x=1 - p["x"]), device(p, y=1 - p["y"])
    zp = device(p, z=p["z"] + 1 - 2 * zb)
    diag = device(p, x=1 - p["x"], c=1 - p["c"])
    greet([sib, xp, yp, zp, diag])
    x, c, y = p["x"], p["c"], p["y"]
    quarter, half = D // 4, D // 8
    rows = lambda q: pl.ds(pl.multiple_of(q * quarter, 16), quarter)
    hrows = lambda q, k: pl.ds(pl.multiple_of(q * quarter + k * half, 16), half)
    mine, qy, qz, dg = y * 2 + zb, (1 - y) * 2 + zb, y * 2 + 1 - zb, (1 - y) * 2 + 1 - zb
    source = lambda h: (io_ref, up_ref, down_ref)[PLAN[h][0]].at[PLAN[h][1]]
    started = []

    def go(cp):
        cp.start()
        started.append(cp)

    for i, dev in enumerate((sib, xp, diag)):
        go(remote(b_ref, bias_ref.at[x, c], b_ss.at[i], b_rs.at[i], dev))
    ins, backs = [], []
    for h in range(CH):
        go(remote(source(h).at[rows(mine)], out_ref.at[x, c, h, rows(mine)], x_ss.at[h], x_rs.at[h], xp))
        go(remote(source(h), out_ref.at[x, c, h], sib_ss.at[h], sib_rs.at[h], sib))
        ins.append(pltpu.make_async_copy(source(h), held.at[h], in_sem.at[h]))
        ins[h].start()
    bias_ref[x, c] = b_ref[...]
    for h in range(CH):
        ins[h].wait()
        backs.append(pltpu.make_async_copy(held.at[h], out_ref.at[x, c, h], back_sem.at[h]))
        backs[h].start()

    def whole(h, q, ss, rs, dev):
        a = out_ref.at[1 - x, c, h, rows(q)]
        return remote(a, a, ss, rs, dev)

    def part(h, q, k, ss, rs, dev):
        a = out_ref.at[1 - x, c, h, hrows(q, k)]
        return remote(a, a, ss.at[h], rs.at[h], dev)

    def first(h):
        whole(h, mine, x_ss.at[h], x_rs.at[h], xp).wait_recv()
        go(whole(h, mine, y_ss.at[h], y_rs.at[h], yp))
        go(whole(h, mine, z_ss.at[h], z_rs.at[h], zp))
        go(whole(h, mine, f_ss.at[h, 0], f_rs.at[h, 0], sib))

    def second(h):
        whole(h, qy, y_ss.at[h], y_rs.at[h], yp).wait_recv()
        go(part(h, qy, 1, z2_ss, z2_rs, zp))
        go(whole(h, qy, f_ss.at[h, 1], f_rs.at[h, 1], sib))
        whole(h, qz, z_ss.at[h], z_rs.at[h], zp).wait_recv()
        go(part(h, qz, 0, y2_ss, y2_rs, yp))
        go(whole(h, qz, f_ss.at[h, 2], f_rs.at[h, 2], sib))

    def third(h):
        part(h, dg, 0, y2_ss, y2_rs, yp).wait_recv()
        part(h, dg, 1, z2_ss, z2_rs, zp).wait_recv()
        go(whole(h, dg, f_ss.at[h, 3], f_rs.at[h, 3], sib))

    def arrived(h):
        a = out_ref.at[x, 1 - c, h]
        remote(a, a, sib_ss.at[h], sib_rs.at[h], sib).wait_recv()
        for i, q in enumerate((mine, qy, qz, dg)):
            a = out_ref.at[1 - x, 1 - c, h, rows(q)]
            remote(a, a, f_ss.at[h, i], f_rs.at[h, i], sib).wait_recv()
        backs[h].wait()

    for h in range(CH + 2):
        if h < CH:
            first(h)
        if 0 <= h - 1 < CH:
            second(h - 1)
        if 0 <= h - 2 < CH:
            third(h - 2)
    for h in range(CH):
        arrived(h)
    for cp in started:
        cp.wait_send()
    for i, (a, b) in enumerate(((x, 1 - c), (1 - x, c), (1 - x, 1 - c))):
        remote(b_ref, bias_ref.at[a, b], b_ss.at[i], b_rs.at[i], sib).wait_recv()


def weight_gather(io, up, down, bias_rows, cid=1):
    dma = pltpu.SemaphoreType.DMA
    return pl.pallas_call(
        gather_kernel,
        out_shape=(SDS((2, 2, CH, D, D), bf16), SDS((2, 2, 16, D), bf16)),
        in_specs=[ANY, ANY, ANY, VM],
        out_specs=(ANY, VM),
        scratch_shapes=[pltpu.VMEM((CH, D, D), bf16)] + [dma((CH,))] * 12 + [dma((CH, 4))] * 2 + [dma((3,))] * 2 + [dma((CH,))] * 2,
        compiler_params=pltpu.CompilerParams(collective_id=cid, has_side_effects=True, vmem_limit_bytes=32 * 2**20),
    )(io, up, down, bias_rows)


HD = 64
EPS = 1e-12


def dot(a, b, ca, cb):
    return lax.dot_general(a, b, (((ca,), (cb,)), ((), ())), preferred_element_type=f32)


def gelu_pair(u):
    a = jnp.abs(u) * 0.7071067811865476
    t = 1.0 / (1.0 + 0.3275911 * a)
    e = jnp.exp(-(a * a))
    poly = t * (0.254829592 + t * (-0.284496736 + t * (1.421413741 + t * (-1.453152027 + t * 1.061405429))))
    tail = 0.5 * poly * e
    cdf = jnp.where(u >= 0, 1.0 - tail, tail)
    return u * cdf, cdf + u * (e * 0.3989422804014327)


def loop(n, fn):
    def run(i, c):
        fn(i)
        return c

    lax.fori_loop(0, n, run, 0)


def norm(r, gain, shift):
    c = r - jnp.mean(r, axis=-1, keepdims=True)
    inv = lax.rsqrt(jnp.mean(c * c, axis=-1, keepdims=True) + EPS)
    n = c * inv
    return n * gain + shift, n, inv


def spot(seqs, length):
    tokens = seqs * length
    if length % 128 == 0:
        return length, seqs, 1
    return tokens, 1, seqs


W_SHAPES = ((3 * D, D), (D, D), (4, D, D), (4, D, D))


def load_weights(e, w_ref, win, wout, up, down, sem):
    base = 3 * (1 - e)
    q = D // 4
    kinds = [[], [], [], []]
    for t in range(4):
        src = w_ref.at[t // 2, t % 2]
        for j in range(3):
            kinds[0].append((src.at[base, pl.ds(j * q, q)], win.at[pl.ds(j * D + t * q, q)]))
        kinds[1].append((src.at[base, pl.ds(3 * q, q)], wout.at[pl.ds(t * q, q)]))
        kinds[2].append((src.at[base + 1], up.at[t]))
        kinds[3].append((src.at[base + 2], down.at[t]))
    n = 0
    copies = []
    for kind in kinds:
        copies.append([pltpu.make_async_copy(a, b, sem.at[n + i]) for i, (a, b) in enumerate(kind)])
        n += len(kind)

    def ready(k):
        for cp in copies[k]:
            cp.wait()

    for kind in copies:
        for cp in kind:
            cp.start()
    return ready


def forward_kernel(e, seqs, length, x_ref, w_ref, bcol_ref, ub_ref, vec_ref,
                   y_ref, qkv_ref, p_ref, o_ref, n1_ref, i1_ref, hb_ref, g_ref, d_ref, n2_ref, i2_ref, h_s, f_s, win_ref, wout_ref, up_ref, down_ref, w_sem):
    ready = load_weights(e, w_ref, win_ref, wout_ref, up_ref, down_ref, w_sem)
    ready(0)
    group, groups, per = spot(seqs, length)
    tokens = seqs * length
    blocks = tokens // group
    span = lambda i, n: pl.ds(pl.multiple_of(i * n, n), n)
    vec = lambda i: vec_ref[i : i + 1, :]

    def project(i):
        r = span(i, 256)
        v = (dot(win_ref[r, :], x_ref[...], 1, 1) + bcol_ref[r, :]).astype(bf16)
        qkv_ref[r, :] = v * jnp.where(i < 3, 0.125, 1.0).astype(bf16)

    loop(9, project)
    ready(1)

    for g in range(groups):
        tok = slice(g * group, (g + 1) * group)

        def heads(i):
            for k in range(2):
                h = i * 2 + k
                q = qkv_ref[pl.ds(pl.multiple_of(h * HD, HD), HD), tok]
                kk = qkv_ref[pl.ds(pl.multiple_of(D + h * HD, HD), HD), tok]
                vv = qkv_ref[pl.ds(pl.multiple_of(2 * D + h * HD, HD), HD), tok]
                s = dot(kk, q, 0, 0)
                if per > 1:
                    a = lax.broadcasted_iota(jnp.int32, s.shape, 0) // length
                    b = lax.broadcasted_iota(jnp.int32, s.shape, 1) // length
                    s = jnp.where(a == b, s, -1e30)
                e = jnp.exp(s - jnp.max(s, axis=0, keepdims=True))
                p = (e * (1.0 / jnp.sum(e, axis=0, keepdims=True))).astype(bf16)
                p_ref[g * 12 + h] = p
                o_ref[pl.ds(pl.multiple_of(h * HD, HD), HD), tok] = dot(vv, p, 1, 0).astype(bf16)

        loop(6, heads)

    for b in range(blocks):
        tok = slice(b * group, (b + 1) * group)
        r = dot(o_ref[:, tok], wout_ref[...], 0, 0) + x_ref[tok, :].astype(f32) + vec(4)
        h, n, inv = norm(r, vec(0), vec(2))
        h_s[tok, :] = h
        hb_ref[tok, :] = h.astype(bf16)
        n1_ref[tok, :] = n.astype(bf16)
        i1_ref[tok, :] = inv

    ready(2)
    ready(3)

    def hidden(i):
        for b in range(blocks):
            tok = slice(b * group, (b + 1) * group)
            for k in range(3):
                c = slice(k * 256, (k + 1) * 256)
                u = dot(hb_ref[tok, :], up_ref[i, :, c], 1, 0) + ub_ref[i, :, c]
                g, d = gelu_pair(u)
                g_ref[i, tok, c] = g.astype(bf16)
                d_ref[i, tok, c] = d.astype(bf16)
            part = dot(g_ref[i, tok, :], down_ref[i], 1, 0)
            f_s[tok, :] = jnp.where(i == 0, part, f_s[tok, :] + part)

    loop(4, hidden)
    for b in range(blocks):
        tok = slice(b * group, (b + 1) * group)
        y, n, inv = norm(h_s[tok, :] + (f_s[tok, :] + vec(5)), vec(1), vec(3))
        y_ref[tok, :] = y.astype(bf16)
        n2_ref[tok, :] = n.astype(bf16)
        i2_ref[tok, :] = inv


def encoder_forward(e, x, w, bias_col, up_rows, vec):
    seqs, length, _ = x.shape
    t = seqs * length
    group, groups, _ = spot(seqs, length)
    outs = (SDS((t, D), bf16), SDS((3 * D, t), bf16), SDS((groups * 12, group, group), bf16), SDS((D, t), bf16), SDS((t, D), bf16), SDS((t, 1), f32),
            SDS((t, D), bf16), SDS((4, t, D), bf16), SDS((4, t, D), bf16), SDS((t, D), bf16), SDS((t, 1), f32))
    return pl.pallas_call(
        functools.partial(forward_kernel, e, seqs, length), out_shape=outs, in_specs=[VM, ANY, VM, VM, VM], out_specs=(VM,) * len(outs),
        scratch_shapes=[pltpu.VMEM((t, D), f32), pltpu.VMEM((t, D), f32)] + [pltpu.VMEM(s, bf16) for s in W_SHAPES] + [pltpu.SemaphoreType.DMA((24,))],
        compiler_params=pltpu.CompilerParams(vmem_limit_bytes=60 * 2**20),
    )(x.reshape(t, D), w, bias_col, up_rows, vec)


def norm_back(dz, n, inv):
    return inv * (dz - jnp.mean(dz, axis=-1, keepdims=True) - n * jnp.mean(dz * n, axis=-1, keepdims=True))


def backward_kernel(e, seqs, length, cot_ref, dc_ref, n2_ref, i2_ref, d_ref, w_ref, n1_ref, i1_ref,
                    qkv_ref, p_ref, vec_ref, df_ref, du_ref, da_ref, dqkv_ref, dx_ref, sum_ref, r2_s, r1_s, dh_s, do_s, win_ref, wout_ref, up_ref, down_ref, w_sem):
    ready = load_weights(e, w_ref, win_ref, wout_ref, up_ref, down_ref, w_sem)
    group, groups, per = spot(seqs, length)
    tokens = seqs * length
    blocks = tokens // group
    vec = lambda i: vec_ref[i : i + 1, :]
    col = lambda a: jnp.sum(a, axis=0, keepdims=True)
    sum_ref[...] = jnp.zeros_like(sum_ref)

    def add(row, v):
        sum_ref[row : row + 1, :] += v

    for b in range(blocks):
        tok = slice(b * group, (b + 1) * group)
        dy = cot_ref[tok, :].astype(f32)
        pos = lax.broadcasted_iota(jnp.int32, (group, 1), 0)
        for k in range(per):
            dy = dy + jnp.where(pos == k * length, dc_ref[b * per + k : b * per + k + 1, :], 0.0)
        n = n2_ref[tok, :].astype(f32)
        add(5, col(dy * n))
        add(7, col(dy))
        r2 = norm_back(dy * vec(1), n, i2_ref[tok, :])
        r2_s[tok, :] = r2
        df = r2.astype(bf16)
        df_ref[tok, :] = df
        add(3, col(df.astype(f32)))

    ready(3)
    ready(2)

    def hidden(i):
        for b in range(blocks):
            tok = slice(b * group, (b + 1) * group)
            for k in range(3):
                c = slice(k * 256, (k + 1) * 256)
                du = (dot(df_ref[tok, :], down_ref[i, c, :], 1, 1) * d_ref[i, tok, c].astype(f32)).astype(bf16)
                du_ref[i, tok, c] = du
                sum_ref[pl.ds(8 + i, 1), c] += col(du.astype(f32))
            part = dot(du_ref[i, tok, :], up_ref[i], 1, 1)
            dh_s[tok, :] = jnp.where(i == 0, part, dh_s[tok, :] + part)

    loop(4, hidden)
    for b in range(blocks):
        tok = slice(b * group, (b + 1) * group)
        dh = dh_s[tok, :] + r2_s[tok, :]
        n = n1_ref[tok, :].astype(f32)
        add(4, col(dh * n))
        add(6, col(dh))
        r1 = norm_back(dh * vec(0), n, i1_ref[tok, :])
        r1_s[tok, :] = r1
        da = r1.astype(bf16)
        da_ref[tok, :] = da
        add(2, col(da.astype(f32)))

    span = lambda i, n: pl.ds(pl.multiple_of(i * n, n), n)

    def outward(i):
        do_s[span(i, 256), :] = dot(wout_ref[span(i, 256), :], da_ref[...], 1, 1).astype(bf16)

    ready(1)
    loop(3, outward)
    for g in range(groups):
        tok = slice(g * group, (g + 1) * group)

        def heads(i):
            for k in range(2):
                h = i * 2 + k
                at = lambda base: pl.ds(pl.multiple_of(base + h * HD, HD), HD)
                q, kk, vv, do = qkv_ref[at(0), tok], qkv_ref[at(D), tok], qkv_ref[at(2 * D), tok], do_s[at(0), tok]
                pb = p_ref[g * 12 + h]
                p = pb.astype(f32)
                dp = dot(vv, do, 0, 0)
                ds = (p * (dp - jnp.sum(p * dp, axis=0, keepdims=True))).astype(bf16)
                dqkv_ref[at(0), tok] = (dot(kk, ds, 1, 0) * 0.125).astype(bf16)
                dqkv_ref[at(D), tok] = dot(q, ds, 1, 1).astype(bf16)
                dqkv_ref[at(2 * D), tok] = dot(do, pb, 1, 1).astype(bf16)

        loop(6, heads)
    ready(0)
    ones = jnp.ones((8, tokens), bf16)
    add(0, dot(ones, dqkv_ref[0:D, :], 1, 1)[0:1])
    add(1, dot(ones, dqkv_ref[2 * D :, :], 1, 1)[0:1])
    for b in range(blocks):
        tok = slice(b * group, (b + 1) * group)
        dx_ref[tok, :] = (dot(dqkv_ref[:, tok], win_ref[...], 0, 0) + r1_s[tok, :]).astype(bf16)


def encoder_backward(e, cot, dc, kept, w, vec):
    seqs, length, _ = cot.shape
    t = seqs * length
    qkv, p, o, n1, i1, hb, g, d, n2, i2 = kept
    outs = (SDS((t, D), bf16), SDS((4, t, D), bf16), SDS((t, D), bf16), SDS((3 * D, t), bf16), SDS((t, D), bf16), SDS((16, D), f32))
    args = (cot.reshape(t, D), dc, n2, i2, d, w, n1, i1, qkv, p, vec)
    return pl.pallas_call(
        functools.partial(backward_kernel, e, seqs, length), out_shape=outs, in_specs=[VM] * 5 + [ANY] + [VM] * 5, out_specs=(VM,) * len(outs),
        scratch_shapes=[pltpu.VMEM((t, D), f32), pltpu.VMEM((t, D), f32), pltpu.VMEM((t, D), f32), pltpu.VMEM((D, t), bf16)] + [pltpu.VMEM(s, bf16) for s in W_SHAPES] + [pltpu.SemaphoreType.DMA((24,))],
        compiler_params=pltpu.CompilerParams(vmem_limit_bytes=60 * 2**20),
    )(*args)
def cls_kernel(n, own_ref, out_ref, a_ss, a_rs, b_ss, b_rs):
    dp, t = lax.axis_index("dp"), lax.axis_index("tensor")
    ring = [lax.rem(dp + j, n) for j in range(1, n)]
    group = [lax.rem(t + j, 4) for j in range(1, 4)]
    greet([(q, t) for q in ring] + [(dp, q) for q in group])
    out_ref[t, dp] = own_ref[...]
    first = [remote(own_ref, out_ref.at[t, dp], a_ss.at[j], a_rs.at[n - 2 - j], (q, t)) for j, q in enumerate(ring)]
    for cp in first:
        cp.start()
    for j, q in enumerate(ring):
        a = out_ref.at[t, q]
        remote(a, a, a_ss.at[j], a_rs.at[j], (q, t)).wait_recv()
    second = [remote(out_ref.at[t], out_ref.at[t], b_ss.at[j], b_rs.at[2 - j], (dp, q)) for j, q in enumerate(group)]
    for cp in second:
        cp.start()
    for j, q in enumerate(group):
        a = out_ref.at[q]
        remote(a, a, b_ss.at[j], b_rs.at[j], (dp, q)).wait_recv()
    for cp in first + second:
        cp.wait_send()


def cls_gather(own, n, cid=2):
    dma = pltpu.SemaphoreType.DMA
    return pl.pallas_call(
        functools.partial(cls_kernel, n),
        out_shape=jax.ShapeDtypeStruct((4, n, 16, D), bf16),
        in_specs=[pl.BlockSpec(memory_space=pltpu.VMEM)],
        out_specs=pl.BlockSpec(memory_space=pltpu.VMEM),
        scratch_shapes=[dma((n - 1,)), dma((n - 1,)), dma((3,)), dma((3,))],
        compiler_params=pltpu.CompilerParams(collective_id=cid, has_side_effects=True, vmem_limit_bytes=48 * 2**20),
    )(own)


def mm(a, b, dims):
    return lax.dot_general(a, b, (dims, ((), ())), preferred_element_type=f32)


def body(n_dp, questions, passages, question_cotangent, passage_cotangent, positives, positive_counts,
         attention_in, attention_bias, attention_out, branch_biases, norm_gains, norm_shifts, up_weight, up_bias, down_weight):
    q4 = D // 4
    io = jnp.concatenate([attention_in.transpose(0, 1, 3, 2).reshape(2, 3 * q4, D), attention_out], axis=1)
    bias_rows = jnp.concatenate([attention_bias.reshape(1, D), up_bias, jnp.zeros((13, D), bf16)])
    weights, biases = weight_gather(io, up_weight, down_weight, bias_rows)
    biases = biases.reshape(4, 16, D).astype(f32)
    full_att = biases[:, 0].reshape(4, 2, 2, q4).transpose(1, 2, 0, 3).reshape(2, 2, D)
    nothing = jnp.zeros((2, D), f32)
    kept, ys, vecs = [], [], []
    for e, x in enumerate((questions, passages)):
        vec = jnp.concatenate([norm_gains[e].astype(f32), norm_shifts[e].astype(f32), branch_biases[e].astype(f32), nothing])
        bias_col = jnp.concatenate([full_att[e, 0], nothing[0], full_att[e, 1]]).reshape(3 * D, 1)
        y, *k = encoder_forward(e, x, weights, bias_col, biases[:, 1 + e : 2 + e], vec)
        kept.append(k)
        ys.append(y)
        vecs.append(vec)
    nq, np_ = questions.shape[0], passages.shape[0]
    total = np_ * n_dp * 4
    cq = ys[0].reshape(questions.shape)[:, 0]
    cp = ys[1].reshape(passages.shape)[:, 0]
    live = jnp.arange(positives.shape[1], dtype=jnp.int32)[None, :] < positive_counts[:, None]
    marks = jnp.sum(((positives[:, :, None] == jnp.arange(D, dtype=jnp.int32)[None, None, :]) & live[:, :, None]).astype(f32), axis=1)
    payload = jnp.concatenate([cq, cp, marks.astype(bf16), jnp.zeros((16 - 2 * nq - np_, D), bf16)])
    every = cls_gather(payload, n_dp).transpose(1, 0, 2, 3).reshape(n_dp * 4, 16, D)
    all_q = every[:, :nq].reshape(-1, D)
    all_p = every[:, nq : nq + np_].reshape(-1, D)
    all_m = every[:, nq + np_ : 2 * nq + np_].reshape(-1, D)[:, :total].astype(f32)
    scale = 2.7 * D**-0.5
    scores = mm(all_q, all_p, ((1,), (1,))) * scale
    shifted = jnp.exp(scores - jnp.max(scores, axis=1, keepdims=True))
    all_total = jnp.sum(shifted, axis=1, keepdims=True)
    positive_total = jnp.sum(all_m * shifted, axis=1, keepdims=True)
    losses = (jnp.log(all_total) - jnp.log(positive_total))[:, 0]
    ds = (shifted / all_total - all_m * shifted / positive_total).astype(bf16)
    index = lax.axis_index("dp") * 4 + lax.axis_index("tensor")
    losses = lax.dynamic_slice_in_dim(losses, index * nq, nq, 0)
    dcq = mm(lax.dynamic_slice_in_dim(ds, index * nq, nq, 0), all_p, ((1,), (0,))) * scale
    dcp = mm(lax.dynamic_slice_in_dim(ds, index * np_, np_, 1), all_q, ((0,), (0,))) * scale
    dxs, operands, smalls = [], [], []
    for e, (cot, dc, x) in enumerate(((question_cotangent, dcq, questions), (passage_cotangent, dcp, passages))):
        dc = jnp.concatenate([dc, jnp.zeros((8 - dc.shape[0], D), f32)])
        df, du, da, dqkv, dx, s = encoder_backward(e, cot, dc, kept[e][:2] + [kept[e][2]] + kept[e][3:], weights, vecs[e])
        qkv, p, o, n1, i1, hb, g, d, n2, i2 = kept[e]
        dxs.append(dx)
        operands.append((g, df, hb, du, o, da, dqkv, x.reshape(-1, D)))
        smalls.append(s)
    both = jnp.stack(smalls)
    rows12 = jnp.concatenate([both[:, 2:4].reshape(4, D), both[:, 4:6].reshape(4, D), both[:, 6:8].reshape(4, D)]).reshape(4, 3, D)
    att = both[:, 0:2].reshape(2, 2, 4, q4).transpose(2, 0, 1, 3).reshape(4, 1, D)
    up = both[:, 8:12].transpose(1, 0, 2)
    first = jnp.concatenate([att, up, rows12, jnp.zeros((4, R - 6, D), f32)], axis=1).astype(bf16)
    out, small = grad_sum(first, operands, n_dp)
    res = out[:MACROS].reshape(3, 2, D, D)
    own_small = out[MACROS, :16].astype(f32)
    rep = small.reshape(4, 16, D)[:, 3:6].reshape(12, D).astype(f32)
    return (
        ys[0].reshape(questions.shape), ys[1].reshape(passages.shape), losses,
        dxs[0].reshape(questions.shape), dxs[1].reshape(passages.shape),
        res[2, :, : 3 * q4].reshape(2, 3, q4, D).transpose(0, 1, 3, 2).astype(f32), own_small[0].reshape(2, 2, q4),
        res[2, :, 3 * q4 :].astype(f32), rep[0:4].reshape(2, 2, D), rep[4:8].reshape(2, 2, D), rep[8:12].reshape(2, 2, D),
        res[1].astype(f32), own_small[1:3], res[0].astype(f32))


def solution(mesh):
    both = ("dp", "tensor")
    seq, rep = P(both, None, None), P()
    w4, w3, o3 = P(None, None, None, "tensor"), P(None, None, "tensor"), P(None, "tensor", None)
    in_specs = (seq, seq, seq, seq, P(both, None), P(both), w4, w3, o3, rep, rep, rep, w3, P(None, "tensor"), o3)
    out_specs = (seq, seq, P(both), seq, seq, w4, w3, o3, rep, rep, rep, w3, P(None, "tensor"), o3)
    return jax.shard_map(functools.partial(body, mesh.shape["dp"]), mesh=mesh, in_specs=in_specs, out_specs=out_specs, check_vma=False)
```

```python
import functools

import jax
import jax.numpy as jnp
from jax import lax
from jax.experimental import pallas as pl
from jax.experimental.pallas import tpu as pltpu
from jax.sharding import PartitionSpec as P

D = 768
MESH = pl.DeviceIdType.MESH
bf16, f32 = jnp.bfloat16, jnp.float32
VM = pl.BlockSpec(memory_space=pltpu.VMEM)
ANY = pl.BlockSpec(memory_space=pl.ANY)
SDS = jax.ShapeDtypeStruct


def place():
    dp, t = lax.axis_index("dp"), lax.axis_index("tensor")
    return dict(dp=dp, t=t, x=lax.div(t, 2), c=lax.rem(t, 2), y=lax.rem(dp, 2),
                z=lax.rem(lax.div(dp, 2), 4), o=lax.div(dp, 8))


def device(p, c=None, x=None, y=None, z=None, o=None):
    g = lambda v, k: p[k] if v is None else v
    return (g(o, "o") * 8 + g(z, "z") * 2 + g(y, "y"), g(x, "x") * 2 + g(c, "c"))


def greet(peers):
    bar = pltpu.get_barrier_semaphore()
    for q in peers:
        pl.semaphore_signal(bar, inc=1, device_id=q, device_id_type=MESH)
    pl.semaphore_wait(bar, len(peers))


def remote(src, dst, ssem, rsem, dev):
    return pltpu.make_async_remote_copy(src, dst, ssem, rsem, device_id=dev, device_id_type=MESH)


R = 64
MACRO = 256
HALF = D // 2
MACROS = 18
STEPS = MACROS * 4 + 1
VMEM_LIMIT = 64 * 2**20
LAG = dict(c=2, x=3, y=3, z=2, a=2)


KEPT = ("cot", "n2", "i2", "d", "g", "hb", "n1", "i1", "qkv", "o", "x", "p")


def held_names(e):
    return tuple(k for k in KEPT[:11] if e == 0 or k not in ("o", "x"))


def back_kernel(outer, sizes, *refs):
    w_ref, dc_ref, vec_ref = refs[:3]
    hbm = [dict(zip(KEPT, refs[3 + 12 * e : 15 + 12 * e])) for e in (0, 1)]
    refs = refs[27:]
    (out_ref, rows_ref, small_ref, *dx_ref), refs = refs[:5], refs[5:]
    buf = []
    for e in (0, 1):
        names = held_names(e) + ("df", "da", "r", "dh", "do")
        buf.append(dict(zip(names, refs[: len(names)])))
        refs = refs[len(names) :]
    (p0_ref, win, wout, up, down, sums, load_sem, dx_sem, w_sem,
     made, crecv, xs, xrecv, ys, yrecv, zsum, zrecv, fin, osend, orecv,
     c_ss, c_rs, x_ss, x_rs, y_ss, y_rs, z_ss, z_rs, a_ss, a_rs, o_ss, o_rs, w_ss, w_rs, l_sem, t_ss, t_rs) = refs
    buf[1]["p"], buf[0]["p"] = buf[1]["g"], p0_ref
    buf[1]["o"], buf[1]["x"] = buf[1]["n2"], buf[1]["n1"]

    def load(e, name):
        return pltpu.make_async_copy(hbm[e][name], buf[e][name], load_sem.at[e, KEPT.index(name)])

    def weights(e, kind):
        return weight_copies(e, w_ref, (win, wout, up, down), w_sem, kind)

    def begin(*copies):
        for cp in copies:
            cp.start()

    def ready(*copies):
        for cp in copies:
            cp.wait()

    begin(*[load(1, k) for k in ("cot", "n2", "i2")])
    begin(*[load(1, "d")], *weights(1, 3), *[load(1, k) for k in ("g",)], *weights(1, 2))
    begin(*[load(0, k) for k in ("cot", "n2", "i2")], *[load(1, k) for k in ("n1", "i1")], *weights(1, 1))
    begin(*[load(0, k) for k in ("g", "d")], *[load(1, k) for k in ("hb", "qkv")])
    begin(*[load(0, k) for k in ("hb", "n1", "i1", "qkv", "o", "x", "p")], *weights(1, 0))

    vec = lambda e, i: vec_ref[e, i : i + 1, :]
    col = lambda a: jnp.sum(a, axis=0, keepdims=True)
    sums[...] = jnp.zeros_like(sums)

    def add(e, row, v):
        sums[e, row : row + 1, :] += v

    def tokens(e, b):
        n = spot(*sizes[e])[0]
        return pl.ds(b * n, n) if isinstance(b, int) else pl.ds(pl.multiple_of(b * n, n), n)

    def norm2(e, b):
        group, groups, per = spot(*sizes[e])
        w, tok = buf[e], tokens(e, b)
        dy = w["cot"][tok, :].astype(f32)
        pos = lax.broadcasted_iota(jnp.int32, (group, 1), 0)
        for k in range(per):
            dy = dy + jnp.where(pos == k * sizes[e][1], dc_ref[e, b * per + k : b * per + k + 1, :], 0.0)
        n = w["n2"][tok, :].astype(f32)
        add(e, 5, col(dy * n))
        add(e, 7, col(dy))
        r2 = norm_back(dy * vec(e, 1), n, w["i2"][tok, :])
        w["r"][tok, :] = r2
        df = r2.astype(bf16)
        w["df"][tok, :] = df
        add(e, 3, col(df.astype(f32)))

    def hidden(e, i, b):
        w, tok = buf[e], tokens(e, b)
        for k in range(3):
            c = slice(k * 256, (k + 1) * 256)
            du = (dot(w["df"][tok, :], down[i, c, :], 1, 1) * w["d"][i, tok, c].astype(f32)).astype(bf16)
            w["d"][i, tok, c] = du
            sums[e, pl.ds(8 + i, 1), c] += col(du.astype(f32))
        part = dot(w["d"][i, tok, :], up[i], 1, 1)
        w["dh"][tok, :] = jnp.where(i == 0, part, w["dh"][tok, :] + part)

    def norm1(e, b):
        w, tok = buf[e], tokens(e, b)
        dh = w["dh"][tok, :] + w["r"][tok, :]
        n = w["n1"][tok, :].astype(f32)
        add(e, 4, col(dh * n))
        add(e, 6, col(dh))
        r1 = norm_back(dh * vec(e, 0), n, w["i1"][tok, :])
        w["r"][tok, :] = r1
        da = r1.astype(bf16)
        w["da"][tok, :] = da
        add(e, 2, col(da.astype(f32)))
        w["do"][:, tok] = dot(wout[...], da, 1, 1).astype(bf16)

    def head(e, g, h):
        w, tok = buf[e], tokens(e, g)
        at = lambda base: pl.ds(pl.multiple_of(base + h * HD, HD), HD)
        q, kk, vv, do = w["qkv"][at(0), tok], w["qkv"][at(D), tok], w["qkv"][at(2 * D), tok], w["do"][at(0), tok]
        pb = w["p"][p_at(e, sizes[e], g, h)]
        p = pb.astype(f32)
        dp = dot(vv, do, 0, 0)
        ds = (p * (dp - jnp.sum(p * dp, axis=0, keepdims=True))).astype(bf16)
        w["qkv"][at(0), tok] = (dot(kk, ds, 1, 0) * 0.125).astype(bf16)
        w["qkv"][at(D), tok] = dot(q, ds, 1, 1).astype(bf16)
        w["qkv"][at(2 * D), tok] = dot(do, pb, 1, 1).astype(bf16)

    def input_back(e, b):
        w, tok = buf[e], tokens(e, b)
        w["cot"][tok, :] = (dot(w["qkv"][:, tok], win[...], 0, 0) + w["r"][tok, :]).astype(bf16)

    def dx_copy(e):
        return pltpu.make_async_copy(buf[e]["cot"], dx_ref[e], dx_sem.at[e])

    def bias_sums(e):
        w = buf[e]
        ones = jnp.ones((8, w["da"].shape[0]), bf16)
        add(e, 0, dot(ones, w["qkv"][0:D, :], 1, 1)[0:1])
        add(e, 1, dot(ones, w["qkv"][2 * D :, :], 1, 1)[0:1])

    def at_step(s, first, fn, count=1):
        @pl.when(jnp.logical_and(s >= first, s < first + count))
        def _():
            fn(s - first)

    def work(s):
        @pl.when(jnp.logical_and(s < 16, lax.rem(s, 4) > 0))
        def _():
            idx = lax.div(s, 4) * 3 + lax.rem(s, 4) - 1
            hidden(1, lax.div(idx, 3), lax.rem(idx, 3))

        def s4(_):
            ready(*[load(0, k) for k in ("cot", "n2", "i2")])
            norm2(0, 0)

        def s9(_):
            begin(load(1, "p"))

        def s16(_):
            begin(*weights(0, 3), *weights(0, 2))
            ready(*[load(1, k) for k in ("n1", "i1")], *weights(1, 1))

        def s20(_):
            begin(load(1, "x"), *weights(0, 1))
            ready(*weights(0, 3), *weights(0, 2), load(0, "d"))

        def s25(_):
            ready(load(0, "n1"), load(0, "i1"), *weights(0, 1))
            norm1(0, 0)

        def s26(_):
            ready(load(1, "qkv"), load(1, "p"))

        def att1(a):
            for k in range(2):
                head(1, lax.div(a, 6), lax.rem(a, 6) * 2 + k)

        def s45(_):
            bias_sums(1)
            ready(*weights(1, 0))

        def s49(_):
            begin(dx_copy(1))
            begin(*weights(0, 0))
            ready(load(0, "qkv"), load(0, "p"))

        def att0(a):
            for k in range(2):
                head(0, 0, a * 2 + k)

        def s57(_):
            bias_sums(0)
            ready(*weights(0, 0))
            input_back(0, 0)
            begin(dx_copy(0))

        at_step(s, 4, s4)
        at_step(s, 9, s9)
        at_step(s, 16, s16)
        at_step(s, 17, lambda b: norm1(1, b), 3)
        at_step(s, 20, s20)
        at_step(s, 21, lambda i: hidden(0, i, 0), 4)
        at_step(s, 25, s25)
        at_step(s, 26, s26)
        at_step(s, 27, att1, 18)
        at_step(s, 45, s45)
        at_step(s, 46, lambda b: input_back(1, b), 3)
        at_step(s, 49, s49)
        at_step(s, 51, att0, 6)
        at_step(s, 57, s57)

    ready(*[load(1, k) for k in ("cot", "n2", "i2")])
    for b in range(3):
        norm2(1, b)
    begin(load(1, "o"))
    ready(load(1, "d"), load(1, "g"), *weights(1, 3), *weights(1, 2))

    p = place()
    sib, xp, yp = device(p, c=1 - p["c"]), device(p, x=1 - p["x"]), device(p, y=1 - p["y"])
    zs = [lax.rem(p["z"] + j, 4) for j in (1, 2, 3)]
    zp = [device(p, z=v) for v in zs]
    op = [device(p, o=lax.rem(p["o"] + j, outer)) for j in range(1, outer)]
    diag = device(p, x=1 - p["x"], c=1 - p["c"])
    greet([sib, xp, yp, diag] + zp + op)
    dc, dx, dy, dz, da = (LAG[k] for k in "cxyza")
    lx = dc
    ly = lx + dx
    lz = ly + dy
    la = lz + dz
    lf = la + da
    m16 = lambda v, n: pl.ds(pl.multiple_of(v, 16), n)
    mine16 = m16(p["z"] * 16, 16)
    half = lambda y: pl.ds(pl.multiple_of(y * HALF, 128), HALF)

    def made_at(u, c):
        return made.at[lax.rem(lax.div(u, 4), 2), :, c, m16(lax.rem(u, 4) * R, R)]

    def c_copy(u):
        k = lax.rem(u, 2 * dc)
        return remote(made_at(u, 1 - p["c"]), crecv.at[k], c_ss.at[k], c_rs.at[k], sib)

    def x_copy(u):
        k = lax.rem(u, 2 * dx)
        return remote(xs.at[k, 1 - p["x"]], xrecv.at[k], x_ss.at[k], x_rs.at[k], xp)

    def y_copy(u):
        k = lax.rem(u, 2 * dy)
        return remote(ys.at[k, :, half(1 - p["y"])], yrecv.at[k], y_ss.at[k], y_rs.at[k], yp)

    def z_copy(u, j):
        k = lax.rem(u, 2 * dz)
        return remote(zsum.at[k, m16(zs[j] * 16, 16)], zrecv.at[k, m16(32 - 16 * j, 16)], z_ss.at[k], z_rs.at[k], zp[j])

    def z_all(u):
        k = lax.rem(u, 2 * dz)
        return remote(zsum.at[k, m16(0, 48)], zrecv.at[k], z_ss.at[k], z_rs.at[k], zp[0])

    def a_copy(u, j):
        k = lax.rem(u, 3 * da)
        a = fin.at[k, mine16]
        return remote(a, a, a_ss.at[k], a_rs.at[k], zp[j])

    def a_all(u):
        k = lax.rem(u, 3 * da)
        a = fin.at[k, m16(0, 48)]
        return remote(a, a, a_ss.at[k], a_rs.at[k], zp[0])

    def both(c):
        c.wait_send()
        c.wait_recv()

    def target(u):
        m = lax.div(u, 4)
        g = lax.div(m, 3)
        return out_ref.at[(lax.div(g, 2) * 2 + 1 - lax.rem(g, 2)) * 3 + lax.rem(m, 3), m16(lax.rem(u, 4) * R, R), half(p["y"])]

    def w_remote(u, dst):
        k = lax.rem(u, 3 * da)
        return remote(fin.at[k], dst, w_ss.at[k], w_rs.at[k], yp)

    def w_local(u, dst):
        k = lax.rem(u, 3 * da)
        return pltpu.make_async_copy(fin.at[k], dst, l_sem.at[k])

    def when(u, fn, n=STEPS):
        @pl.when(jnp.logical_and(u >= 0, u < n))
        def _():
            fn(u)

    def finish(u):
        both(a_all(u))

        @pl.when(u < STEPS - 1)
        def _():
            w_remote(u, target(u)).start()
            w_local(u, target(u)).start()

        @pl.when(u == STEPS - 1)
        def _():
            w_remote(u, rows_ref.at[:, half(p["y"])]).start()
            w_local(u, rows_ref.at[:, half(p["y"])]).start()

    def finished(u):
        @pl.when(u < STEPS - 1)
        def _():
            both(w_remote(u, target(u)))
            w_local(u, target(u)).wait()

        @pl.when(u == STEPS - 1)
        def _():
            both(w_remote(u, rows_ref.at[:, half(p["y"])]))
            w_local(u, rows_ref.at[:, half(p["y"])]).wait()

    def take_z(u):
        both(z_all(u))
        k = lax.rem(u, 2 * dz)
        v = zsum[k, mine16].astype(f32)
        for j in range(3):
            v = v + zrecv[k, 16 * j : 16 * j + 16].astype(f32)
        if outer > 1:
            osend[...] = v.astype(bf16)
            for j in range(outer - 1):
                remote(osend, orecv.at[outer - 2 - j], o_ss.at[j], o_rs.at[outer - 2 - j], op[j]).start()
            for j in range(outer - 1):
                both(remote(osend, orecv.at[j], o_ss.at[j], o_rs.at[j], op[j]))
            v = osend[...].astype(f32)
            for j in range(outer - 1):
                v = v + orecv[j].astype(f32)
        fin[lax.rem(u, 3 * da), mine16] = v.astype(bf16)
        for j in range(3):
            a_copy(u, j).start()

    def take_y(u):
        both(y_copy(u))
        k = lax.rem(u, 2 * dy)
        zsum[lax.rem(u, 2 * dz)] = ys[k, :, half(p["y"])] + yrecv[k]
        for j in range(3):
            z_copy(u, j).start()

    def take_x(u):
        both(x_copy(u))
        k = lax.rem(u, 2 * dx)
        ys[lax.rem(u, 2 * dy)] = xs[k, p["x"]] + xrecv[k]
        y_copy(u).start()

    def take_c(u):
        both(c_copy(u))
        k = lax.rem(u, 2 * dc)
        kx = lax.rem(u, 2 * dx)
        own = lambda x: made[lax.rem(lax.div(u, 4), 2), x, p["c"], m16(lax.rem(u, 4) * R, R)]
        o = 1 - p["x"]
        xs[kx, o] = own(o) + crecv[k, o]
        x_copy(u).start()
        xs[kx, p["x"]] = own(p["x"]) + crecv[k, p["x"]]

    def make(m):
        slot = lax.rem(m, 2)
        g = lax.div(m, 3)
        r = lax.rem(m, 3)
        cols = pl.ds(pl.multiple_of(r * MACRO, 128), MACRO)
        for e in (0, 1):
            w = buf[e]

            @pl.when(g == 1 - e)
            def _():
                if e == 0:
                    @pl.when(r == 0)
                    def _():
                        ready(load(0, "g"))
                for t in range(4):
                    made[slot, t // 2, t % 2] = dot(w["g"][t, :, cols], w["df"][...], 0, 0).astype(bf16)

            @pl.when(g == 3 - e)
            def _():
                @pl.when(r == 0)
                def _():
                    ready(load(e, "hb"))
                for t in range(4):
                    made[slot, t // 2, t % 2] = dot(w["hb"][:, cols], w["d"][t], 0, 0).astype(bf16)

            for rr in range(3):
                @pl.when(m == (5 - e) * 3 + rr)
                def _():
                    if rr == 0:
                        ready(load(e, "o"), load(e, "x"))
                    for t in range(4):
                        at = rr * MACRO
                        while at < (rr + 1) * MACRO:
                            j, off = at // 192, at % 192
                            n = min(192 - off, (rr + 1) * MACRO - at)
                            src = w["qkv"][j * D + t * 192 + off : j * D + t * 192 + off + n, :] if j < 3 else w["o"][t * 192 + off : t * 192 + off + n, :]
                            made[slot, t // 2, t % 2, at - rr * MACRO : at - rr * MACRO + n] = dot(
                                src, w["x"][...] if j < 3 else w["da"][...], 1, 0).astype(bf16)
                            at += n

        @pl.when(m == MACROS)
        def _():
            row = lambda e, i: sums[e, i : i + 1, :]
            shared = [row(e, i + k) for i in (2, 4, 6) for e in (0, 1) for k in (0, 1)]
            for t in range(4):
                v = [row(0, 0), row(0, 1), row(1, 0), row(1, 1), row(0, 8 + t), row(1, 8 + t)] + shared[3 * t : 3 * t + 3]
                v = jnp.concatenate(v + [jnp.zeros((7, D), f32)], axis=0)
                made[slot, t // 2, t % 2, 0:16] = v.astype(bf16)
                made[slot, t // 2, t % 2, 16:R] = jnp.zeros((R - 16, D), bf16)

    def fetch(u):
        @pl.when(lax.rem(u, 4) == 0)
        def _():
            make(lax.div(u, 4))

        c_copy(u).start()

    def step(s, _):
        when(s - lf - da, finished)
        when(s - lf, finish)
        when(s - la, take_z)
        when(s - lz, take_y)
        when(s - ly, take_x)
        when(s - lx, take_c)
        when(s, fetch)
        work(s)
        return _

    lax.fori_loop(0, STEPS + lf + da, step, 0)
    ready(dx_copy(0), dx_copy(1))
    x, c = p["x"], p["c"]
    own = rows_ref.at[pl.ds(0, 16)]
    sends = [remote(own, small_ref.at[x, c], t_ss.at[i], t_rs.at[i], dev) for i, dev in enumerate((sib, xp, diag))]
    for cp in sends:
        cp.start()
    small_ref[x, c] = rows_ref[0:16]
    for i, (a, b) in enumerate(((x, 1 - c), (1 - x, c), (1 - x, 1 - c))):
        sends[i].wait_send()
        remote(own, small_ref.at[a, b], t_ss.at[i], t_rs.at[i], sib).wait_recv()


def backward(w_all, dc, vec, kept, sizes, dp, cid=3):
    outer = dp // 8
    dma = pltpu.SemaphoreType.DMA
    lc, lx, ly, lz, la = (LAG[k] for k in "cxyza")
    no = max(outer - 1, 1)
    vm = lambda s, t=bf16: pltpu.VMEM(s, t)
    scratch = []
    for e in (0, 1):
        n = sizes[e][0] * sizes[e][1]
        scratch += [vm(kept[e][k].shape, kept[e][k].dtype) for k in held_names(e)]
        scratch += [vm((n, D)), vm((n, D)), vm((n, D), f32), vm((n, D), f32), vm((D, n))]
    args = [w_all, dc, vec] + [kept[e][k] for e in (0, 1) for k in KEPT]
    return pl.pallas_call(
        functools.partial(back_kernel, outer, sizes),
        out_shape=(SDS((MACROS, MACRO, D), bf16), SDS((R, D), bf16), SDS((2, 2, 16, D), bf16),
                   SDS(kept[0]["x"].shape, bf16), SDS(kept[1]["x"].shape, bf16)),
        in_specs=[ANY, VM, VM] + [ANY] * 24,
        out_specs=(ANY, VM, VM, ANY, ANY),
        scratch_shapes=scratch + [
            vm(kept[0]["p"].shape), *[vm(s) for s in W_SHAPES], vm((2, 16, D), f32), dma((2, 12)), dma((2,)), dma((24,)),
            vm((2, 2, 2, MACRO, D)), vm((2 * lc, 2, R, D)), vm((2 * lx, 2, R, D)), vm((2 * lx, R, D)),
            vm((2 * ly, R, D)), vm((2 * ly, R, HALF)), vm((2 * lz, R, HALF)), vm((2 * lz, 48, HALF)), vm((3 * la, R, HALF)),
            vm((16, HALF)), vm((no, 16, HALF)),
            dma((2 * lc,)), dma((2 * lc,)), dma((2 * lx,)), dma((2 * lx,)), dma((2 * ly,)), dma((2 * ly,)),
            dma((2 * lz,)), dma((2 * lz,)), dma((3 * la,)), dma((3 * la,)), dma((no,)), dma((no,)),
            dma((3 * la,)), dma((3 * la,)), dma((3 * la,)), dma((3,)), dma((3,)),
        ],
        compiler_params=pltpu.CompilerParams(collective_id=cid, has_side_effects=True, vmem_limit_bytes=VMEM_LIMIT),
    )(*args)


CH = 6
PLAN = ((0, 1), (1, 1), (2, 1), (0, 0), (1, 0), (2, 0))


def gather_kernel(io_ref, up_ref, down_ref, b_ref, out_ref, bias_ref, held, *sems):
    (x_ss, x_rs, y_ss, y_rs, z_ss, z_rs, y2_ss, y2_rs, z2_ss, z2_rs, sib_ss, sib_rs, f_ss, f_rs, b_ss, b_rs, in_sem, back_sem) = sems
    p = place()
    zb = lax.rem(p["z"], 2)
    sib, xp, yp = device(p, c=1 - p["c"]), device(p, x=1 - p["x"]), device(p, y=1 - p["y"])
    zp = device(p, z=p["z"] + 1 - 2 * zb)
    diag = device(p, x=1 - p["x"], c=1 - p["c"])
    greet([sib, xp, yp, zp, diag])
    x, c, y = p["x"], p["c"], p["y"]
    quarter, half = D // 4, D // 8
    rows = lambda q: pl.ds(pl.multiple_of(q * quarter, 16), quarter)
    hrows = lambda q, k: pl.ds(pl.multiple_of(q * quarter + k * half, 16), half)
    mine, qy, qz, dg = y * 2 + zb, (1 - y) * 2 + zb, y * 2 + 1 - zb, (1 - y) * 2 + 1 - zb
    source = lambda h: (io_ref, up_ref, down_ref)[PLAN[h][0]].at[PLAN[h][1]]
    started = []

    def go(cp):
        cp.start()
        started.append(cp)

    for i, dev in enumerate((sib, xp, diag)):
        go(remote(b_ref, bias_ref.at[x, c], b_ss.at[i], b_rs.at[i], dev))
    ins, backs = [], []
    for h in range(CH):
        go(remote(source(h).at[rows(mine)], out_ref.at[x, c, h, rows(mine)], x_ss.at[h], x_rs.at[h], xp))
        go(remote(source(h), out_ref.at[x, c, h], sib_ss.at[h], sib_rs.at[h], sib))
        ins.append(pltpu.make_async_copy(source(h), held.at[h], in_sem.at[h]))
        ins[h].start()
    bias_ref[x, c] = b_ref[...]
    for h in range(CH):
        ins[h].wait()
        backs.append(pltpu.make_async_copy(held.at[h], out_ref.at[x, c, h], back_sem.at[h]))
        backs[h].start()

    def whole(h, q, ss, rs, dev):
        a = out_ref.at[1 - x, c, h, rows(q)]
        return remote(a, a, ss, rs, dev)

    def part(h, q, k, ss, rs, dev):
        a = out_ref.at[1 - x, c, h, hrows(q, k)]
        return remote(a, a, ss.at[h], rs.at[h], dev)

    def first(h):
        whole(h, mine, x_ss.at[h], x_rs.at[h], xp).wait_recv()
        go(whole(h, mine, y_ss.at[h], y_rs.at[h], yp))
        go(whole(h, mine, z_ss.at[h], z_rs.at[h], zp))
        go(whole(h, mine, f_ss.at[h, 0], f_rs.at[h, 0], sib))

    def second(h):
        whole(h, qy, y_ss.at[h], y_rs.at[h], yp).wait_recv()
        go(part(h, qy, 1, z2_ss, z2_rs, zp))
        go(whole(h, qy, f_ss.at[h, 1], f_rs.at[h, 1], sib))
        whole(h, qz, z_ss.at[h], z_rs.at[h], zp).wait_recv()
        go(part(h, qz, 0, y2_ss, y2_rs, yp))
        go(whole(h, qz, f_ss.at[h, 2], f_rs.at[h, 2], sib))

    def third(h):
        part(h, dg, 0, y2_ss, y2_rs, yp).wait_recv()
        part(h, dg, 1, z2_ss, z2_rs, zp).wait_recv()
        go(whole(h, dg, f_ss.at[h, 3], f_rs.at[h, 3], sib))

    def arrived(h):
        a = out_ref.at[x, 1 - c, h]
        remote(a, a, sib_ss.at[h], sib_rs.at[h], sib).wait_recv()
        for i, q in enumerate((mine, qy, qz, dg)):
            a = out_ref.at[1 - x, 1 - c, h, rows(q)]
            remote(a, a, f_ss.at[h, i], f_rs.at[h, i], sib).wait_recv()
        backs[h].wait()

    for h in range(CH + 2):
        if h < CH:
            first(h)
        if 0 <= h - 1 < CH:
            second(h - 1)
        if 0 <= h - 2 < CH:
            third(h - 2)
    for h in range(CH):
        arrived(h)
    for cp in started:
        cp.wait_send()
    for i, (a, b) in enumerate(((x, 1 - c), (1 - x, c), (1 - x, 1 - c))):
        remote(b_ref, bias_ref.at[a, b], b_ss.at[i], b_rs.at[i], sib).wait_recv()


def weight_gather(io, up, down, bias_rows, cid=1):
    dma = pltpu.SemaphoreType.DMA
    return pl.pallas_call(
        gather_kernel,
        out_shape=(SDS((2, 2, CH, D, D), bf16), SDS((2, 2, 16, D), bf16)),
        in_specs=[ANY, ANY, ANY, VM],
        out_specs=(ANY, VM),
        scratch_shapes=[pltpu.VMEM((CH, D, D), bf16)] + [dma((CH,))] * 12 + [dma((CH, 4))] * 2 + [dma((3,))] * 2 + [dma((CH,))] * 2,
        compiler_params=pltpu.CompilerParams(collective_id=cid, has_side_effects=True, vmem_limit_bytes=32 * 2**20),
    )(io, up, down, bias_rows)


HD = 64
EPS = 1e-12


def dot(a, b, ca, cb):
    return lax.dot_general(a, b, (((ca,), (cb,)), ((), ())), preferred_element_type=f32)


def gelu_pair(u):
    a = jnp.abs(u) * 0.7071067811865476
    t = 1.0 / (1.0 + 0.3275911 * a)
    e = jnp.exp(-(a * a))
    poly = t * (0.254829592 + t * (-0.284496736 + t * (1.421413741 + t * (-1.453152027 + t * 1.061405429))))
    tail = 0.5 * poly * e
    cdf = jnp.where(u >= 0, 1.0 - tail, tail)
    return u * cdf, cdf + u * (e * 0.3989422804014327)


def loop(n, fn):
    def run(i, c):
        fn(i)
        return c

    lax.fori_loop(0, n, run, 0)


def norm(r, gain, shift):
    c = r - jnp.mean(r, axis=-1, keepdims=True)
    inv = lax.rsqrt(jnp.mean(c * c, axis=-1, keepdims=True) + EPS)
    n = c * inv
    return n * gain + shift, n, inv


def spot(seqs, length):
    tokens = seqs * length
    if length % 128 == 0:
        return length, seqs, 1
    return tokens, 1, seqs


W_SHAPES = ((3 * D, D), (D, D), (4, D, D), (4, D, D))


def weight_copies(e, w_ref, refs, sem, kind):
    base, q = 3 * (1 - e), D // 4
    dst = refs[kind]
    pairs = []
    for t in range(4):
        src = w_ref.at[t // 2, t % 2]
        if kind == 0:
            pairs += [(src.at[base, pl.ds(j * q, q)], dst.at[pl.ds(j * D + t * q, q)]) for j in range(3)]
        elif kind == 1:
            pairs.append((src.at[base, pl.ds(3 * q, q)], dst.at[pl.ds(t * q, q)]))
        else:
            pairs.append((src.at[base + kind - 1], dst.at[t]))
    first = (0, 12, 16, 20)[kind]
    return [pltpu.make_async_copy(a, b, sem.at[first + i]) for i, (a, b) in enumerate(pairs)]


def load_weights(e, w_ref, win, wout, up, down, sem):
    copies = [weight_copies(e, w_ref, (win, wout, up, down), sem, k) for k in range(4)]
    for kind in copies:
        for cp in kind:
            cp.start()

    def ready(k):
        for cp in copies[k]:
            cp.wait()

    return ready


def p_at(e, size, g, h):
    group, groups, _ = spot(*size)
    if groups == 1:
        return (h,)
    return (h // 3 if isinstance(h, int) else lax.div(h, 3),
            pl.ds(g * group if isinstance(g, int) else pl.multiple_of(g * group, group), group),
            pl.ds(pl.multiple_of((h % 3 if isinstance(h, int) else lax.rem(h, 3)) * group, 128), group))


def forward_kernel(e, seqs, length, x_ref, w_ref, bcol_ref, ub_ref, vec_ref,
                   y_ref, qkv_ref, p_ref, o_ref, n1_ref, i1_ref, hb_ref, g_ref, d_ref, n2_ref, i2_ref, h_s, f_s, win_ref, wout_ref, up_ref, down_ref, w_sem):
    ready = load_weights(e, w_ref, win_ref, wout_ref, up_ref, down_ref, w_sem)
    ready(0)
    group, groups, per = spot(seqs, length)
    tokens = seqs * length
    blocks = tokens // group
    span = lambda i, n: pl.ds(pl.multiple_of(i * n, n), n)
    vec = lambda i: vec_ref[i : i + 1, :]

    def project(i):
        r = span(i, 256)
        v = (dot(win_ref[r, :], x_ref[...], 1, 1) + bcol_ref[r, :]).astype(bf16)
        qkv_ref[r, :] = v * jnp.where(i < 3, 0.125, 1.0).astype(bf16)

    loop(9, project)
    ready(1)

    for g in range(groups):
        tok = slice(g * group, (g + 1) * group)

        def heads(i):
            for k in range(2):
                h = i * 2 + k
                q = qkv_ref[pl.ds(pl.multiple_of(h * HD, HD), HD), tok]
                kk = qkv_ref[pl.ds(pl.multiple_of(D + h * HD, HD), HD), tok]
                vv = qkv_ref[pl.ds(pl.multiple_of(2 * D + h * HD, HD), HD), tok]
                s = dot(kk, q, 0, 0)
                if per > 1:
                    a = lax.broadcasted_iota(jnp.int32, s.shape, 0) // length
                    b = lax.broadcasted_iota(jnp.int32, s.shape, 1) // length
                    s = jnp.where(a == b, s, -1e30)
                e = jnp.exp(s - jnp.max(s, axis=0, keepdims=True))
                p = (e * (1.0 / jnp.sum(e, axis=0, keepdims=True))).astype(bf16)
                p_ref[p_at(e, (seqs, length), g, h)] = p
                o_ref[pl.ds(pl.multiple_of(h * HD, HD), HD), tok] = dot(vv, p, 1, 0).astype(bf16)

        loop(6, heads)

    for b in range(blocks):
        tok = slice(b * group, (b + 1) * group)
        r = dot(o_ref[:, tok], wout_ref[...], 0, 0) + x_ref[tok, :].astype(f32) + vec(4)
        h, n, inv = norm(r, vec(0), vec(2))
        h_s[tok, :] = h
        hb_ref[tok, :] = h.astype(bf16)
        n1_ref[tok, :] = n.astype(bf16)
        i1_ref[tok, :] = inv

    ready(2)
    ready(3)

    def hidden(i):
        for b in range(blocks):
            tok = slice(b * group, (b + 1) * group)
            for k in range(3):
                c = slice(k * 256, (k + 1) * 256)
                u = dot(hb_ref[tok, :], up_ref[i, :, c], 1, 0) + ub_ref[i, :, c]
                g, d = gelu_pair(u)
                g_ref[i, tok, c] = g.astype(bf16)
                d_ref[i, tok, c] = d.astype(bf16)
            part = dot(g_ref[i, tok, :], down_ref[i], 1, 0)
            f_s[tok, :] = jnp.where(i == 0, part, f_s[tok, :] + part)

    loop(4, hidden)
    for b in range(blocks):
        tok = slice(b * group, (b + 1) * group)
        y, n, inv = norm(h_s[tok, :] + (f_s[tok, :] + vec(5)), vec(1), vec(3))
        y_ref[tok, :] = y.astype(bf16)
        n2_ref[tok, :] = n.astype(bf16)
        i2_ref[tok, :] = inv


def encoder_forward(e, x, w, bias_col, up_rows, vec):
    seqs, length, _ = x.shape
    t = seqs * length
    group, groups, _ = spot(seqs, length)
    outs = (SDS((t, D), bf16), SDS((3 * D, t), bf16), SDS((4, t, D) if groups > 1 else (12, group, group), bf16), SDS((D, t), bf16), SDS((t, D), bf16), SDS((t, 1), f32),
            SDS((t, D), bf16), SDS((4, t, D), bf16), SDS((4, t, D), bf16), SDS((t, D), bf16), SDS((t, 1), f32))
    return pl.pallas_call(
        functools.partial(forward_kernel, e, seqs, length), out_shape=outs, in_specs=[VM, ANY, VM, VM, VM], out_specs=(VM,) * len(outs),
        scratch_shapes=[pltpu.VMEM((t, D), f32), pltpu.VMEM((t, D), f32)] + [pltpu.VMEM(s, bf16) for s in W_SHAPES] + [pltpu.SemaphoreType.DMA((24,))],
        compiler_params=pltpu.CompilerParams(vmem_limit_bytes=60 * 2**20),
    )(x.reshape(t, D), w, bias_col, up_rows, vec)


def norm_back(dz, n, inv):
    return inv * (dz - jnp.mean(dz, axis=-1, keepdims=True) - n * jnp.mean(dz * n, axis=-1, keepdims=True))


def cls_kernel(n, own_ref, out_ref, a_ss, a_rs, b_ss, b_rs):
    dp, t = lax.axis_index("dp"), lax.axis_index("tensor")
    ring = [lax.rem(dp + j, n) for j in range(1, n)]
    group = [lax.rem(t + j, 4) for j in range(1, 4)]
    greet([(q, t) for q in ring] + [(dp, q) for q in group])
    out_ref[t, dp] = own_ref[...]
    first = [remote(own_ref, out_ref.at[t, dp], a_ss.at[j], a_rs.at[n - 2 - j], (q, t)) for j, q in enumerate(ring)]
    for cp in first:
        cp.start()
    for j, q in enumerate(ring):
        a = out_ref.at[t, q]
        remote(a, a, a_ss.at[j], a_rs.at[j], (q, t)).wait_recv()
    second = [remote(out_ref.at[t], out_ref.at[t], b_ss.at[j], b_rs.at[2 - j], (dp, q)) for j, q in enumerate(group)]
    for cp in second:
        cp.start()
    for j, q in enumerate(group):
        a = out_ref.at[q]
        remote(a, a, b_ss.at[j], b_rs.at[j], (dp, q)).wait_recv()
    for cp in first + second:
        cp.wait_send()


def cls_gather(own, n, cid=2):
    dma = pltpu.SemaphoreType.DMA
    return pl.pallas_call(
        functools.partial(cls_kernel, n),
        out_shape=jax.ShapeDtypeStruct((4, n, 16, D), bf16),
        in_specs=[pl.BlockSpec(memory_space=pltpu.VMEM)],
        out_specs=pl.BlockSpec(memory_space=pltpu.VMEM),
        scratch_shapes=[dma((n - 1,)), dma((n - 1,)), dma((3,)), dma((3,))],
        compiler_params=pltpu.CompilerParams(collective_id=cid, has_side_effects=True, vmem_limit_bytes=48 * 2**20),
    )(own)


def mm(a, b, dims):
    return lax.dot_general(a, b, (dims, ((), ())), preferred_element_type=f32)


def body(n_dp, questions, passages, question_cotangent, passage_cotangent, positives, positive_counts,
         attention_in, attention_bias, attention_out, branch_biases, norm_gains, norm_shifts, up_weight, up_bias, down_weight):
    q4 = D // 4
    io = jnp.concatenate([attention_in.transpose(0, 1, 3, 2).reshape(2, 3 * q4, D), attention_out], axis=1)
    bias_rows = jnp.concatenate([attention_bias.reshape(1, D), up_bias, jnp.zeros((13, D), bf16)])
    weights, biases = weight_gather(io, up_weight, down_weight, bias_rows)
    biases = biases.reshape(4, 16, D).astype(f32)
    full_att = biases[:, 0].reshape(4, 2, 2, q4).transpose(1, 2, 0, 3).reshape(2, 2, D)
    nothing = jnp.zeros((2, D), f32)
    kept, ys, vecs = [], [], []
    for e, x in enumerate((questions, passages)):
        vec = jnp.concatenate([norm_gains[e].astype(f32), norm_shifts[e].astype(f32), branch_biases[e].astype(f32), nothing])
        bias_col = jnp.concatenate([full_att[e, 0], nothing[0], full_att[e, 1]]).reshape(3 * D, 1)
        y, *k = encoder_forward(e, x, weights, bias_col, biases[:, 1 + e : 2 + e], vec)
        kept.append(k)
        ys.append(y)
        vecs.append(vec)
    nq, np_ = questions.shape[0], passages.shape[0]
    total = np_ * n_dp * 4
    cq = ys[0].reshape(questions.shape)[:, 0]
    cp = ys[1].reshape(passages.shape)[:, 0]
    live = jnp.arange(positives.shape[1], dtype=jnp.int32)[None, :] < positive_counts[:, None]
    marks = jnp.sum(((positives[:, :, None] == jnp.arange(D, dtype=jnp.int32)[None, None, :]) & live[:, :, None]).astype(f32), axis=1)
    payload = jnp.concatenate([cq, cp, marks.astype(bf16), jnp.zeros((16 - 2 * nq - np_, D), bf16)])
    every = cls_gather(payload, n_dp).transpose(1, 0, 2, 3).reshape(n_dp * 4, 16, D)
    all_q = every[:, :nq].reshape(-1, D)
    all_p = every[:, nq : nq + np_].reshape(-1, D)
    all_m = every[:, nq + np_ : 2 * nq + np_].reshape(-1, D)[:, :total].astype(f32)
    scale = 2.7 * D**-0.5
    scores = mm(all_q, all_p, ((1,), (1,))) * scale
    shifted = jnp.exp(scores - jnp.max(scores, axis=1, keepdims=True))
    all_total = jnp.sum(shifted, axis=1, keepdims=True)
    positive_total = jnp.sum(all_m * shifted, axis=1, keepdims=True)
    losses = (jnp.log(all_total) - jnp.log(positive_total))[:, 0]
    ds = (shifted / all_total - all_m * shifted / positive_total).astype(bf16)
    index = lax.axis_index("dp") * 4 + lax.axis_index("tensor")
    losses = lax.dynamic_slice_in_dim(losses, index * nq, nq, 0)
    dcq = mm(lax.dynamic_slice_in_dim(ds, index * nq, nq, 0), all_p, ((1,), (0,))) * scale
    dcp = mm(lax.dynamic_slice_in_dim(ds, index * np_, np_, 1), all_q, ((0,), (0,))) * scale
    pad = jnp.zeros((8 - nq, D), f32)
    dc = jnp.stack([jnp.concatenate([dcq, pad]), jnp.concatenate([dcp, pad])])
    for e, (cot, x) in enumerate(((question_cotangent, questions), (passage_cotangent, passages))):
        qkv, p, o, n1, i1, hb, g, d, n2, i2 = kept[e]
        kept[e] = dict(cot=cot.reshape(-1, D), n2=n2, i2=i2, d=d, g=g, hb=hb, n1=n1, i1=i1, qkv=qkv, o=o, x=x.reshape(-1, D), p=p)
    sizes = (questions.shape[:2], passages.shape[:2])
    out, own_rows, small, *dxs = backward(weights, dc, jnp.stack(vecs), kept, sizes, n_dp)
    res = out.reshape(3, 2, D, D)
    own_small = own_rows[:16].astype(f32)
    rep = small.reshape(4, 16, D)[:, 6:9].reshape(12, D).astype(f32)
    att = lax.dynamic_slice_in_dim(own_small[0:4], lax.axis_index("tensor") * q4, q4, 1)
    return (
        ys[0].reshape(questions.shape), ys[1].reshape(passages.shape), losses,
        dxs[0].reshape(questions.shape), dxs[1].reshape(passages.shape),
        res[2, :, : 3 * q4].reshape(2, 3, q4, D).transpose(0, 1, 3, 2).astype(f32), att.reshape(2, 2, q4),
        res[2, :, 3 * q4 :].astype(f32), rep[0:4].reshape(2, 2, D), rep[4:8].reshape(2, 2, D), rep[8:12].reshape(2, 2, D),
        res[1].astype(f32), own_small[4:6], res[0].astype(f32))


def solution(mesh):
    both = ("dp", "tensor")
    seq, rep = P(both, None, None), P()
    w4, w3, o3 = P(None, None, None, "tensor"), P(None, None, "tensor"), P(None, "tensor", None)
    in_specs = (seq, seq, seq, seq, P(both, None), P(both), w4, w3, o3, rep, rep, rep, w3, P(None, "tensor"), o3)
    out_specs = (seq, seq, P(both), seq, seq, w4, w3, o3, rep, rep, rep, w3, P(None, "tensor"), o3)
    return jax.shard_map(functools.partial(body, mesh.shape["dp"]), mesh=mesh, in_specs=in_specs, out_specs=out_specs, check_vma=False)
```

```python
import functools

import jax
import jax.numpy as jnp
from jax import lax
from jax.experimental import pallas as pl
from jax.experimental.pallas import tpu as pltpu
from jax.sharding import PartitionSpec as P

D = 768
MESH = pl.DeviceIdType.MESH
bf16, f32 = jnp.bfloat16, jnp.float32
VM = pl.BlockSpec(memory_space=pltpu.VMEM)
ANY = pl.BlockSpec(memory_space=pl.ANY)
SDS = jax.ShapeDtypeStruct


def place():
    dp, t = lax.axis_index("dp"), lax.axis_index("tensor")
    return dict(dp=dp, t=t, x=lax.div(t, 2), c=lax.rem(t, 2), y=lax.rem(dp, 2),
                z=lax.rem(lax.div(dp, 2), 4), o=lax.div(dp, 8))


def device(p, c=None, x=None, y=None, z=None, o=None):
    g = lambda v, k: p[k] if v is None else v
    return (g(o, "o") * 8 + g(z, "z") * 2 + g(y, "y"), g(x, "x") * 2 + g(c, "c"))


def greet(peers):
    bar = pltpu.get_barrier_semaphore()
    for q in peers:
        pl.semaphore_signal(bar, inc=1, device_id=q, device_id_type=MESH)
    pl.semaphore_wait(bar, len(peers))


def remote(src, dst, ssem, rsem, dev):
    return pltpu.make_async_remote_copy(src, dst, ssem, rsem, device_id=dev, device_id_type=MESH)


R = 64
MACRO = 256
HALF = D // 2
MACROS = 18
STEPS = MACROS * 4 + 1
VMEM_LIMIT = 64 * 2**20
LAG = dict(c=2, x=3, y=3, z=2, a=2)


KEPT = ("cot", "n2", "i2", "d", "g", "hb", "n1", "i1", "qkv", "o", "x", "p")


def cls_row(sizes, e):
    return sizes[0][0] if e else 0


def held_names(e):
    return tuple(k for k in KEPT[:11] if e == 0 or k not in ("o", "x"))


def back_kernel(outer, sizes, *refs):
    w_ref, dc_ref, vec_ref = refs[:3]
    hbm = [dict(zip(KEPT, refs[3 + 12 * e : 15 + 12 * e])) for e in (0, 1)]
    refs = refs[27:]
    (out_ref, rows_ref, small_ref, *dx_ref), refs = refs[:5], refs[5:]
    buf = []
    for e in (0, 1):
        names = held_names(e) + ("df", "da", "r", "dh", "do")
        buf.append(dict(zip(names, refs[: len(names)])))
        refs = refs[len(names) :]
    (p0_ref, win, wout, up, down, sums, load_sem, dx_sem, w_sem,
     made, crecv, xs, xrecv, ys, yrecv, zsum, zrecv, fin, osend, orecv,
     c_ss, c_rs, x_ss, x_rs, y_ss, y_rs, z_ss, z_rs, a_ss, a_rs, o_ss, o_rs, w_ss, w_rs, l_sem, t_ss, t_rs) = refs
    buf[1]["p"], buf[0]["p"] = buf[1]["g"], p0_ref
    buf[1]["o"], buf[1]["x"] = buf[1]["n2"], buf[1]["n1"]

    def load(e, name):
        return pltpu.make_async_copy(hbm[e][name], buf[e][name], load_sem.at[e, KEPT.index(name)])

    def weights(e, kind):
        return weight_copies(e, w_ref, (win, wout, up, down), w_sem, kind)

    def begin(*copies):
        for cp in copies:
            cp.start()

    def ready(*copies):
        for cp in copies:
            cp.wait()

    begin(*[load(1, k) for k in ("cot", "n2", "i2")])
    begin(*[load(1, "d")], *weights(1, 3), *[load(1, k) for k in ("g",)], *weights(1, 2))
    begin(*[load(0, k) for k in ("cot", "n2", "i2")], *[load(1, k) for k in ("n1", "i1")], *weights(1, 1))
    begin(*[load(0, k) for k in ("g", "d")], *[load(1, k) for k in ("hb", "qkv")])
    begin(*[load(0, k) for k in ("hb", "n1", "i1", "qkv", "o", "x", "p")], *weights(1, 0))

    vec = lambda e, i: vec_ref[e, i : i + 1, :]
    col = lambda a: jnp.sum(a, axis=0, keepdims=True)
    sums[...] = jnp.zeros_like(sums)

    def add(e, row, v):
        sums[e, row : row + 1, :] += v

    def tokens(e, b):
        n = spot(*sizes[e])[0]
        return pl.ds(b * n, n) if isinstance(b, int) else pl.ds(pl.multiple_of(b * n, n), n)

    def norm2(e, b):
        group, groups, per = spot(*sizes[e])
        w, tok = buf[e], tokens(e, b)
        dy = w["cot"][tok, :].astype(f32)
        pos = lax.broadcasted_iota(jnp.int32, (group, 1), 0)
        for k in range(per):
            dy = dy + jnp.where(pos == k * sizes[e][1], dc_ref[e, cls_row(sizes, e) + b * per + k : cls_row(sizes, e) + b * per + k + 1, :], 0.0)
        n = w["n2"][tok, :].astype(f32)
        add(e, 5, col(dy * n))
        add(e, 7, col(dy))
        r2 = norm_back(dy * vec(e, 1), n, w["i2"][tok, :])
        w["r"][tok, :] = r2
        df = r2.astype(bf16)
        w["df"][tok, :] = df
        add(e, 3, col(df.astype(f32)))

    def hidden(e, i, b):
        w, tok = buf[e], tokens(e, b)
        for k in range(3):
            c = slice(k * 256, (k + 1) * 256)
            du = (dot(w["df"][tok, :], down[i, c, :], 1, 1) * w["d"][i, tok, c].astype(f32)).astype(bf16)
            w["d"][i, tok, c] = du
            sums[e, pl.ds(8 + i, 1), c] += col(du.astype(f32))
        part = dot(w["d"][i, tok, :], up[i], 1, 1)
        w["dh"][tok, :] = jnp.where(i == 0, part, w["dh"][tok, :] + part)

    def norm1(e, b):
        w, tok = buf[e], tokens(e, b)
        dh = w["dh"][tok, :] + w["r"][tok, :]
        n = w["n1"][tok, :].astype(f32)
        add(e, 4, col(dh * n))
        add(e, 6, col(dh))
        r1 = norm_back(dh * vec(e, 0), n, w["i1"][tok, :])
        w["r"][tok, :] = r1
        da = r1.astype(bf16)
        w["da"][tok, :] = da
        add(e, 2, col(da.astype(f32)))
        w["do"][:, tok] = dot(wout[...], da, 1, 1).astype(bf16)

    def head(e, g, h):
        w, tok = buf[e], tokens(e, g)
        at = lambda base: pl.ds(pl.multiple_of(base + h * HD, HD), HD)
        q, kk, vv, do = w["qkv"][at(0), tok], w["qkv"][at(D), tok], w["qkv"][at(2 * D), tok], w["do"][at(0), tok]
        pb = w["p"][p_at(e, sizes[e], g, h)]
        p = pb.astype(f32)
        dp = dot(vv, do, 0, 0)
        ds = (p * (dp - jnp.sum(p * dp, axis=0, keepdims=True))).astype(bf16)
        w["qkv"][at(0), tok] = (dot(kk, ds, 1, 0) * 0.125).astype(bf16)
        w["qkv"][at(D), tok] = dot(q, ds, 1, 1).astype(bf16)
        w["qkv"][at(2 * D), tok] = dot(do, pb, 1, 1).astype(bf16)

    def input_back(e, b):
        w, tok = buf[e], tokens(e, b)
        w["cot"][tok, :] = (dot(w["qkv"][:, tok], win[...], 0, 0) + w["r"][tok, :]).astype(bf16)

    def dx_copy(e):
        return pltpu.make_async_copy(buf[e]["cot"], dx_ref[e], dx_sem.at[e])

    def bias_sums(e):
        w = buf[e]
        ones = jnp.ones((8, w["da"].shape[0]), bf16)
        add(e, 0, dot(ones, w["qkv"][0:D, :], 1, 1)[0:1])
        add(e, 1, dot(ones, w["qkv"][2 * D :, :], 1, 1)[0:1])

    def at_step(s, first, fn, count=1):
        @pl.when(jnp.logical_and(s >= first, s < first + count))
        def _():
            fn(s - first)

    def work(s):
        @pl.when(jnp.logical_and(s < 16, lax.rem(s, 4) > 0))
        def _():
            idx = lax.div(s, 4) * 3 + lax.rem(s, 4) - 1
            hidden(1, lax.div(idx, 3), lax.rem(idx, 3))

        def s4(_):
            ready(*[load(0, k) for k in ("cot", "n2", "i2")])
            norm2(0, 0)

        def s9(_):
            begin(load(1, "p"))

        def s16(_):
            begin(*weights(0, 3), *weights(0, 2))
            ready(*[load(1, k) for k in ("n1", "i1")], *weights(1, 1))

        def s20(_):
            begin(load(1, "x"), *weights(0, 1))
            ready(*weights(0, 3), *weights(0, 2), load(0, "d"))

        def s25(_):
            ready(load(0, "n1"), load(0, "i1"), *weights(0, 1))
            norm1(0, 0)

        def s26(_):
            ready(load(1, "qkv"), load(1, "p"))

        def att1(a):
            for k in range(2):
                head(1, lax.div(a, 6), lax.rem(a, 6) * 2 + k)

        def s45(_):
            bias_sums(1)
            ready(*weights(1, 0))

        def s49(_):
            begin(dx_copy(1))
            begin(*weights(0, 0))
            ready(load(0, "qkv"), load(0, "p"))

        def att0(a):
            for k in range(2):
                head(0, 0, a * 2 + k)

        def s57(_):
            bias_sums(0)
            ready(*weights(0, 0))
            input_back(0, 0)
            begin(dx_copy(0))

        at_step(s, 4, s4)
        at_step(s, 9, s9)
        at_step(s, 16, s16)
        at_step(s, 17, lambda b: norm1(1, b), 3)
        at_step(s, 20, s20)
        at_step(s, 21, lambda i: hidden(0, i, 0), 4)
        at_step(s, 25, s25)
        at_step(s, 26, s26)
        at_step(s, 27, att1, 18)
        at_step(s, 45, s45)
        at_step(s, 46, lambda b: input_back(1, b), 3)
        at_step(s, 49, s49)
        at_step(s, 51, att0, 6)
        at_step(s, 57, s57)

    ready(*[load(1, k) for k in ("cot", "n2", "i2")])
    for b in range(3):
        norm2(1, b)
    begin(load(1, "o"))
    ready(load(1, "d"), load(1, "g"), *weights(1, 3), *weights(1, 2))

    p = place()
    sib, xp, yp = device(p, c=1 - p["c"]), device(p, x=1 - p["x"]), device(p, y=1 - p["y"])
    zs = [lax.rem(p["z"] + j, 4) for j in (1, 2, 3)]
    zp = [device(p, z=v) for v in zs]
    op = [device(p, o=lax.rem(p["o"] + j, outer)) for j in range(1, outer)]
    diag = device(p, x=1 - p["x"], c=1 - p["c"])
    greet([sib, xp, yp, diag] + zp + op)
    dc, dx, dy, dz, da = (LAG[k] for k in "cxyza")
    lx = dc
    ly = lx + dx
    lz = ly + dy
    la = lz + dz
    lf = la + da
    m16 = lambda v, n: pl.ds(pl.multiple_of(v, 16), n)
    mine16 = m16(p["z"] * 16, 16)
    half = lambda y: pl.ds(pl.multiple_of(y * HALF, 128), HALF)

    def made_at(u, c):
        return made.at[lax.rem(lax.div(u, 4), 2), :, c, m16(lax.rem(u, 4) * R, R)]

    def c_copy(u):
        k = lax.rem(u, 2 * dc)
        return remote(made_at(u, 1 - p["c"]), crecv.at[k], c_ss.at[k], c_rs.at[k], sib)

    def x_copy(u):
        k = lax.rem(u, 2 * dx)
        return remote(xs.at[k, 1 - p["x"]], xrecv.at[k], x_ss.at[k], x_rs.at[k], xp)

    def y_copy(u):
        k = lax.rem(u, 2 * dy)
        return remote(ys.at[k, :, half(1 - p["y"])], yrecv.at[k], y_ss.at[k], y_rs.at[k], yp)

    def z_copy(u, j):
        k = lax.rem(u, 2 * dz)
        return remote(zsum.at[k, m16(zs[j] * 16, 16)], zrecv.at[k, m16(32 - 16 * j, 16)], z_ss.at[k], z_rs.at[k], zp[j])

    def z_all(u):
        k = lax.rem(u, 2 * dz)
        return remote(zsum.at[k, m16(0, 48)], zrecv.at[k], z_ss.at[k], z_rs.at[k], zp[0])

    def a_copy(u, j):
        k = lax.rem(u, 3 * da)
        a = fin.at[k, mine16]
        return remote(a, a, a_ss.at[k], a_rs.at[k], zp[j])

    def a_all(u):
        k = lax.rem(u, 3 * da)
        a = fin.at[k, m16(0, 48)]
        return remote(a, a, a_ss.at[k], a_rs.at[k], zp[0])

    def both(c):
        c.wait_send()
        c.wait_recv()

    def target(u):
        m = lax.div(u, 4)
        g = lax.div(m, 3)
        return out_ref.at[(lax.div(g, 2) * 2 + 1 - lax.rem(g, 2)) * 3 + lax.rem(m, 3), m16(lax.rem(u, 4) * R, R), half(p["y"])]

    def w_remote(u, dst):
        k = lax.rem(u, 3 * da)
        return remote(fin.at[k], dst, w_ss.at[k], w_rs.at[k], yp)

    def w_local(u, dst):
        k = lax.rem(u, 3 * da)
        return pltpu.make_async_copy(fin.at[k], dst, l_sem.at[k])

    def when(u, fn, n=STEPS):
        @pl.when(jnp.logical_and(u >= 0, u < n))
        def _():
            fn(u)

    def finish(u):
        both(a_all(u))

        @pl.when(u < STEPS - 1)
        def _():
            w_remote(u, target(u)).start()
            w_local(u, target(u)).start()

        @pl.when(u == STEPS - 1)
        def _():
            w_remote(u, rows_ref.at[:, half(p["y"])]).start()
            w_local(u, rows_ref.at[:, half(p["y"])]).start()

    def finished(u):
        @pl.when(u < STEPS - 1)
        def _():
            both(w_remote(u, target(u)))
            w_local(u, target(u)).wait()

        @pl.when(u == STEPS - 1)
        def _():
            both(w_remote(u, rows_ref.at[:, half(p["y"])]))
            w_local(u, rows_ref.at[:, half(p["y"])]).wait()

    def take_z(u):
        both(z_all(u))
        k = lax.rem(u, 2 * dz)
        v = zsum[k, mine16].astype(f32)
        for j in range(3):
            v = v + zrecv[k, 16 * j : 16 * j + 16].astype(f32)
        if outer > 1:
            osend[...] = v.astype(bf16)
            for j in range(outer - 1):
                remote(osend, orecv.at[outer - 2 - j], o_ss.at[j], o_rs.at[outer - 2 - j], op[j]).start()
            for j in range(outer - 1):
                both(remote(osend, orecv.at[j], o_ss.at[j], o_rs.at[j], op[j]))
            v = osend[...].astype(f32)
            for j in range(outer - 1):
                v = v + orecv[j].astype(f32)
        fin[lax.rem(u, 3 * da), mine16] = v.astype(bf16)
        for j in range(3):
            a_copy(u, j).start()

    def take_y(u):
        both(y_copy(u))
        k = lax.rem(u, 2 * dy)
        zsum[lax.rem(u, 2 * dz)] = ys[k, :, half(p["y"])] + yrecv[k]
        for j in range(3):
            z_copy(u, j).start()

    def take_x(u):
        both(x_copy(u))
        k = lax.rem(u, 2 * dx)
        ys[lax.rem(u, 2 * dy)] = xs[k, p["x"]] + xrecv[k]
        y_copy(u).start()

    def take_c(u):
        both(c_copy(u))
        k = lax.rem(u, 2 * dc)
        kx = lax.rem(u, 2 * dx)
        own = lambda x: made[lax.rem(lax.div(u, 4), 2), x, p["c"], m16(lax.rem(u, 4) * R, R)]
        o = 1 - p["x"]
        xs[kx, o] = own(o) + crecv[k, o]
        x_copy(u).start()
        xs[kx, p["x"]] = own(p["x"]) + crecv[k, p["x"]]

    def make(m):
        slot = lax.rem(m, 2)
        g = lax.div(m, 3)
        r = lax.rem(m, 3)
        cols = pl.ds(pl.multiple_of(r * MACRO, 128), MACRO)
        for e in (0, 1):
            w = buf[e]

            @pl.when(g == 1 - e)
            def _():
                if e == 0:
                    @pl.when(r == 0)
                    def _():
                        ready(load(0, "g"))
                for t in range(4):
                    made[slot, t // 2, t % 2] = dot(w["g"][t, :, cols], w["df"][...], 0, 0).astype(bf16)

            @pl.when(g == 3 - e)
            def _():
                @pl.when(r == 0)
                def _():
                    ready(load(e, "hb"))
                for t in range(4):
                    made[slot, t // 2, t % 2] = dot(w["hb"][:, cols], w["d"][t], 0, 0).astype(bf16)

            for rr in range(3):
                @pl.when(m == (5 - e) * 3 + rr)
                def _():
                    if rr == 0:
                        ready(load(e, "o"), load(e, "x"))
                    for t in range(4):
                        at = rr * MACRO
                        while at < (rr + 1) * MACRO:
                            j, off = at // 192, at % 192
                            n = min(192 - off, (rr + 1) * MACRO - at)
                            src = w["qkv"][j * D + t * 192 + off : j * D + t * 192 + off + n, :] if j < 3 else w["o"][t * 192 + off : t * 192 + off + n, :]
                            made[slot, t // 2, t % 2, at - rr * MACRO : at - rr * MACRO + n] = dot(
                                src, w["x"][...] if j < 3 else w["da"][...], 1, 0).astype(bf16)
                            at += n

        @pl.when(m == MACROS)
        def _():
            row = lambda e, i: sums[e, i : i + 1, :]
            shared = [row(e, i + k) for i in (2, 4, 6) for e in (0, 1) for k in (0, 1)]
            for t in range(4):
                v = [row(0, 0), row(0, 1), row(1, 0), row(1, 1), row(0, 8 + t), row(1, 8 + t)] + shared[3 * t : 3 * t + 3]
                v = jnp.concatenate(v + [jnp.zeros((7, D), f32)], axis=0)
                made[slot, t // 2, t % 2, 0:16] = v.astype(bf16)
                made[slot, t // 2, t % 2, 16:R] = jnp.zeros((R - 16, D), bf16)

    def fetch(u):
        @pl.when(lax.rem(u, 4) == 0)
        def _():
            make(lax.div(u, 4))

        c_copy(u).start()

    def step(s, _):
        when(s - lf - da, finished)
        when(s - lf, finish)
        when(s - la, take_z)
        when(s - lz, take_y)
        when(s - ly, take_x)
        when(s - lx, take_c)
        when(s, fetch)
        work(s)
        return _

    lax.fori_loop(0, STEPS + lf + da, step, 0)
    ready(dx_copy(0), dx_copy(1))
    x, c = p["x"], p["c"]
    own = rows_ref.at[pl.ds(0, 16)]
    sends = [remote(own, small_ref.at[x, c], t_ss.at[i], t_rs.at[i], dev) for i, dev in enumerate((sib, xp, diag))]
    for cp in sends:
        cp.start()
    small_ref[x, c] = rows_ref[0:16]
    for i, (a, b) in enumerate(((x, 1 - c), (1 - x, c), (1 - x, 1 - c))):
        sends[i].wait_send()
        remote(own, small_ref.at[a, b], t_ss.at[i], t_rs.at[i], sib).wait_recv()


def backward(w_all, dc, vec, kept, sizes, dp, cid=3):
    outer = dp // 8
    dma = pltpu.SemaphoreType.DMA
    lc, lx, ly, lz, la = (LAG[k] for k in "cxyza")
    no = max(outer - 1, 1)
    vm = lambda s, t=bf16: pltpu.VMEM(s, t)
    scratch = []
    for e in (0, 1):
        n = sizes[e][0] * sizes[e][1]
        scratch += [vm(kept[e][k].shape, kept[e][k].dtype) for k in held_names(e)]
        scratch += [vm((n, D)), vm((n, D)), vm((n, D), f32), vm((n, D), f32), vm((D, n))]
    args = [w_all, dc, vec] + [kept[e][k] for e in (0, 1) for k in KEPT]
    return pl.pallas_call(
        functools.partial(back_kernel, outer, sizes),
        out_shape=(SDS((MACROS, MACRO, D), bf16), SDS((R, D), bf16), SDS((2, 2, 16, D), bf16),
                   SDS(kept[0]["x"].shape, bf16), SDS(kept[1]["x"].shape, bf16)),
        in_specs=[ANY, VM, VM] + [ANY] * 24,
        out_specs=(ANY, VM, VM, ANY, ANY),
        scratch_shapes=scratch + [
            vm(kept[0]["p"].shape), *[vm(s) for s in W_SHAPES], vm((2, 16, D), f32), dma((2, 12)), dma((2,)), dma((24,)),
            vm((2, 2, 2, MACRO, D)), vm((2 * lc, 2, R, D)), vm((2 * lx, 2, R, D)), vm((2 * lx, R, D)),
            vm((2 * ly, R, D)), vm((2 * ly, R, HALF)), vm((2 * lz, R, HALF)), vm((2 * lz, 48, HALF)), vm((3 * la, R, HALF)),
            vm((16, HALF)), vm((no, 16, HALF)),
            dma((2 * lc,)), dma((2 * lc,)), dma((2 * lx,)), dma((2 * lx,)), dma((2 * ly,)), dma((2 * ly,)),
            dma((2 * lz,)), dma((2 * lz,)), dma((3 * la,)), dma((3 * la,)), dma((no,)), dma((no,)),
            dma((3 * la,)), dma((3 * la,)), dma((3 * la,)), dma((3,)), dma((3,)),
        ],
        compiler_params=pltpu.CompilerParams(collective_id=cid, has_side_effects=True, vmem_limit_bytes=VMEM_LIMIT),
    )(*args)


HD = 64
EPS = 1e-12


def dot(a, b, ca, cb):
    return lax.dot_general(a, b, (((ca,), (cb,)), ((), ())), preferred_element_type=f32)


def gelu_pair(u):
    a = jnp.abs(u) * 0.7071067811865476
    t = 1.0 / (1.0 + 0.3275911 * a)
    e = jnp.exp(-(a * a))
    poly = t * (0.254829592 + t * (-0.284496736 + t * (1.421413741 + t * (-1.453152027 + t * 1.061405429))))
    tail = 0.5 * poly * e
    cdf = jnp.where(u >= 0, 1.0 - tail, tail)
    return u * cdf, cdf + u * (e * 0.3989422804014327)


def loop(n, fn):
    def run(i, c):
        fn(i)
        return c

    lax.fori_loop(0, n, run, 0)


def norm(r, gain, shift):
    c = r - jnp.mean(r, axis=-1, keepdims=True)
    inv = lax.rsqrt(jnp.mean(c * c, axis=-1, keepdims=True) + EPS)
    n = c * inv
    return n * gain + shift, n, inv


def spot(seqs, length):
    tokens = seqs * length
    if length % 128 == 0:
        return length, seqs, 1
    return tokens, 1, seqs


W_SHAPES = ((3 * D, D), (D, D), (4, D, D), (4, D, D))


def weight_copies(e, w_ref, refs, sem, kind):
    base, q = 3 * (1 - e), D // 4
    dst = refs[kind]
    pairs = []
    for t in range(4):
        src = w_ref.at[t // 2, t % 2]
        if kind == 0:
            pairs += [(src.at[base, pl.ds(j * q, q)], dst.at[pl.ds(j * D + t * q, q)]) for j in range(3)]
        elif kind == 1:
            pairs.append((src.at[base, pl.ds(3 * q, q)], dst.at[pl.ds(t * q, q)]))
        else:
            pairs.append((src.at[base + kind - 1], dst.at[t]))
    first = (0, 12, 16, 20)[kind]
    return [pltpu.make_async_copy(a, b, sem.at[first + i]) for i, (a, b) in enumerate(pairs)]


def p_at(e, size, g, h):
    group, groups, _ = spot(*size)
    if groups == 1:
        return (h,)
    return (h // 3 if isinstance(h, int) else lax.div(h, 3),
            pl.ds(g * group if isinstance(g, int) else pl.multiple_of(g * group, group), group),
            pl.ds(pl.multiple_of((h % 3 if isinstance(h, int) else lax.rem(h, 3)) * group, 128), group))


def norm_back(dz, n, inv):
    return inv * (dz - jnp.mean(dz, axis=-1, keepdims=True) - n * jnp.mean(dz * n, axis=-1, keepdims=True))


CH = 6
PLAN = ((0, 1), (1, 1), (2, 1), (0, 0), (1, 0), (2, 0))
MADE = ("y", "qkv", "p", "o", "n1", "i1", "hb", "g", "d", "n2", "i2")


def made_shapes(size):
    t = size[0] * size[1]
    group, groups, _ = spot(*size)
    return dict(y=(t, D), qkv=(3 * D, t), p=(4, t, D) if groups > 1 else (12, group, group), o=(D, t), n1=(t, D), i1=(t, 1),
                hb=(t, D), g=(4, t, D), d=(4, t, D), n2=(t, D), i2=(t, 1))


def front_kernel(n, sizes, io_ref, up_ref, down_ref, b_ref, x0_ref, x1_ref, vec_ref, code_ref, *refs):
    (out_ref, dc_ref, loss_ref), refs = refs[:3], refs[3:]
    hbm = [dict(zip(MADE, refs[11 * e : 11 * e + 11])) for e in (0, 1)]
    refs = refs[22:]
    buf = [dict(zip(MADE, refs[11 * e : 11 * e + 11])) for e in (0, 1)]
    refs = refs[22:]
    (h0, f0, h1, f1, win, wout, up, down, bias_ref, bias_in, held, cls, full, codes, pay, w_sem, made_sem,
     x_ss, x_rs, y_ss, y_rs, z_ss, z_rs, y2_ss, y2_rs, z2_ss, z2_rs, sib_ss, sib_rs, f_ss, f_rs, b_ss, b_rs, in_sem, back_sem,
     r_ss, r_rs, g_ss, g_rs) = refs
    xin, hs, fs = (x0_ref, x1_ref), (h0, h1), (f0, f1)
    p = place()
    zb = lax.rem(p["z"], 2)
    sib, xp, yp = device(p, c=1 - p["c"]), device(p, x=1 - p["x"]), device(p, y=1 - p["y"])
    zp = device(p, z=p["z"] + 1 - 2 * zb)
    diag = device(p, x=1 - p["x"], c=1 - p["c"])
    ring = [lax.rem(p["dp"] + j, n) for j in range(1, n)]
    group4 = [lax.rem(p["t"] + j, 4) for j in range(1, 4)]
    greet([(q, p["t"]) for q in ring] + [(p["dp"], q) for q in group4])
    x, c, y = p["x"], p["c"], p["y"]
    quarter, half = D // 4, D // 8
    rows = lambda q: pl.ds(pl.multiple_of(q * quarter, 16), quarter)
    hrows = lambda q, k: pl.ds(pl.multiple_of(q * quarter + k * half, 16), half)
    mine, qy, qz, dg = y * 2 + zb, (1 - y) * 2 + zb, y * 2 + 1 - zb, (1 - y) * 2 + 1 - zb
    source = lambda h: (io_ref, up_ref, down_ref)[PLAN[h][0]].at[PLAN[h][1]]
    started = []

    def go(cp):
        cp.start()
        started.append(cp)

    for i, dev in enumerate((sib, xp, diag)):
        go(remote(b_ref, bias_ref.at[x, c], b_ss.at[i], b_rs.at[i], dev))
    for h in range(CH):
        go(remote(source(h).at[rows(mine)], out_ref.at[x, c, h, rows(mine)], x_ss.at[h], x_rs.at[h], xp))
        go(remote(source(h), out_ref.at[x, c, h], sib_ss.at[h], sib_rs.at[h], sib))
    ins = [pltpu.make_async_copy(source(h), held.at[h % 2], in_sem.at[h]) for h in range(CH)]
    backs = [pltpu.make_async_copy(held.at[h % 2], out_ref.at[x, c, h], back_sem.at[h]) for h in range(CH)]
    ins[0].start()
    ins[1].start()
    bias_ref[x, c] = b_ref[...]
    def bounce(h):
        ins[h].wait()
        backs[h].start()
        if h + 2 < CH:
            backs[h].wait()
            ins[h + 2].start()

    def whole(h, q, ss, rs, dev):
        a = out_ref.at[1 - x, c, h, rows(q)]
        return remote(a, a, ss, rs, dev)

    def part(h, q, k, ss, rs, dev):
        a = out_ref.at[1 - x, c, h, hrows(q, k)]
        return remote(a, a, ss.at[h], rs.at[h], dev)

    def first(h):
        whole(h, mine, x_ss.at[h], x_rs.at[h], xp).wait_recv()
        go(whole(h, mine, y_ss.at[h], y_rs.at[h], yp))
        go(whole(h, mine, z_ss.at[h], z_rs.at[h], zp))
        go(whole(h, mine, f_ss.at[h, 0], f_rs.at[h, 0], sib))

    def second(h):
        whole(h, qy, y_ss.at[h], y_rs.at[h], yp).wait_recv()
        go(part(h, qy, 1, z2_ss, z2_rs, zp))
        go(whole(h, qy, f_ss.at[h, 1], f_rs.at[h, 1], sib))
        whole(h, qz, z_ss.at[h], z_rs.at[h], zp).wait_recv()
        go(part(h, qz, 0, y2_ss, y2_rs, yp))
        go(whole(h, qz, f_ss.at[h, 2], f_rs.at[h, 2], sib))

    def third(h):
        part(h, dg, 0, y2_ss, y2_rs, yp).wait_recv()
        part(h, dg, 1, z2_ss, z2_rs, zp).wait_recv()
        go(whole(h, dg, f_ss.at[h, 3], f_rs.at[h, 3], sib))

    def arrived(h):
        a = out_ref.at[x, 1 - c, h]
        remote(a, a, sib_ss.at[h], sib_rs.at[h], sib).wait_recv()
        for i, q in enumerate((mine, qy, qz, dg)):
            a = out_ref.at[1 - x, 1 - c, h, rows(q)]
            remote(a, a, f_ss.at[h, i], f_rs.at[h, i], sib).wait_recv()
        if h >= CH - 2:
            backs[h].wait()

    def weights(e, kind):
        return weight_copies(e, out_ref, (win, wout, up, down), w_sem, kind)

    def begin(*copies):
        for cp in copies:
            cp.start()

    def ready(*copies):
        for cp in copies:
            cp.wait()

    def keep(e, *names):
        for k in names:
            cp = pltpu.make_async_copy(buf[e][k], hbm[e][k], made_sem.at[e, MADE.index(k)])
            cp.start()
            keeps.append(cp)

    keeps = []
    vec = lambda e, i: vec_ref[e, i : i + 1, :]

    def tokens(e, b):
        m = spot(*sizes[e])[0]
        return pl.ds(b * m, m)

    def project(e, i):
        r = pl.ds(pl.multiple_of(i * 256, 256), 256)
        ones = jnp.ones((16, xin[e].shape[0]), bf16)
        bias = bias_in[e, lax.div(i, 3), :, pl.ds(pl.multiple_of(lax.rem(i, 3) * 256, 128), 256)]
        v = (dot(win[r, :], xin[e][...], 1, 1) + dot(bias, ones, 0, 0)).astype(bf16)
        buf[e]["qkv"][r, :] = v * jnp.where(i < 3, 0.125, 1.0).astype(bf16)

    def heads(e, g, i):
        group, groups, per = spot(*sizes[e])
        tok, w = tokens(e, g), buf[e]
        for k in range(2):
            h = i * 2 + k
            at = lambda base: pl.ds(pl.multiple_of(base + h * HD, HD), HD)
            s = dot(w["qkv"][at(D), tok], w["qkv"][at(0), tok], 0, 0)
            if per > 1:
                a = lax.broadcasted_iota(jnp.int32, s.shape, 0) // sizes[e][1]
                b = lax.broadcasted_iota(jnp.int32, s.shape, 1) // sizes[e][1]
                s = jnp.where(a == b, s, -1e30)
            ex = jnp.exp(s - jnp.max(s, axis=0, keepdims=True))
            pr = (ex * (1.0 / jnp.sum(ex, axis=0, keepdims=True))).astype(bf16)
            w["p"][p_at(e, sizes[e], g, h)] = pr
            w["o"][at(0), tok] = dot(w["qkv"][at(2 * D), tok], pr, 1, 0).astype(bf16)

    def out_norm(e, b):
        tok, w = tokens(e, b), buf[e]
        r = dot(w["o"][:, tok], wout[...], 0, 0) + xin[e][tok, :].astype(f32) + vec(e, 4)
        h, m, inv = norm(r, vec(e, 0), vec(e, 2))
        hs[e][tok, :] = h
        w["hb"][tok, :] = h.astype(bf16)
        w["n1"][tok, :] = m.astype(bf16)
        w["i1"][tok, :] = inv

    def hidden(e, i, b):
        tok, w = tokens(e, b), buf[e]
        ub = bias_ref[i // 2, i % 2, 0:16, :].astype(f32)[4 + e : 5 + e]
        for k in range(3):
            cc = slice(k * 256, (k + 1) * 256)
            u = dot(w["hb"][tok, :], up[i, :, cc], 1, 0) + ub[:, cc]
            g, d = gelu_pair(u)
            w["g"][i, tok, cc] = g.astype(bf16)
            w["d"][i, tok, cc] = d.astype(bf16)

    def shrink(e, i, b):
        tok, w = tokens(e, b), buf[e]
        part_ = dot(w["g"][i, tok, :], down[i], 1, 0)
        fs[e][tok, :] = part_ if i == 0 else fs[e][tok, :] + part_

    def norm2(e, b):
        tok, w = tokens(e, b), buf[e]
        v, m, inv = norm(hs[e][tok, :] + (fs[e][tok, :] + vec(e, 5)), vec(e, 1), vec(e, 3))
        w["y"][tok, :] = v.astype(bf16)
        w["n2"][tok, :] = m.astype(bf16)
        w["i2"][tok, :] = inv

    def projects(e, a, b):
        lax.fori_loop(a, b, lambda i, cc: (project(e, i), cc)[1], 0)

    def attend(e, g):
        loop(6, lambda i: heads(e, g, i))

    bounce(0)
    bounce(1)
    first(0)
    bounce(2)
    bounce(3)
    for i, (a, b) in enumerate(((x, 1 - c), (1 - x, c), (1 - x, 1 - c))):
        remote(b_ref, bias_ref.at[a, b], b_ss.at[i], b_rs.at[i], sib).wait_recv()
    for e in (0, 1):
        for j in range(3):
            if j == 1:
                bias_in[e, j] = jnp.zeros((16, D), bf16)
            else:
                r = 2 * e + j // 2
                got = [bias_ref[t // 2, t % 2].astype(f32)[r : r + 1] for t in range(4)]
                bias_in[e, j] = jnp.concatenate(got + [jnp.zeros((12, D), f32)], axis=0).astype(bf16)
    first(1)
    second(0)
    bounce(4)
    bounce(5)
    first(2)
    second(1)
    third(0)
    arrived(0)
    begin(*weights(1, 0), *weights(1, 1))
    ready(*weights(1, 0))
    projects(1, 0, 4)
    first(3)
    projects(1, 4, 9)
    second(2)
    attend(1, 0)
    third(1)
    arrived(1)
    first(4)
    begin(*weights(1, 2))
    attend(1, 1)
    second(3)
    first(5)
    attend(1, 2)
    keep(1, "qkv", "p", "o")
    third(2)
    arrived(2)
    begin(*weights(1, 3))
    ready(*weights(1, 1))
    for b in range(3):
        out_norm(1, b)
    second(4)
    keep(1, "n1", "i1", "hb")
    ready(*weights(1, 2), *weights(1, 3))
    for i in range(4):
        for b in range(3):
            hidden(1, i, b)
            shrink(1, i, b)
        if i == 0:
            third(3)
            arrived(3)
            begin(*weights(0, 0), *weights(0, 1))
        if i == 1:
            second(5)
        if i == 2:
            third(4)
            arrived(4)
    keep(1, "g", "d")
    begin(*weights(0, 2))
    third(5)
    arrived(5)
    begin(*weights(0, 3))
    for b in range(3):
        norm2(1, b)
    keep(1, "y", "n2", "i2")
    ready(*weights(0, 0))
    projects(0, 0, 9)
    attend(0, 0)
    keep(0, "qkv", "p", "o")
    ready(*weights(0, 1))
    out_norm(0, 0)
    keep(0, "n1", "i1", "hb")
    ready(*weights(0, 2), *weights(0, 3))
    for i in range(4):
        hidden(0, i, 0)
        shrink(0, i, 0)
    norm2(0, 0)
    nq, np_ = sizes[0][0], sizes[1][0]
    got = [buf[e]["y"][i * sizes[e][1] : i * sizes[e][1] + 16, :].astype(f32)[0:1] for e in (0, 1) for i in range(sizes[e][0])]
    blank = jnp.zeros((16 - 2 * (nq + np_), HALF), f32)
    pay[...] = (jnp.concatenate([v[:, :HALF] for v in got] + [v[:, HALF:] for v in got] + [blank], axis=0) + code_ref[...]).astype(bf16)
    place_of = lambda t, d: pl.ds(pl.multiple_of((t * n + d) * 16, 16), 16)
    here = cls.at[place_of(p["t"], p["dp"])]
    cls[place_of(p["t"], p["dp"]), :] = pay[...]
    for j, q in enumerate(ring):
        go(remote(pay, here, r_ss.at[j], r_rs.at[n - 2 - j], (q, p["t"])))
    keep(0, "g", "d", "y", "n2", "i2")
    for j, q in enumerate(ring):
        remote(pay, cls.at[place_of(p["t"], q)], r_ss.at[j], r_rs.at[j], (q, p["t"])).wait_recv()
    band = lambda x_, c_: cls.at[pl.ds(pl.multiple_of((x_ * 2 + c_) * n * 16, 16), n * 16)]
    go(remote(band(x, c), band(x, c), g_ss.at[0], g_rs.at[0], xp))
    go(remote(band(x, c), band(x, c), g_ss.at[1], g_rs.at[1], sib))
    remote(band(1 - x, c), band(1 - x, c), g_ss.at[0], g_rs.at[0], xp).wait_recv()
    go(remote(band(1 - x, c), band(1 - x, c), g_ss.at[2], g_rs.at[2], sib))
    remote(band(x, 1 - c), band(x, 1 - c), g_ss.at[1], g_rs.at[1], sib).wait_recv()
    remote(band(1 - x, 1 - c), band(1 - x, 1 - c), g_ss.at[2], g_rs.at[2], sib).wait_recv()

    total = 4 * n * 16
    scale = 2.7 * D**-0.5
    count = nq + np_

    def unfold(v):
        v = v.astype(f32)
        k = v.shape[0]
        return jnp.concatenate([v, pltpu.roll(v, k - count, 0), pltpu.roll(v[:, 0:128], k - 2 * count, 0)], axis=1)

    own = unfold(pay[...])
    own_code, own = own[:, D:], own[:, :D].astype(bf16)
    wide = unfold(cls[...])
    full[...] = wide[:, :D].astype(bf16)
    codes[...] = wide[:, D:]
    at = lax.broadcasted_iota(jnp.int32, (1, total), 1)
    block, pos = at // 16, at % 16
    name = (((block % n) * 4 + block // n) * np_ + (pos - nq)).astype(f32)
    live = jnp.logical_and(pos >= nq, pos < nq + np_)

    def marks(code, names):
        m = jnp.zeros((code.shape[0], names.shape[1]), f32)
        for k in range(4):
            m = m + (code[:, k : k + 1] * 16.0 + code[:, 4 + k : 5 + k] == names).astype(f32)
        return m

    def spread(block_rows, code):
        s = jnp.where(live, dot(block_rows, full[...], 1, 1) * scale, -1e30)
        top = jnp.max(s, axis=1, keepdims=True)
        ex = jnp.exp(s - top)
        m = jnp.where(live, marks(code, name), 0.0)
        return top, ex, jnp.sum(ex, axis=1, keepdims=True), m, jnp.sum(m * ex, axis=1, keepdims=True)

    row = lax.broadcasted_iota(jnp.int32, (16, 1), 0)
    top, ex, z, m, pz = spread(own, own_code)
    loss_ref[...] = jnp.broadcast_to(jnp.log(z) - jnp.log(pz), loss_ref.shape)
    ds = jnp.where(row < nq, ex / z - m * ex / pz, 0.0).astype(bf16)
    dc_ref[0] = dot(ds, full[...], 1, 0) * scale
    own_pos = lax.broadcasted_iota(jnp.int32, (1, 16), 1)
    own_name = ((p["dp"] * 4 + p["t"]) * np_ + (own_pos - nq)).astype(f32)
    own_live = jnp.logical_and(own_pos >= nq, own_pos < nq + np_)
    step = min(total, max(16, 131072 // total))
    dc_ref[1] = jnp.zeros((16, D), f32)

    def block_of(i):
        r = pl.ds(pl.multiple_of(i * step, 16), step)
        rows_ = full[r, :]
        code = codes[r, :]
        top, _, z, _, pz = spread(rows_, code)
        e_ = jnp.exp(dot(rows_, own, 1, 1) * scale - top)
        real = lax.broadcasted_iota(jnp.int32, (step, 1), 0) % 16 < nq
        ds = jnp.where(jnp.logical_and(real, own_live), e_ / z - marks(code, own_name) * e_ / pz, 0.0).astype(bf16)
        dc_ref[1] += dot(ds, rows_, 0, 0) * scale

    loop(total // step, block_of)
    for cp in keeps:
        cp.wait()
    for cp in started:
        cp.wait_send()


def forward(io, up, down, bias_rows, xs_, vec, code, sizes, n, cid=1):
    dma = pltpu.SemaphoreType.DMA
    vm = lambda s, t=bf16: pltpu.VMEM(s, t)
    shapes = [made_shapes(z) for z in sizes]
    kind = lambda k: f32 if k in ("i1", "i2") else bf16
    tok = [a * b for a, b in sizes]
    outs = [SDS(shapes[e][k], kind(k)) for e in (0, 1) for k in MADE]
    scratch = [vm(shapes[e][k], kind(k)) for e in (0, 1) for k in MADE]
    for t in tok:
        scratch += [vm((t, D), f32), vm((t, D), f32)]
    return pl.pallas_call(
        functools.partial(front_kernel, n, sizes),
        out_shape=[SDS((2, 2, CH, D, D), bf16), SDS((2, 16, D), f32), SDS((16, 128), f32)] + outs,
        in_specs=[ANY, ANY, ANY, VM, VM, VM, VM, VM],
        out_specs=[ANY, VM, VM] + [ANY] * 22,
        scratch_shapes=scratch + [vm(s) for s in W_SHAPES] + [
            vm((2, 2, 16, D)), vm((2, 3, 16, D)), vm((2, D, D)), vm((4 * n * 16, HALF)), vm((4 * n * 16, D)), vm((4 * n * 16, 128), f32), vm((16, HALF)), dma((24,)), dma((2, 11))]
        + [dma((CH,))] * 12 + [dma((CH, 4))] * 2 + [dma((3,))] * 2 + [dma((CH,))] * 2 + [dma((n - 1,))] * 2 + [dma((3,))] * 2,
        compiler_params=pltpu.CompilerParams(collective_id=cid, has_side_effects=True, vmem_limit_bytes=VMEM_LIMIT),
    )(io, up, down, bias_rows, *xs_, vec, code)


def body(n_dp, questions, passages, question_cotangent, passage_cotangent, positives, positive_counts,
         attention_in, attention_bias, attention_out, branch_biases, norm_gains, norm_shifts, up_weight, up_bias, down_weight):
    q4 = D // 4
    nq = questions.shape[0]
    sizes = (questions.shape[:2], passages.shape[:2])
    io = jnp.concatenate([attention_in.transpose(0, 1, 3, 2).reshape(2, 3 * q4, D), attention_out], axis=1)
    own_columns = jnp.arange(D, dtype=jnp.int32)[None, :] // q4 == lax.axis_index("tensor")
    att_rows = jnp.where(own_columns, jnp.tile(attention_bias.reshape(4, q4), (1, 4)), 0.0)
    bias_rows = jnp.concatenate([att_rows.astype(bf16), up_bias, jnp.zeros((10, D), bf16)])
    vec = jnp.concatenate([norm_gains, norm_shifts, branch_biases, jnp.zeros((2, 2, D), bf16)], axis=1).astype(f32)
    slots = positives.shape[1]
    live = jnp.arange(slots, dtype=jnp.int32)[None, :] < positive_counts[:, None]
    named = jnp.where(live, positives, -16)
    code = jnp.concatenate([named // 16, named % 16], axis=1)
    code = jnp.pad(code, ((2 * (nq + passages.shape[0]), 16 - 3 * nq - 2 * passages.shape[0]), (0, HALF - 2 * slots))).astype(f32)
    xs_ = (questions.reshape(-1, D), passages.reshape(-1, D))
    weights, dc, losses, *made = forward(io, up_weight, down_weight, bias_rows, xs_, vec, code, sizes, n_dp)
    kept = []
    for e, cot in enumerate((question_cotangent, passage_cotangent)):
        kept.append(dict(zip(MADE, made[11 * e : 11 * e + 11]), cot=cot.reshape(-1, D), x=xs_[e]))
    out, own_rows, small, *dxs = backward(weights, dc, vec, kept, sizes, n_dp)
    res = out.reshape(3, 2, D, D)
    own_small = own_rows[:16].astype(f32)
    rep = small.reshape(4, 16, D)[:, 6:9].reshape(12, D).astype(f32)
    att = lax.dynamic_slice_in_dim(own_small[0:4], lax.axis_index("tensor") * q4, q4, 1)
    return (
        kept[0]["y"].reshape(questions.shape), kept[1]["y"].reshape(passages.shape), losses[:nq, 0],
        dxs[0].reshape(questions.shape), dxs[1].reshape(passages.shape),
        res[2, :, : 3 * q4].reshape(2, 3, q4, D).transpose(0, 1, 3, 2).astype(f32), att.reshape(2, 2, q4),
        res[2, :, 3 * q4 :].astype(f32), rep[0:4].reshape(2, 2, D), rep[4:8].reshape(2, 2, D), rep[8:12].reshape(2, 2, D),
        res[1].astype(f32), own_small[4:6], res[0].astype(f32))


def solution(mesh):
    both = ("dp", "tensor")
    seq, rep = P(both, None, None), P()
    w4, w3, o3 = P(None, None, None, "tensor"), P(None, None, "tensor"), P(None, "tensor", None)
    in_specs = (seq, seq, seq, seq, P(both, None), P(both), w4, w3, o3, rep, rep, rep, w3, P(None, "tensor"), o3)
    out_specs = (seq, seq, P(both), seq, seq, w4, w3, o3, rep, rep, rep, w3, P(None, "tensor"), o3)
    return jax.shard_map(functools.partial(body, mesh.shape["dp"]), mesh=mesh, in_specs=in_specs, out_specs=out_specs, check_vma=False)
```

```python
import functools

import jax
import jax.numpy as jnp
from jax import lax
from jax.experimental import pallas as pl
from jax.experimental.pallas import tpu as pltpu
from jax.sharding import PartitionSpec as P

D = 768
MESH = pl.DeviceIdType.MESH
bf16, f32 = jnp.bfloat16, jnp.float32
VM = pl.BlockSpec(memory_space=pltpu.VMEM)
ANY = pl.BlockSpec(memory_space=pl.ANY)
SDS = jax.ShapeDtypeStruct


def place():
    dp, t = lax.axis_index("dp"), lax.axis_index("tensor")
    return dict(dp=dp, t=t, x=lax.div(t, 2), c=lax.rem(t, 2), y=lax.rem(dp, 2),
                z=lax.rem(lax.div(dp, 2), 4), o=lax.div(dp, 8))


def device(p, c=None, x=None, y=None, z=None, o=None):
    g = lambda v, k: p[k] if v is None else v
    return (g(o, "o") * 8 + g(z, "z") * 2 + g(y, "y"), g(x, "x") * 2 + g(c, "c"))


def greet(peers):
    bar = pltpu.get_barrier_semaphore()
    for q in peers:
        pl.semaphore_signal(bar, inc=1, device_id=q, device_id_type=MESH)
    pl.semaphore_wait(bar, len(peers))


def remote(src, dst, ssem, rsem, dev):
    return pltpu.make_async_remote_copy(src, dst, ssem, rsem, device_id=dev, device_id_type=MESH)


R = 64
MACRO = 256
HALF = D // 2
MACROS = 18
STEPS = MACROS * 4 + 1
VMEM_LIMIT = 64 * 2**20
LAG = dict(c=2, x=3, y=3, z=3, a=3)


KEPT = ("cot", "n2", "i2", "d", "g", "hb", "n1", "i1", "qkv", "o", "x", "p")


def cls_row(sizes, e):
    return sizes[0][0] if e else 0


def held_names(e):
    return tuple(k for k in KEPT[:11] if e == 0 or k not in ("o", "x"))


def back_kernel(outer, sizes, *refs):
    w_ref, dc_ref, *vec_ref = refs[:5]
    hbm = [dict(zip(KEPT, refs[5 + 12 * e : 17 + 12 * e])) for e in (0, 1)]
    refs = refs[29:]
    (down_out, up_out, io_out, rows_ref, small_ref, *shared_ref), refs = refs[:8], refs[8:]
    dx_ref, refs = refs[:2], refs[2:]
    buf = []
    for e in (0, 1):
        names = held_names(e) + ("df", "da", "r", "dh", "do")
        buf.append(dict(zip(names, refs[: len(names)])))
        refs = refs[len(names) :]
    (p0_ref, win, wout, up, down, sums, load_sem, dx_sem, w_sem,
     made, crecv, xs, xrecv, ys, yrecv, zsum, zrecv, fin, osend, orecv,
     c_ss, c_rs, x_ss, x_rs, y_ss, y_rs, z_ss, z_rs, a_ss, a_rs, o_ss, o_rs, w_ss, w_rs, l_sem, t_ss, t_rs) = refs
    buf[1]["p"], buf[0]["p"] = buf[1]["g"], p0_ref
    buf[1]["o"], buf[1]["x"] = buf[1]["n2"], buf[1]["n1"]

    def load(e, name):
        return pltpu.make_async_copy(hbm[e][name], buf[e][name], load_sem.at[e, KEPT.index(name)])

    def weights(e, kind):
        return weight_copies(e, w_ref, (win, wout, up, down), w_sem, kind)

    def begin(*copies):
        for cp in copies:
            cp.start()

    def ready(*copies):
        for cp in copies:
            cp.wait()

    begin(*[load(1, k) for k in ("cot", "n2", "i2")])
    begin(*[load(1, "d")], *weights(1, 3), *[load(1, k) for k in ("g",)], *weights(1, 2))
    begin(*[load(0, k) for k in ("cot", "n2", "i2")], *[load(1, k) for k in ("n1", "i1")], *weights(1, 1))
    begin(*[load(0, k) for k in ("g", "d")], *[load(1, k) for k in ("hb", "qkv")])
    begin(*[load(0, k) for k in ("hb", "n1", "i1", "qkv", "o", "x", "p")], *weights(1, 0))

    vec = lambda e, i: vec_ref[i // 2][e].astype(f32)[i % 2 : i % 2 + 1]
    col = lambda a: jnp.sum(a, axis=0, keepdims=True)
    sums[...] = jnp.zeros_like(sums)

    def add(e, row, v):
        sums[e, row : row + 1, :] += v

    def tokens(e, b):
        n = spot(*sizes[e])[0]
        return pl.ds(b * n, n) if isinstance(b, int) else pl.ds(pl.multiple_of(b * n, n), n)

    def norm2(e, b):
        group, groups, per = spot(*sizes[e])
        w, tok = buf[e], tokens(e, b)
        dy = w["cot"][tok, :].astype(f32)
        pos = lax.broadcasted_iota(jnp.int32, (group, 1), 0)
        for k in range(per):
            dy = dy + jnp.where(pos == k * sizes[e][1], dc_ref[e, cls_row(sizes, e) + b * per + k : cls_row(sizes, e) + b * per + k + 1, :], 0.0)
        n = w["n2"][tok, :].astype(f32)
        add(e, 5, col(dy * n))
        add(e, 7, col(dy))
        r2 = norm_back(dy * vec(e, 1), n, w["i2"][tok, :])
        w["r"][tok, :] = r2
        df = r2.astype(bf16)
        w["df"][tok, :] = df
        add(e, 3, col(df.astype(f32)))

    def hidden(e, i, b):
        w, tok = buf[e], tokens(e, b)
        for k in range(3):
            c = slice(k * 256, (k + 1) * 256)
            du = (dot(w["df"][tok, :], down[i, c, :], 1, 1) * w["d"][i, tok, c].astype(f32)).astype(bf16)
            w["d"][i, tok, c] = du
            sums[e, pl.ds(8 + i, 1), c] += col(du.astype(f32))
        part = dot(w["d"][i, tok, :], up[i], 1, 1)
        w["dh"][tok, :] = jnp.where(i == 0, part, w["dh"][tok, :] + part)

    def norm1(e, b):
        w, tok = buf[e], tokens(e, b)
        dh = w["dh"][tok, :] + w["r"][tok, :]
        n = w["n1"][tok, :].astype(f32)
        add(e, 4, col(dh * n))
        add(e, 6, col(dh))
        r1 = norm_back(dh * vec(e, 0), n, w["i1"][tok, :])
        w["r"][tok, :] = r1
        da = r1.astype(bf16)
        w["da"][tok, :] = da
        add(e, 2, col(da.astype(f32)))
        w["do"][:, tok] = dot(wout[...], da, 1, 1).astype(bf16)

    def head(e, g, h):
        w, tok = buf[e], tokens(e, g)
        at = lambda base: pl.ds(pl.multiple_of(base + h * HD, HD), HD)
        q, kk, vv, do = w["qkv"][at(0), tok], w["qkv"][at(D), tok], w["qkv"][at(2 * D), tok], w["do"][at(0), tok]
        pb = w["p"][p_at(e, sizes[e], g, h)]
        p = pb.astype(f32)
        dp = dot(vv, do, 0, 0)
        ds = (p * (dp - jnp.sum(p * dp, axis=0, keepdims=True))).astype(bf16)
        w["qkv"][at(0), tok] = (dot(kk, ds, 1, 0) * 0.125).astype(bf16)
        w["qkv"][at(D), tok] = dot(q, ds, 1, 1).astype(bf16)
        w["qkv"][at(2 * D), tok] = dot(do, pb, 1, 1).astype(bf16)

    def input_back(e, b):
        w, tok = buf[e], tokens(e, b)
        w["cot"][tok, :] = (dot(w["qkv"][:, tok], win[...], 0, 0) + w["r"][tok, :]).astype(bf16)

    def dx_copy(e):
        return pltpu.make_async_copy(buf[e]["cot"], dx_ref[e], dx_sem.at[e])

    def bias_sums(e):
        w = buf[e]
        ones = jnp.ones((8, w["da"].shape[0]), bf16)
        add(e, 0, dot(ones, w["qkv"][0:D, :], 1, 1)[0:1])
        add(e, 1, dot(ones, w["qkv"][2 * D :, :], 1, 1)[0:1])

    def at_step(s, first, fn, count=1):
        @pl.when(jnp.logical_and(s >= first, s < first + count))
        def _():
            fn(s - first)

    def work(s):
        @pl.when(jnp.logical_and(s < 16, lax.rem(s, 4) > 0))
        def _():
            idx = lax.div(s, 4) * 3 + lax.rem(s, 4) - 1
            hidden(1, lax.div(idx, 3), lax.rem(idx, 3))

        def s4(_):
            ready(*[load(0, k) for k in ("cot", "n2", "i2")])
            norm2(0, 0)

        def s9(_):
            begin(load(1, "p"))

        def s16(_):
            begin(*weights(0, 3), *weights(0, 2))
            ready(*[load(1, k) for k in ("n1", "i1")], *weights(1, 1))

        def s20(_):
            begin(load(1, "x"), *weights(0, 1))
            ready(*weights(0, 3), *weights(0, 2), load(0, "d"))

        def s25(_):
            ready(load(0, "n1"), load(0, "i1"), *weights(0, 1))
            norm1(0, 0)

        def s26(_):
            ready(load(1, "qkv"), load(1, "p"))

        def att1(a):
            for k in range(2):
                head(1, lax.div(a, 6), lax.rem(a, 6) * 2 + k)

        def s45(_):
            bias_sums(1)
            ready(*weights(1, 0))

        def s49(_):
            begin(dx_copy(1))
            begin(*weights(0, 0))
            ready(load(0, "qkv"), load(0, "p"))

        def att0(a):
            for k in range(2):
                head(0, 0, a * 2 + k)

        def s57(_):
            bias_sums(0)
            ready(*weights(0, 0))
            input_back(0, 0)
            begin(dx_copy(0))

        at_step(s, 4, s4)
        at_step(s, 9, s9)
        at_step(s, 16, s16)
        at_step(s, 17, lambda b: norm1(1, b), 3)
        at_step(s, 20, s20)
        at_step(s, 21, lambda i: hidden(0, i, 0), 4)
        at_step(s, 25, s25)
        at_step(s, 26, s26)
        at_step(s, 27, att1, 18)
        at_step(s, 45, s45)
        at_step(s, 46, lambda b: input_back(1, b), 3)
        at_step(s, 49, s49)
        at_step(s, 51, att0, 6)
        at_step(s, 57, s57)

    ready(*[load(1, k) for k in ("cot", "n2", "i2")])
    for b in range(3):
        norm2(1, b)
    begin(load(1, "o"))
    ready(load(1, "d"), load(1, "g"), *weights(1, 3), *weights(1, 2))

    p = place()
    sib, xp, yp = device(p, c=1 - p["c"]), device(p, x=1 - p["x"]), device(p, y=1 - p["y"])
    zs = [lax.rem(p["z"] + j, 4) for j in (1, 2, 3)]
    zp = [device(p, z=v) for v in zs]
    op = [device(p, o=lax.rem(p["o"] + j, outer)) for j in range(1, outer)]
    diag = device(p, x=1 - p["x"], c=1 - p["c"])
    greet([sib, xp, yp, diag] + zp + op)
    dc, dx, dy, dz, da = (LAG[k] for k in "cxyza")
    lx = dc
    ly = lx + dx
    lz = ly + dy
    la = lz + dz
    lf = la + da
    m16 = lambda v, n: pl.ds(pl.multiple_of(v, 16), n)
    mine16 = m16(p["z"] * 16, 16)
    half = lambda y: pl.ds(pl.multiple_of(y * HALF, 128), HALF)

    def made_at(u, c):
        return made.at[lax.rem(lax.div(u, 4), 2), :, c, m16(lax.rem(u, 4) * R, R)]

    def c_copy(u):
        k = lax.rem(u, 2 * dc)
        return remote(made_at(u, 1 - p["c"]), crecv.at[k], c_ss.at[k], c_rs.at[k], sib)

    def x_copy(u):
        k = lax.rem(u, 2 * dx)
        return remote(xs.at[k, 1 - p["x"]], xrecv.at[k], x_ss.at[k], x_rs.at[k], xp)

    def y_copy(u):
        k = lax.rem(u, 2 * dy)
        return remote(ys.at[k, :, half(1 - p["y"])], yrecv.at[k], y_ss.at[k], y_rs.at[k], yp)

    def z_copy(u, j):
        k = lax.rem(u, 2 * dz)
        return remote(zsum.at[k, m16(zs[j] * 16, 16)], zrecv.at[k, m16(32 - 16 * j, 16)], z_ss.at[k], z_rs.at[k], zp[j])

    def z_all(u):
        k = lax.rem(u, 2 * dz)
        return remote(zsum.at[k, m16(0, 48)], zrecv.at[k], z_ss.at[k], z_rs.at[k], zp[0])

    def a_copy(u, j):
        k = lax.rem(u, 3 * da)
        a = fin.at[k, mine16]
        return remote(a, a, a_ss.at[k], a_rs.at[k], zp[j])

    def a_all(u):
        k = lax.rem(u, 3 * da)
        a = fin.at[k, m16(0, 48)]
        return remote(a, a, a_ss.at[k], a_rs.at[k], zp[0])

    def both(c):
        c.wait_send()
        c.wait_recv()

    def targets(u):
        m, g = lax.div(u, 4), lax.div(u, 12)
        at = m16(lax.rem(m, 3) * MACRO + lax.rem(u, 4) * R, R)
        found = [(lax.div(g, 2) == k, ref.at[1 - lax.rem(g, 2), at, half(p["y"])]) for k, ref in enumerate((down_out, up_out, io_out))]
        return found + [(u == STEPS - 1, rows_ref.at[:, half(p["y"])])]

    def w_remote(u, dst):
        k = lax.rem(u, 3 * da)
        return remote(fin.at[k], dst, w_ss.at[k], w_rs.at[k], yp)

    def w_local(u, dst):
        k = lax.rem(u, 3 * da)
        return pltpu.make_async_copy(fin.at[k], dst, l_sem.at[k])

    def when(u, fn, n=STEPS):
        @pl.when(jnp.logical_and(u >= 0, u < n))
        def _():
            fn(u)

    def finish(u):
        both(a_all(u))
        for here, dst in targets(u):
            @pl.when(here)
            def _():
                w_remote(u, dst).start()
                w_local(u, dst).start()

    def finished(u):
        for here, dst in targets(u):
            @pl.when(here)
            def _():
                both(w_remote(u, dst))
                w_local(u, dst).wait()

    def take_z(u):
        both(z_all(u))
        k = lax.rem(u, 2 * dz)
        v = zsum[k, mine16].astype(f32)
        for j in range(3):
            v = v + zrecv[k, 16 * j : 16 * j + 16].astype(f32)
        if outer > 1:
            osend[...] = v.astype(bf16)
            for j in range(outer - 1):
                remote(osend, orecv.at[outer - 2 - j], o_ss.at[j], o_rs.at[outer - 2 - j], op[j]).start()
            for j in range(outer - 1):
                both(remote(osend, orecv.at[j], o_ss.at[j], o_rs.at[j], op[j]))
            v = osend[...].astype(f32)
            for j in range(outer - 1):
                v = v + orecv[j].astype(f32)
        fin[lax.rem(u, 3 * da), mine16] = v.astype(bf16)
        for j in range(3):
            a_copy(u, j).start()

    def take_y(u):
        both(y_copy(u))
        k = lax.rem(u, 2 * dy)
        zsum[lax.rem(u, 2 * dz)] = ys[k, :, half(p["y"])] + yrecv[k]
        for j in range(3):
            z_copy(u, j).start()

    def take_x(u):
        both(x_copy(u))
        k = lax.rem(u, 2 * dx)
        ys[lax.rem(u, 2 * dy)] = xs[k, p["x"]] + xrecv[k]
        y_copy(u).start()

    def take_c(u):
        both(c_copy(u))
        k = lax.rem(u, 2 * dc)
        kx = lax.rem(u, 2 * dx)
        own = lambda x: made[lax.rem(lax.div(u, 4), 2), x, p["c"], m16(lax.rem(u, 4) * R, R)]
        o = 1 - p["x"]
        xs[kx, o] = own(o) + crecv[k, o]
        x_copy(u).start()
        xs[kx, p["x"]] = own(p["x"]) + crecv[k, p["x"]]

    def make(m):
        slot = lax.rem(m, 2)
        g = lax.div(m, 3)
        r = lax.rem(m, 3)
        cols = pl.ds(pl.multiple_of(r * MACRO, 128), MACRO)
        for e in (0, 1):
            w = buf[e]

            @pl.when(g == 1 - e)
            def _():
                if e == 0:
                    @pl.when(r == 0)
                    def _():
                        ready(load(0, "g"))
                for t in range(4):
                    made[slot, t // 2, t % 2] = dot(w["g"][t, :, cols], w["df"][...], 0, 0).astype(bf16)

            @pl.when(g == 3 - e)
            def _():
                @pl.when(r == 0)
                def _():
                    ready(load(e, "hb"))
                for t in range(4):
                    made[slot, t // 2, t % 2] = dot(w["hb"][:, cols], w["d"][t], 0, 0).astype(bf16)

            for rr in range(3):
                @pl.when(m == (5 - e) * 3 + rr)
                def _():
                    if rr == 0:
                        ready(load(e, "o"), load(e, "x"))
                    for t in range(4):
                        at = rr * MACRO
                        while at < (rr + 1) * MACRO:
                            j, off = at // 192, at % 192
                            n = min(192 - off, (rr + 1) * MACRO - at)
                            src = w["qkv"][j * D + t * 192 + off : j * D + t * 192 + off + n, :] if j < 3 else w["o"][t * 192 + off : t * 192 + off + n, :]
                            made[slot, t // 2, t % 2, at - rr * MACRO : at - rr * MACRO + n] = dot(
                                src, w["x"][...] if j < 3 else w["da"][...], 1, 0).astype(bf16)
                            at += n

        @pl.when(m == MACROS)
        def _():
            row = lambda e, i: sums[e, i : i + 1, :]
            shared = [row(e, i + k) for i in (2, 4, 6) for e in (0, 1) for k in (0, 1)]
            for t in range(4):
                v = [row(0, 0), row(0, 1), row(1, 0), row(1, 1), row(0, 8 + t), row(1, 8 + t)] + shared[3 * t : 3 * t + 3]
                v = jnp.concatenate(v + [jnp.zeros((7, D), f32)], axis=0)
                made[slot, t // 2, t % 2, 0:16] = v.astype(bf16)
                made[slot, t // 2, t % 2, 16:R] = jnp.zeros((R - 16, D), bf16)

    def fetch(u):
        @pl.when(lax.rem(u, 4) == 0)
        def _():
            make(lax.div(u, 4))

        c_copy(u).start()

    def step(s, _):
        when(s - lf - da, finished)
        when(s - lf, finish)
        when(s - la, take_z)
        when(s - lz, take_y)
        when(s - ly, take_x)
        when(s - lx, take_c)
        when(s, fetch)
        work(s)
        return _

    lax.fori_loop(0, STEPS + lf + da, step, 0)
    ready(dx_copy(0), dx_copy(1))
    x, c = p["x"], p["c"]
    own = rows_ref.at[pl.ds(0, 16)]
    sends = [remote(own, small_ref.at[x, c], t_ss.at[i], t_rs.at[i], dev) for i, dev in enumerate((sib, xp, diag))]
    for cp in sends:
        cp.start()
    small_ref[x, c] = rows_ref[0:16]
    for i, (a, b) in enumerate(((x, 1 - c), (1 - x, c), (1 - x, 1 - c))):
        sends[i].wait_send()
        remote(own, small_ref.at[a, b], t_ss.at[i], t_rs.at[i], sib).wait_recv()
    got = [small_ref[t // 2, t % 2].astype(f32) for t in range(4)]
    for r in range(12):
        shared_ref[r // 4][(r // 2) % 2, r % 2 : r % 2 + 1] = got[r // 3][6 + r % 3 : 7 + r % 3]


def backward(w_all, dc, vec, kept, sizes, dp, cid=3):
    outer = dp // 8
    dma = pltpu.SemaphoreType.DMA
    lc, lx, ly, lz, la = (LAG[k] for k in "cxyza")
    no = max(outer - 1, 1)
    vm = lambda s, t=bf16: pltpu.VMEM(s, t)
    scratch = []
    for e in (0, 1):
        n = sizes[e][0] * sizes[e][1]
        scratch += [vm(kept[e][k].shape, kept[e][k].dtype) for k in held_names(e)]
        scratch += [vm((n, D)), vm((n, D)), vm((n, D), f32), vm((n, D), f32), vm((D, n))]
    args = [w_all, dc, *vec] + [kept[e][k] for e in (0, 1) for k in KEPT]
    return pl.pallas_call(
        functools.partial(back_kernel, outer, sizes),
        out_shape=(*[SDS((2, D, D), bf16)] * 3, SDS((R, D), bf16), SDS((2, 2, 16, D), bf16), *[SDS((2, 2, D), f32)] * 3,
                   SDS(kept[0]["x"].shape, bf16), SDS(kept[1]["x"].shape, bf16)),
        in_specs=[ANY] + [VM] * 4 + [ANY] * 24,
        out_specs=(ANY, ANY, ANY, VM, VM, VM, VM, VM, ANY, ANY),
        scratch_shapes=scratch + [
            vm(kept[0]["p"].shape), *[vm(s) for s in W_SHAPES], vm((2, 16, D), f32), dma((2, 12)), dma((2,)), dma((24,)),
            vm((2, 2, 2, MACRO, D)), vm((2 * lc, 2, R, D)), vm((2 * lx, 2, R, D)), vm((2 * lx, R, D)),
            vm((2 * ly, R, D)), vm((2 * ly, R, HALF)), vm((2 * lz, R, HALF)), vm((2 * lz, 48, HALF)), vm((3 * la, R, HALF)),
            vm((16, HALF)), vm((no, 16, HALF)),
            dma((2 * lc,)), dma((2 * lc,)), dma((2 * lx,)), dma((2 * lx,)), dma((2 * ly,)), dma((2 * ly,)),
            dma((2 * lz,)), dma((2 * lz,)), dma((3 * la,)), dma((3 * la,)), dma((no,)), dma((no,)),
            dma((3 * la,)), dma((3 * la,)), dma((3 * la,)), dma((3,)), dma((3,)),
        ],
        compiler_params=pltpu.CompilerParams(collective_id=cid, has_side_effects=True, vmem_limit_bytes=VMEM_LIMIT),
    )(*args)


HD = 64
EPS = 1e-12


def dot(a, b, ca, cb):
    return lax.dot_general(a, b, (((ca,), (cb,)), ((), ())), preferred_element_type=f32)


def gelu_pair(u):
    a = jnp.abs(u) * 0.7071067811865476
    t = 1.0 / (1.0 + 0.3275911 * a)
    e = jnp.exp(-(a * a))
    poly = t * (0.254829592 + t * (-0.284496736 + t * (1.421413741 + t * (-1.453152027 + t * 1.061405429))))
    tail = 0.5 * poly * e
    cdf = jnp.where(u >= 0, 1.0 - tail, tail)
    return u * cdf, cdf + u * (e * 0.3989422804014327)


def loop(n, fn):
    def run(i, c):
        fn(i)
        return c

    lax.fori_loop(0, n, run, 0)


def norm(r, gain, shift):
    c = r - jnp.mean(r, axis=-1, keepdims=True)
    inv = lax.rsqrt(jnp.mean(c * c, axis=-1, keepdims=True) + EPS)
    n = c * inv
    return n * gain + shift, n, inv


def spot(seqs, length):
    tokens = seqs * length
    if length % 128 == 0:
        return length, seqs, 1
    return tokens, 1, seqs


W_SHAPES = ((3 * D, D), (D, D), (4, D, D), (4, D, D))


def weight_copies(e, w_ref, refs, sem, kind):
    base, q = 3 * (1 - e), D // 4
    dst = refs[kind]
    pairs = []
    for t in range(4):
        src = w_ref.at[t // 2, t % 2]
        if kind == 0:
            pairs += [(src.at[base, pl.ds(j * q, q)], dst.at[pl.ds(j * D + t * q, q)]) for j in range(3)]
        elif kind == 1:
            pairs.append((src.at[base, pl.ds(3 * q, q)], dst.at[pl.ds(t * q, q)]))
        else:
            pairs.append((src.at[base + kind - 1], dst.at[t]))
    first = (0, 12, 16, 20)[kind]
    return [pltpu.make_async_copy(a, b, sem.at[first + i]) for i, (a, b) in enumerate(pairs)]


def p_at(e, size, g, h):
    group, groups, _ = spot(*size)
    if groups == 1:
        return (h,)
    return (h // 3 if isinstance(h, int) else lax.div(h, 3),
            pl.ds(g * group if isinstance(g, int) else pl.multiple_of(g * group, group), group),
            pl.ds(pl.multiple_of((h % 3 if isinstance(h, int) else lax.rem(h, 3)) * group, 128), group))


def norm_back(dz, n, inv):
    return inv * (dz - jnp.mean(dz, axis=-1, keepdims=True) - n * jnp.mean(dz * n, axis=-1, keepdims=True))


CH = 6
PLAN = ((0, 1), (1, 1), (2, 1), (0, 0), (1, 0), (2, 0))
PIECES = [(h, 0, D) for h in range(CH)]
NP_ = len(PIECES)
MADE = ("y", "qkv", "p", "o", "n1", "i1", "hb", "g", "d", "n2", "i2")


def made_shapes(size):
    t = size[0] * size[1]
    group, groups, _ = spot(*size)
    return dict(y=(t, D), qkv=(3 * D, t), p=(4, t, D) if groups > 1 else (12, group, group), o=(D, t), n1=(t, D), i1=(t, 1),
                hb=(t, D), g=(4, t, D), d=(4, t, D), n2=(t, D), i2=(t, 1))


def front_kernel(n, sizes, io_ref, up_ref, down_ref, b_ref, x0_ref, x1_ref, *refs):
    (*vec_ref, code_ref), refs = refs[:4], refs[4:]
    (out_ref, dc_ref, loss_ref), refs = refs[:3], refs[3:]
    hbm = [dict(zip(MADE, refs[11 * e : 11 * e + 11])) for e in (0, 1)]
    refs = refs[22:]
    buf = [dict(zip(MADE, refs[11 * e : 11 * e + 11])) for e in (0, 1)]
    refs = refs[22:]
    (h0, f0, h1, f1, win, wout, up, down, bias_ref, bias_in, held, cls, full, codes, pay, w_sem, made_sem,
     x_ss, x_rs, y_ss, y_rs, z_ss, z_rs, y2_ss, y2_rs, z2_ss, z2_rs, sib_ss, sib_rs, f_ss, f_rs, b_ss, b_rs, in_sem, back_sem,
     r_ss, r_rs, g_ss, g_rs, x2_ss, x2_rs) = refs
    xin, hs, fs = (x0_ref, x1_ref), (h0, h1), (f0, f1)
    p = place()
    zb = lax.rem(p["z"], 2)
    sib, xp, yp = device(p, c=1 - p["c"]), device(p, x=1 - p["x"]), device(p, y=1 - p["y"])
    zp = device(p, z=p["z"] + 1 - 2 * zb)
    diag = device(p, x=1 - p["x"], c=1 - p["c"])
    ring = [lax.rem(p["dp"] + j, n) for j in range(1, n)]
    group4 = [lax.rem(p["t"] + j, 4) for j in range(1, 4)]
    greet([(q, p["t"]) for q in ring] + [(p["dp"], q) for q in group4])
    x, c, y = p["x"], p["c"], p["y"]
    def rows(i, q):
        _, r, k = PIECES[i]
        return pl.ds(pl.multiple_of(r + q * (k // 4), 16), k // 4)

    def hrows(i, q, j):
        _, r, k = PIECES[i]
        return pl.ds(pl.multiple_of(r + q * (k // 4) + j * (k // 12), 16), k // 12)

    mine, qy, qz, dg = y * 2 + zb, (1 - y) * 2 + zb, y * 2 + 1 - zb, (1 - y) * 2 + 1 - zb
    source = lambda h: (io_ref, up_ref, down_ref)[PLAN[h][0]].at[PLAN[h][1]]
    started = []

    def go(cp):
        cp.start()
        started.append(cp)

    for i, dev in enumerate((sib, xp, diag)):
        go(remote(b_ref, bias_ref.at[x, c], b_ss.at[i], b_rs.at[i], dev))
    for i in range(NP_ + 1):
        if i < NP_:
            h = PIECES[i][0]
            go(remote(source(h).at[rows(i, mine)], out_ref.at[x, c, h, rows(i, mine)], x_ss.at[i], x_rs.at[i], xp))
            if PIECES[i][1] == 0:
                go(remote(source(h), out_ref.at[x, c, h], sib_ss.at[h], sib_rs.at[h], sib))
        if i > 0:
            h, r = PIECES[i - 1][0], hrows(i - 1, dg, 2)
            go(remote(source(h).at[r], out_ref.at[x, c, h, r], x2_ss.at[i - 1], x2_rs.at[i - 1], xp))
    ins = [pltpu.make_async_copy(source(h), held.at[h % 2], in_sem.at[h]) for h in range(CH)]
    backs = [pltpu.make_async_copy(held.at[h % 2], out_ref.at[x, c, h], back_sem.at[h]) for h in range(CH)]
    ins[0].start()
    ins[1].start()
    bias_ref[x, c] = b_ref[...]
    def bounce(h):
        ins[h].wait()
        backs[h].start()
        if h + 2 < CH:
            backs[h].wait()
            ins[h + 2].start()

    def whole(i, q, ss, rs, dev):
        a = out_ref.at[1 - x, c, PIECES[i][0], rows(i, q)]
        return remote(a, a, ss, rs, dev)

    def part(i, q, k, ss, rs, dev):
        a = out_ref.at[1 - x, c, PIECES[i][0], hrows(i, q, k)]
        return remote(a, a, ss.at[i], rs.at[i], dev)

    def first(i):
        whole(i, mine, x_ss.at[i], x_rs.at[i], xp).wait_recv()
        go(whole(i, mine, y_ss.at[i], y_rs.at[i], yp))
        go(whole(i, mine, z_ss.at[i], z_rs.at[i], zp))
        go(whole(i, mine, f_ss.at[i, 0], f_rs.at[i, 0], sib))

    def second(i):
        whole(i, qy, y_ss.at[i], y_rs.at[i], yp).wait_recv()
        go(part(i, qy, 1, z2_ss, z2_rs, zp))
        whole(i, qz, z_ss.at[i], z_rs.at[i], zp).wait_recv()
        go(part(i, qz, 0, y2_ss, y2_rs, yp))
        go(whole(i, qy, f_ss.at[i, 1], f_rs.at[i, 1], sib))
        go(whole(i, qz, f_ss.at[i, 2], f_rs.at[i, 2], sib))

    def third(i):
        part(i, dg, 0, y2_ss, y2_rs, yp).wait_recv()
        part(i, dg, 1, z2_ss, z2_rs, zp).wait_recv()
        part(i, dg, 2, x2_ss, x2_rs, xp).wait_recv()
        go(whole(i, dg, f_ss.at[i, 3], f_rs.at[i, 3], sib))

    def arrived(h):
        a = out_ref.at[x, 1 - c, h]
        remote(a, a, sib_ss.at[h], sib_rs.at[h], sib).wait_recv()
        for i in range(NP_):
            if PIECES[i][0] == h:
                for j, q in enumerate((mine, qy, qz, dg)):
                    a = out_ref.at[1 - x, 1 - c, h, rows(i, q)]
                    remote(a, a, f_ss.at[i, j], f_rs.at[i, j], sib).wait_recv()
        if h >= CH - 2:
            backs[h].wait()

    def weights(e, kind):
        return weight_copies(e, out_ref, (win, wout, up, down), w_sem, kind)

    def begin(*copies):
        for cp in copies:
            cp.start()

    def ready(*copies):
        for cp in copies:
            cp.wait()

    def keep(e, *names):
        for k in names:
            cp = pltpu.make_async_copy(buf[e][k], hbm[e][k], made_sem.at[e, MADE.index(k)])
            cp.start()
            keeps.append(cp)

    keeps = []
    vec = lambda e, i: vec_ref[i // 2][e].astype(f32)[i % 2 : i % 2 + 1]

    def tokens(e, b):
        m = spot(*sizes[e])[0]
        return pl.ds(b * m, m)

    def project(e, i):
        r = pl.ds(pl.multiple_of(i * 256, 256), 256)
        ones = jnp.ones((16, xin[e].shape[0]), bf16)
        bias = bias_in[e, lax.div(i, 3), :, pl.ds(pl.multiple_of(lax.rem(i, 3) * 256, 128), 256)]
        v = (dot(win[r, :], xin[e][...], 1, 1) + dot(bias, ones, 0, 0)).astype(bf16)
        buf[e]["qkv"][r, :] = v * jnp.where(i < 3, 0.125, 1.0).astype(bf16)

    def heads(e, g, i):
        group, groups, per = spot(*sizes[e])
        tok, w = tokens(e, g), buf[e]
        for k in range(2):
            h = i * 2 + k
            at = lambda base: pl.ds(pl.multiple_of(base + h * HD, HD), HD)
            s = dot(w["qkv"][at(D), tok], w["qkv"][at(0), tok], 0, 0)
            if per > 1:
                a = lax.broadcasted_iota(jnp.int32, s.shape, 0) // sizes[e][1]
                b = lax.broadcasted_iota(jnp.int32, s.shape, 1) // sizes[e][1]
                s = jnp.where(a == b, s, -1e30)
            ex = jnp.exp(s - jnp.max(s, axis=0, keepdims=True))
            pr = (ex * (1.0 / jnp.sum(ex, axis=0, keepdims=True))).astype(bf16)
            w["p"][p_at(e, sizes[e], g, h)] = pr
            w["o"][at(0), tok] = dot(w["qkv"][at(2 * D), tok], pr, 1, 0).astype(bf16)

    def out_norm(e, b):
        tok, w = tokens(e, b), buf[e]
        r = dot(w["o"][:, tok], wout[...], 0, 0) + xin[e][tok, :].astype(f32) + vec(e, 4)
        h, m, inv = norm(r, vec(e, 0), vec(e, 2))
        hs[e][tok, :] = h
        w["hb"][tok, :] = h.astype(bf16)
        w["n1"][tok, :] = m.astype(bf16)
        w["i1"][tok, :] = inv

    def hidden(e, i, b):
        tok, w = tokens(e, b), buf[e]
        ub = bias_ref[i // 2, i % 2, 0:16, :].astype(f32)[4 + e : 5 + e]
        for k in range(3):
            cc = slice(k * 256, (k + 1) * 256)
            u = dot(w["hb"][tok, :], up[i, :, cc], 1, 0) + ub[:, cc]
            g, d = gelu_pair(u)
            w["g"][i, tok, cc] = g.astype(bf16)
            w["d"][i, tok, cc] = d.astype(bf16)

    def shrink(e, i, b):
        tok, w = tokens(e, b), buf[e]
        part_ = dot(w["g"][i, tok, :], down[i], 1, 0)
        fs[e][tok, :] = part_ if i == 0 else fs[e][tok, :] + part_

    def norm2(e, b):
        tok, w = tokens(e, b), buf[e]
        v, m, inv = norm(hs[e][tok, :] + (fs[e][tok, :] + vec(e, 5)), vec(e, 1), vec(e, 3))
        w["y"][tok, :] = v.astype(bf16)
        w["n2"][tok, :] = m.astype(bf16)
        w["i2"][tok, :] = inv

    def projects(e, a, b):
        lax.fori_loop(a, b, lambda i, cc: (project(e, i), cc)[1], 0)

    def biases():
        for i, (a, b) in enumerate(((x, 1 - c), (1 - x, c), (1 - x, 1 - c))):
            remote(b_ref, bias_ref.at[a, b], b_ss.at[i], b_rs.at[i], sib).wait_recv()
        for e in (0, 1):
            for j in range(3):
                if j == 1:
                    bias_in[e, j] = jnp.zeros((16, D), bf16)
                else:
                    r = 2 * e + j // 2
                    got = [bias_ref[t // 2, t % 2].astype(f32)[r : r + 1] for t in range(4)]
                    bias_in[e, j] = jnp.concatenate(got + [jnp.zeros((12, D), f32)], axis=0).astype(bf16)

    def attend(e, g, lo, hi):
        lax.fori_loop(lo, hi, lambda i, cc: (heads(e, g, i), cc)[1], 0)

    tasks = []

    def task(name, us, needs, fn):
        tasks.append((name, us, tuple(needs), fn))

    for h in range(2):
        task(f"bounce{h}", 1.0, (), functools.partial(bounce, h))
    task("biases", 0.3, (), biases)
    for h in range(2, CH):
        task(f"bounce{h}", 1.0, (f"bounce{h - 2}",), functools.partial(bounce, h))
    for e in (1, 0):
        base = 0 if e else 3
        k, blocks, groups = (1.0, 3, 3) if e else (0.45, 1, 1)
        free = lambda *names: () if e else names
        task(f"w0{e}", 0.3, (f"arrived{base}", *free("project1")), lambda e=e: begin(*weights(e, 0)))
        task(f"w1{e}", 0.1, (f"arrived{base}", *free("out1")), lambda e=e: begin(*weights(e, 1)))
        task(f"w2{e}", 0.1, (f"arrived{base + 1}", *free("hidden1")), lambda e=e: begin(*weights(e, 2)))
        task(f"w3{e}", 0.1, (f"arrived{base + 2}", *free("shrink1")), lambda e=e: begin(*weights(e, 3)))
        task(f"r0{e}", 0.8, (f"w0{e}", "biases"), lambda e=e: ready(*weights(e, 0)))
        for i in range(3):
            last = "project%d" % e if i == 2 else "project%d_%d" % (e, i)
            task(last, 2.2 * k, (f"r0{e}",), lambda e=e, i=i: projects(e, 3 * i, 3 * i + 3))
        for g in range(groups):
            for half_ in (0, 1):
                task(f"att{e}_{g}_{half_}", 2.6, (f"project{e}",), lambda e=e, g=g, q=half_: attend(e, g, 3 * q, 3 * q + 3))
        every = [f"att{e}_{g}_{q}" for g in range(groups) for q in (0, 1)]
        task(f"keepa{e}", 0.1, every, lambda e=e: keep(e, "qkv", "p", "o"))
        task(f"r1{e}", 0.3, (f"w1{e}", *every), lambda e=e: ready(*weights(e, 1)))
        for b in range(blocks):
            task(f"out{e}" if b == blocks - 1 else f"out{e}_{b}", 1.4, (f"r1{e}",), lambda e=e, b=b: out_norm(e, b))
        task(f"keepb{e}", 0.1, (f"out{e}",), lambda e=e: keep(e, "n1", "i1", "hb"))
        task(f"r2{e}", 0.6, (f"w2{e}", f"out{e}"), lambda e=e: ready(*weights(e, 2)))
        task(f"r3{e}", 0.6, (f"w3{e}", f"out{e}"), lambda e=e: ready(*weights(e, 3)))
        for i in range(4):
            for b in range(blocks):
                end = i == 3 and b == blocks - 1
                task(f"hidden{e}" if end else f"hidden{e}_{i}_{b}", 1.2, (f"r2{e}",), lambda e=e, i=i, b=b: hidden(e, i, b))
        for i in range(4):
            for b in range(blocks):
                end = i == 3 and b == blocks - 1
                task(f"shrink{e}" if end else f"shrink{e}_{i}_{b}", 0.6,
                     (f"r3{e}", "hidden%d" % e if i == 3 and b == blocks - 1 else f"hidden{e}_{i}_{b}"),
                     lambda e=e, i=i, b=b: shrink(e, i, b))
        task(f"keepc{e}", 0.1, (f"hidden{e}",), lambda e=e: keep(e, "g", "d"))
        for b in range(blocks):
            task(f"norm{e}" if b == blocks - 1 else f"norm{e}_{b}", 0.8, (f"shrink{e}",), lambda e=e, b=b: norm2(e, b))
        task(f"keepd{e}", 0.1, (f"norm{e}",), lambda e=e: keep(e, "y", "n2", "i2"))

    span_ = [k * 2 * D * 2 / 4 / 75e3 for _, _, k in PIECES]
    at_x, at_x2, t_ = {}, {}, 3.0
    for i in range(NP_ + 1):
        if i < NP_:
            t_ += span_[i]
            at_x[i] = t_ + 1.5
        if i > 0:
            t_ += span_[i - 1] / 3
            at_x2[i - 1] = t_ + 1.5
    order = [("f", 0)]
    for i in range(NP_ + 2):
        order += [("f", i + 1)] if i + 1 < NP_ else []
        order += [("s", i)] if i < NP_ else []
        order += [("t", i - 1)] if 0 <= i - 1 < NP_ else []
    line, landed, done, now = 3.0, {}, set(), 3.0
    comm = {"f": first, "s": second, "t": third}
    while order or tasks:
        kind, i = order[0] if order else (None, None)
        due = {"f": lambda: at_x[i], "s": lambda: landed["f", i], "t": lambda: max(landed["s", i], at_x2[i])}[kind]() if kind else 1e9
        pick = next((k for k in tasks if all(d in done for d in k[2])), None)
        if due <= now or pick is None:
            now = max(now, due) + 0.25
            comm[kind](i)
            order.pop(0)
            if kind in "fs":
                line = max(line, now) + span_[i] / (1 if kind == "f" else 3)
                landed[kind, i] = line + 1.5
            elif i + 1 == NP_ or PIECES[i + 1][0] != PIECES[i][0]:
                arrived(PIECES[i][0])
                now += 0.8
                done.add(f"arrived{PIECES[i][0]}")
        else:
            pick[3]()
            now += pick[1]
            done.add(pick[0])
            tasks.remove(pick)
    nq, np_ = sizes[0][0], sizes[1][0]
    got = [buf[e]["y"][i * sizes[e][1] : i * sizes[e][1] + 16, :].astype(f32)[0:1] for e in (0, 1) for i in range(sizes[e][0])]
    blank = jnp.zeros((16 - 2 * (nq + np_), HALF), f32)
    pay[...] = (jnp.concatenate([v[:, :HALF] for v in got] + [v[:, HALF:] for v in got] + [blank], axis=0) + code_ref[...]).astype(bf16)
    place_of = lambda t, d: pl.ds(pl.multiple_of((t * n + d) * 16, 16), 16)
    here = cls.at[place_of(p["t"], p["dp"])]
    cls[place_of(p["t"], p["dp"]), :] = pay[...]
    for j, q in enumerate(ring):
        go(remote(pay, here, r_ss.at[j], r_rs.at[n - 2 - j], (q, p["t"])))
    for j, q in enumerate(ring):
        remote(pay, cls.at[place_of(p["t"], q)], r_ss.at[j], r_rs.at[j], (q, p["t"])).wait_recv()
    band = lambda x_, c_: cls.at[pl.ds(pl.multiple_of((x_ * 2 + c_) * n * 16, 16), n * 16)]
    go(remote(band(x, c), band(x, c), g_ss.at[0], g_rs.at[0], xp))
    go(remote(band(x, c), band(x, c), g_ss.at[1], g_rs.at[1], sib))
    remote(band(1 - x, c), band(1 - x, c), g_ss.at[0], g_rs.at[0], xp).wait_recv()
    go(remote(band(1 - x, c), band(1 - x, c), g_ss.at[2], g_rs.at[2], sib))
    remote(band(x, 1 - c), band(x, 1 - c), g_ss.at[1], g_rs.at[1], sib).wait_recv()
    remote(band(1 - x, 1 - c), band(1 - x, 1 - c), g_ss.at[2], g_rs.at[2], sib).wait_recv()

    total = 4 * n * 16
    scale = 2.7 * D**-0.5
    count = nq + np_

    def unfold(v):
        v = v.astype(f32)
        k = v.shape[0]
        return jnp.concatenate([v, pltpu.roll(v, k - count, 0), pltpu.roll(v[:, 0:128], k - 2 * count, 0)], axis=1)

    own = unfold(pay[...])
    own_code, own = own[:, D:], own[:, :D].astype(bf16)
    wide = unfold(cls[...])
    full[...] = wide[:, :D].astype(bf16)
    codes[...] = wide[:, D:]
    at = lax.broadcasted_iota(jnp.int32, (1, total), 1)
    block, pos = at // 16, at % 16
    name = (((block % n) * 4 + block // n) * np_ + (pos - nq)).astype(f32)
    live = jnp.logical_and(pos >= nq, pos < nq + np_)

    def marks(code, names):
        m = jnp.zeros((code.shape[0], names.shape[1]), f32)
        for k in range(4):
            m = m + (code[:, k : k + 1] * 16.0 + code[:, 4 + k : 5 + k] == names).astype(f32)
        return m

    def spread(block_rows, code):
        s = jnp.where(live, dot(block_rows, full[...], 1, 1) * scale, -1e30)
        top = jnp.max(s, axis=1, keepdims=True)
        ex = jnp.exp(s - top)
        m = jnp.where(live, marks(code, name), 0.0)
        return top, ex, jnp.sum(ex, axis=1, keepdims=True), m, jnp.sum(m * ex, axis=1, keepdims=True)

    row = lax.broadcasted_iota(jnp.int32, (16, 1), 0)
    top, ex, z, m, pz = spread(own, own_code)
    loss_ref[...] = jnp.broadcast_to(jnp.log(z) - jnp.log(pz), loss_ref.shape)
    ds = jnp.where(row < nq, ex / z - m * ex / pz, 0.0).astype(bf16)
    dc_ref[0] = dot(ds, full[...], 1, 0) * scale
    own_pos = lax.broadcasted_iota(jnp.int32, (1, 16), 1)
    own_name = ((p["dp"] * 4 + p["t"]) * np_ + (own_pos - nq)).astype(f32)
    own_live = jnp.logical_and(own_pos >= nq, own_pos < nq + np_)
    step = min(total, max(16, 131072 // total))
    dc_ref[1] = jnp.zeros((16, D), f32)

    def block_of(i):
        r = pl.ds(pl.multiple_of(i * step, 16), step)
        rows_ = full[r, :]
        code = codes[r, :]
        top, _, z, _, pz = spread(rows_, code)
        e_ = jnp.exp(dot(rows_, own, 1, 1) * scale - top)
        real = lax.broadcasted_iota(jnp.int32, (step, 1), 0) % 16 < nq
        ds = jnp.where(jnp.logical_and(real, own_live), e_ / z - marks(code, own_name) * e_ / pz, 0.0).astype(bf16)
        dc_ref[1] += dot(ds, rows_, 0, 0) * scale

    loop(total // step, block_of)
    for cp in keeps:
        cp.wait()
    for cp in started:
        cp.wait_send()


def forward(io, up, down, bias_rows, xs_, vec, code, sizes, n, cid=1):
    dma = pltpu.SemaphoreType.DMA
    vm = lambda s, t=bf16: pltpu.VMEM(s, t)
    shapes = [made_shapes(z) for z in sizes]
    kind = lambda k: f32 if k in ("i1", "i2") else bf16
    tok = [a * b for a, b in sizes]
    outs = [SDS(shapes[e][k], kind(k)) for e in (0, 1) for k in MADE]
    scratch = [vm(shapes[e][k], kind(k)) for e in (0, 1) for k in MADE]
    for t in tok:
        scratch += [vm((t, D), f32), vm((t, D), f32)]
    return pl.pallas_call(
        functools.partial(front_kernel, n, sizes),
        out_shape=[SDS((2, 2, CH, D, D), bf16), SDS((2, 16, D), f32), SDS((16, 128), f32)] + outs,
        in_specs=[ANY] * 3 + [VM] * 7,
        out_specs=[ANY, VM, VM] + [ANY] * 22,
        scratch_shapes=scratch + [vm(s) for s in W_SHAPES] + [
            vm((2, 2, 16, D)), vm((2, 3, 16, D)), vm((2, D, D)), vm((4 * n * 16, HALF)), vm((4 * n * 16, D)), vm((4 * n * 16, 128), f32), vm((16, HALF)), dma((24,)), dma((2, 11))]
        + [dma((NP_,))] * 10 + [dma((CH,))] * 2 + [dma((NP_, 4))] * 2 + [dma((3,))] * 2 + [dma((CH,))] * 2 + [dma((n - 1,))] * 2 + [dma((3,))] * 2 + [dma((NP_,))] * 2,
        compiler_params=pltpu.CompilerParams(collective_id=cid, has_side_effects=True, vmem_limit_bytes=VMEM_LIMIT),
    )(io, up, down, bias_rows, *xs_, *vec, code)


def body(n_dp, questions, passages, question_cotangent, passage_cotangent, positives, positive_counts,
         attention_in, attention_bias, attention_out, branch_biases, norm_gains, norm_shifts, up_weight, up_bias, down_weight):
    q4 = D // 4
    nq = questions.shape[0]
    sizes = (questions.shape[:2], passages.shape[:2])
    io = jnp.concatenate([attention_in.transpose(0, 1, 3, 2).reshape(2, 3 * q4, D), attention_out], axis=1)
    own_columns = jnp.arange(D, dtype=jnp.int32)[None, :] // q4 == lax.axis_index("tensor")
    att_rows = jnp.where(own_columns, jnp.tile(attention_bias.reshape(4, q4), (1, 4)), 0.0)
    bias_rows = jnp.concatenate([att_rows.astype(bf16), up_bias, jnp.zeros((10, D), bf16)])
    vec = (norm_gains, norm_shifts, branch_biases)
    slots = positives.shape[1]
    live = jnp.arange(slots, dtype=jnp.int32)[None, :] < positive_counts[:, None]
    named = jnp.where(live, positives, -16)
    code = jnp.concatenate([named // 16, named % 16], axis=1)
    code = jnp.pad(code, ((2 * (nq + passages.shape[0]), 16 - 3 * nq - 2 * passages.shape[0]), (0, HALF - 2 * slots))).astype(f32)
    xs_ = (questions.reshape(-1, D), passages.reshape(-1, D))
    weights, dc, losses, *made = forward(io, up_weight, down_weight, bias_rows, xs_, vec, code, sizes, n_dp)
    kept = []
    for e, cot in enumerate((question_cotangent, passage_cotangent)):
        kept.append(dict(zip(MADE, made[11 * e : 11 * e + 11]), cot=cot.reshape(-1, D), x=xs_[e]))
    down_g, up_g, io_g, own_rows, _, branch_g, gains_g, shifts_g, *dxs = backward(weights, dc, vec, kept, sizes, n_dp)
    own_small = own_rows[:16].astype(f32)
    att = lax.dynamic_slice_in_dim(own_small[0:4], lax.axis_index("tensor") * q4, q4, 1)
    return (
        kept[0]["y"].reshape(questions.shape), kept[1]["y"].reshape(passages.shape), losses[:nq, 0],
        dxs[0].reshape(questions.shape), dxs[1].reshape(passages.shape),
        io_g[:, : 3 * q4].reshape(2, 3, q4, D).transpose(0, 1, 3, 2).astype(f32), att.reshape(2, 2, q4),
        io_g[:, 3 * q4 :].astype(f32), branch_g, gains_g, shifts_g,
        up_g.astype(f32), own_small[4:6], down_g.astype(f32))


def solution(mesh):
    both = ("dp", "tensor")
    seq, rep = P(both, None, None), P()
    w4, w3, o3 = P(None, None, None, "tensor"), P(None, None, "tensor"), P(None, "tensor", None)
    in_specs = (seq, seq, seq, seq, P(both, None), P(both), w4, w3, o3, rep, rep, rep, w3, P(None, "tensor"), o3)
    out_specs = (seq, seq, P(both), seq, seq, w4, w3, o3, rep, rep, rep, w3, P(None, "tensor"), o3)
    return jax.shard_map(functools.partial(body, mesh.shape["dp"]), mesh=mesh, in_specs=in_specs, out_specs=out_specs, check_vma=False)
```

```python
import functools

import jax
import jax.numpy as jnp
from jax import lax
from jax.experimental import pallas as pl
from jax.experimental.pallas import tpu as pltpu
from jax.sharding import PartitionSpec as P

D = 768
MESH = pl.DeviceIdType.MESH
bf16, f32 = jnp.bfloat16, jnp.float32
VM = pl.BlockSpec(memory_space=pltpu.VMEM)
ANY = pl.BlockSpec(memory_space=pl.ANY)
SDS = jax.ShapeDtypeStruct


def place():
    dp, t = lax.axis_index("dp"), lax.axis_index("tensor")
    return dict(dp=dp, t=t, x=lax.div(t, 2), c=lax.rem(t, 2), y=lax.rem(dp, 2),
                z=lax.rem(lax.div(dp, 2), 4), o=lax.div(dp, 8))


def device(p, c=None, x=None, y=None, z=None, o=None):
    g = lambda v, k: p[k] if v is None else v
    return (g(o, "o") * 8 + g(z, "z") * 2 + g(y, "y"), g(x, "x") * 2 + g(c, "c"))


def greet(peers):
    bar = pltpu.get_barrier_semaphore()
    for q in peers:
        pl.semaphore_signal(bar, inc=1, device_id=q, device_id_type=MESH)
    pl.semaphore_wait(bar, len(peers))


def remote(src, dst, ssem, rsem, dev):
    return pltpu.make_async_remote_copy(src, dst, ssem, rsem, device_id=dev, device_id_type=MESH)


R = 64
MACRO = 256
HALF = D // 2
MACROS = 18
STEPS = MACROS * 4 + 1
VMEM_LIMIT = 64 * 2**20
LAG = dict(c=2, x=3, y=3, z=3, a=3)


KEPT = ("cot", "n2", "i2", "d", "g", "hb", "n1", "i1", "qkv", "o", "x", "p")


def cls_row(sizes, e):
    return sizes[0][0] if e else 0


def held_names(e):
    return tuple(k for k in KEPT[:11] if e == 0 or k not in ("o", "x"))


def back_kernel(outer, sizes, *refs):
    w_ref, dc_ref, *vec_ref = refs[:5]
    hbm = [dict(zip(KEPT, refs[5 + 12 * e : 17 + 12 * e])) for e in (0, 1)]
    refs = refs[29:]
    (down_out, up_out, in_out, wo_out, rows_ref, small_ref, *shared_ref), refs = refs[:9], refs[9:]
    dx_ref, refs = refs[:2], refs[2:]
    buf = []
    for e in (0, 1):
        names = held_names(e) + ("df", "da", "r", "dh", "do")
        buf.append(dict(zip(names, refs[: len(names)])))
        refs = refs[len(names) :]
    (p0_ref, win, wout, up, down, sums, load_sem, dx_sem, w_sem,
     made, crecv, xs, xrecv, ys, yrecv, zsum, zrecv, fin, osend, orecv,
     c_ss, c_rs, x_ss, x_rs, y_ss, y_rs, z_ss, z_rs, a_ss, a_rs, o_ss, o_rs, w_ss, w_rs, l_sem, t_ss, t_rs) = refs
    buf[1]["p"], buf[0]["p"] = buf[1]["g"], p0_ref
    buf[1]["o"], buf[1]["x"] = buf[1]["n2"], buf[1]["n1"]

    def load(e, name):
        return pltpu.make_async_copy(hbm[e][name], buf[e][name], load_sem.at[e, KEPT.index(name)])

    def weights(e, kind):
        return weight_copies(e, w_ref, (win, wout, up, down), w_sem, kind)

    def begin(*copies):
        for cp in copies:
            cp.start()

    def ready(*copies):
        for cp in copies:
            cp.wait()

    begin(*[load(1, k) for k in ("cot", "n2", "i2")])
    begin(*[load(1, "d")], *weights(1, 3), *[load(1, k) for k in ("g",)], *weights(1, 2))
    begin(*[load(0, k) for k in ("cot", "n2", "i2")], *[load(1, k) for k in ("n1", "i1")], *weights(1, 1))
    begin(*[load(0, k) for k in ("g", "d")], *[load(1, k) for k in ("hb", "qkv")])
    begin(*[load(0, k) for k in ("hb", "n1", "i1", "qkv", "o", "x", "p")], *weights(1, 0))

    vec = lambda e, i: vec_ref[i // 2][e].astype(f32)[i % 2 : i % 2 + 1]
    col = lambda a: jnp.sum(a, axis=0, keepdims=True)
    sums[...] = jnp.zeros_like(sums)

    def add(e, row, v):
        sums[e, row : row + 1, :] += v

    def tokens(e, b):
        n = spot(*sizes[e])[0]
        return pl.ds(b * n, n) if isinstance(b, int) else pl.ds(pl.multiple_of(b * n, n), n)

    def norm2(e, b):
        group, groups, per = spot(*sizes[e])
        w, tok = buf[e], tokens(e, b)
        dy = w["cot"][tok, :].astype(f32)
        pos = lax.broadcasted_iota(jnp.int32, (group, 1), 0)
        for k in range(per):
            dy = dy + jnp.where(pos == k * sizes[e][1], dc_ref[e, cls_row(sizes, e) + b * per + k : cls_row(sizes, e) + b * per + k + 1, :], 0.0)
        n = w["n2"][tok, :].astype(f32)
        add(e, 5, col(dy * n))
        add(e, 7, col(dy))
        r2 = norm_back(dy * vec(e, 1), n, w["i2"][tok, :])
        w["r"][tok, :] = r2
        df = r2.astype(bf16)
        w["df"][tok, :] = df
        add(e, 3, col(df.astype(f32)))

    def hidden(e, i, b):
        w, tok = buf[e], tokens(e, b)
        for k in range(3):
            c = slice(k * 256, (k + 1) * 256)
            du = (dot(w["df"][tok, :], down[i, c, :], 1, 1) * w["d"][i, tok, c].astype(f32)).astype(bf16)
            w["d"][i, tok, c] = du
            sums[e, pl.ds(8 + i, 1), c] += col(du.astype(f32))
        part = dot(w["d"][i, tok, :], up[i], 1, 1)
        w["dh"][tok, :] = jnp.where(i == 0, part, w["dh"][tok, :] + part)

    def norm1(e, b):
        w, tok = buf[e], tokens(e, b)
        dh = w["dh"][tok, :] + w["r"][tok, :]
        n = w["n1"][tok, :].astype(f32)
        add(e, 4, col(dh * n))
        add(e, 6, col(dh))
        r1 = norm_back(dh * vec(e, 0), n, w["i1"][tok, :])
        w["r"][tok, :] = r1
        da = r1.astype(bf16)
        w["da"][tok, :] = da
        add(e, 2, col(da.astype(f32)))
        w["do"][:, tok] = dot(wout[...], da, 1, 1).astype(bf16)

    def head(e, g, h):
        w, tok = buf[e], tokens(e, g)
        at = lambda base: pl.ds(pl.multiple_of(base + h * HD, HD), HD)
        q, kk, vv, do = w["qkv"][at(0), tok], w["qkv"][at(D), tok], w["qkv"][at(2 * D), tok], w["do"][at(0), tok]
        pb = w["p"][p_at(e, sizes[e], g, h)]
        p = pb.astype(f32)
        dp = dot(vv, do, 0, 0)
        ds = (p * (dp - jnp.sum(p * dp, axis=0, keepdims=True))).astype(bf16)
        w["qkv"][at(0), tok] = (dot(kk, ds, 1, 0) * 0.125).astype(bf16)
        w["qkv"][at(D), tok] = dot(q, ds, 1, 1).astype(bf16)
        w["qkv"][at(2 * D), tok] = dot(do, pb, 1, 1).astype(bf16)

    def input_back(e, b):
        w, tok = buf[e], tokens(e, b)
        w["cot"][tok, :] = (dot(w["qkv"][:, tok], win[...], 0, 0) + w["r"][tok, :]).astype(bf16)

    def dx_copy(e):
        return pltpu.make_async_copy(buf[e]["cot"], dx_ref[e], dx_sem.at[e])

    def bias_sums(e):
        w = buf[e]
        ones = jnp.ones((8, w["da"].shape[0]), bf16)
        add(e, 0, dot(ones, w["qkv"][0:D, :], 1, 1)[0:1])
        add(e, 1, dot(ones, w["qkv"][2 * D :, :], 1, 1)[0:1])

    def at_step(s, first, fn, count=1):
        @pl.when(jnp.logical_and(s >= first, s < first + count))
        def _():
            fn(s - first)

    def work(s):
        @pl.when(jnp.logical_and(s < 16, lax.rem(s, 4) > 0))
        def _():
            idx = lax.div(s, 4) * 3 + lax.rem(s, 4) - 1
            hidden(1, lax.div(idx, 3), lax.rem(idx, 3))

        def s4(_):
            ready(*[load(0, k) for k in ("cot", "n2", "i2")])
            norm2(0, 0)

        def s9(_):
            begin(load(1, "p"))

        def s16(_):
            begin(*weights(0, 3), *weights(0, 2))
            ready(*[load(1, k) for k in ("n1", "i1")], *weights(1, 1))

        def s20(_):
            begin(load(1, "x"), *weights(0, 1))
            ready(*weights(0, 3), *weights(0, 2), load(0, "d"))

        def s25(_):
            ready(load(0, "n1"), load(0, "i1"), *weights(0, 1))
            norm1(0, 0)

        def s26(_):
            ready(load(1, "qkv"), load(1, "p"))

        def att1(a):
            for k in range(2):
                head(1, lax.div(a, 6), lax.rem(a, 6) * 2 + k)

        def s45(_):
            bias_sums(1)
            ready(*weights(1, 0))

        def s49(_):
            begin(dx_copy(1))
            begin(*weights(0, 0))
            ready(load(0, "qkv"), load(0, "p"))

        def att0(a):
            for k in range(2):
                head(0, 0, a * 2 + k)

        def s57(_):
            bias_sums(0)
            ready(*weights(0, 0))
            input_back(0, 0)
            begin(dx_copy(0))

        at_step(s, 4, s4)
        at_step(s, 9, s9)
        at_step(s, 16, s16)
        at_step(s, 17, lambda b: norm1(1, b), 3)
        at_step(s, 20, s20)
        at_step(s, 21, lambda i: hidden(0, i, 0), 4)
        at_step(s, 25, s25)
        at_step(s, 26, s26)
        at_step(s, 27, att1, 18)
        at_step(s, 45, s45)
        at_step(s, 46, lambda b: input_back(1, b), 3)
        at_step(s, 49, s49)
        at_step(s, 51, att0, 6)
        at_step(s, 57, s57)

    ready(*[load(1, k) for k in ("cot", "n2", "i2")])
    for b in range(3):
        norm2(1, b)
    begin(load(1, "o"))
    ready(load(1, "d"), load(1, "g"), *weights(1, 3), *weights(1, 2))

    p = place()
    sib, xp, yp = device(p, c=1 - p["c"]), device(p, x=1 - p["x"]), device(p, y=1 - p["y"])
    zs = [lax.rem(p["z"] + j, 4) for j in (1, 2, 3)]
    zp = [device(p, z=v) for v in zs]
    op = [device(p, o=lax.rem(p["o"] + j, outer)) for j in range(1, outer)]
    diag = device(p, x=1 - p["x"], c=1 - p["c"])
    greet([sib, xp, yp, diag] + zp + op)
    dc, dx, dy, dz, da = (LAG[k] for k in "cxyza")
    lx = dc
    ly = lx + dx
    lz = ly + dy
    la = lz + dz
    lf = la + da
    m16 = lambda v, n: pl.ds(pl.multiple_of(v, 16), n)
    mine16 = m16(p["z"] * 16, 16)
    half = lambda y: pl.ds(pl.multiple_of(y * HALF, 128), HALF)

    def made_at(u, c):
        return made.at[lax.rem(lax.div(u, 4), 2), :, c, m16(lax.rem(u, 4) * R, R)]

    def c_copy(u):
        k = lax.rem(u, 2 * dc)
        return remote(made_at(u, 1 - p["c"]), crecv.at[k], c_ss.at[k], c_rs.at[k], sib)

    def x_copy(u):
        k = lax.rem(u, 2 * dx)
        return remote(xs.at[k, 1 - p["x"]], xrecv.at[k], x_ss.at[k], x_rs.at[k], xp)

    def y_copy(u):
        k = lax.rem(u, 2 * dy)
        return remote(ys.at[k, :, half(1 - p["y"])], yrecv.at[k], y_ss.at[k], y_rs.at[k], yp)

    def z_copy(u, j):
        k = lax.rem(u, 2 * dz)
        return remote(zsum.at[k, m16(zs[j] * 16, 16)], zrecv.at[k, m16(32 - 16 * j, 16)], z_ss.at[k], z_rs.at[k], zp[j])

    def z_all(u):
        k = lax.rem(u, 2 * dz)
        return remote(zsum.at[k, m16(0, 48)], zrecv.at[k], z_ss.at[k], z_rs.at[k], zp[0])

    def a_copy(u, j):
        k = lax.rem(u, 3 * da)
        a = fin.at[k, mine16]
        return remote(a, a, a_ss.at[k], a_rs.at[k], zp[j])

    def a_all(u):
        k = lax.rem(u, 3 * da)
        a = fin.at[k, m16(0, 48)]
        return remote(a, a, a_ss.at[k], a_rs.at[k], zp[0])

    def both(c):
        c.wait_send()
        c.wait_recv()

    def targets(u):
        m, g = lax.div(u, 4), lax.div(u, 12)
        r, e, kind = lax.rem(m, 3) * MACRO + lax.rem(u, 4) * R, 1 - lax.rem(g, 2), lax.div(g, 2)
        whole = [(kind == k, ref.at[e, m16(r, R), half(p["y"])]) for k, ref in enumerate((down_out, up_out))]
        split = 3 * D // 4
        parts = [(jnp.logical_and(kind == 2, r < split), in_out.at[e, m16(r, R), half(p["y"])]),
                 (jnp.logical_and(kind == 2, r >= split), wo_out.at[e, m16(r - split, R), half(p["y"])])]
        return whole + parts + [(u == STEPS - 1, rows_ref.at[:, half(p["y"])])]

    def w_remote(u, dst):
        k = lax.rem(u, 3 * da)
        return remote(fin.at[k], dst, w_ss.at[k], w_rs.at[k], yp)

    def w_local(u, dst):
        k = lax.rem(u, 3 * da)
        return pltpu.make_async_copy(fin.at[k], dst, l_sem.at[k])

    def when(u, fn, n=STEPS):
        @pl.when(jnp.logical_and(u >= 0, u < n))
        def _():
            fn(u)

    def finish(u):
        both(a_all(u))
        for here, dst in targets(u):
            @pl.when(here)
            def _():
                w_remote(u, dst).start()
                w_local(u, dst).start()

    def finished(u):
        for here, dst in targets(u):
            @pl.when(here)
            def _():
                both(w_remote(u, dst))
                w_local(u, dst).wait()

    def take_z(u):
        both(z_all(u))
        k = lax.rem(u, 2 * dz)
        v = zsum[k, mine16].astype(f32)
        for j in range(3):
            v = v + zrecv[k, 16 * j : 16 * j + 16].astype(f32)
        if outer > 1:
            osend[...] = v.astype(bf16)
            for j in range(outer - 1):
                remote(osend, orecv.at[outer - 2 - j], o_ss.at[j], o_rs.at[outer - 2 - j], op[j]).start()
            for j in range(outer - 1):
                both(remote(osend, orecv.at[j], o_ss.at[j], o_rs.at[j], op[j]))
            v = osend[...].astype(f32)
            for j in range(outer - 1):
                v = v + orecv[j].astype(f32)
        fin[lax.rem(u, 3 * da), mine16] = v.astype(bf16)
        for j in range(3):
            a_copy(u, j).start()

    def take_y(u):
        both(y_copy(u))
        k = lax.rem(u, 2 * dy)
        zsum[lax.rem(u, 2 * dz)] = ys[k, :, half(p["y"])] + yrecv[k]
        for j in range(3):
            z_copy(u, j).start()

    def take_x(u):
        both(x_copy(u))
        k = lax.rem(u, 2 * dx)
        ys[lax.rem(u, 2 * dy)] = xs[k, p["x"]] + xrecv[k]
        y_copy(u).start()

    def take_c(u):
        both(c_copy(u))
        k = lax.rem(u, 2 * dc)
        kx = lax.rem(u, 2 * dx)
        own = lambda x: made[lax.rem(lax.div(u, 4), 2), x, p["c"], m16(lax.rem(u, 4) * R, R)]
        o = 1 - p["x"]
        xs[kx, o] = own(o) + crecv[k, o]
        x_copy(u).start()
        xs[kx, p["x"]] = own(p["x"]) + crecv[k, p["x"]]

    def make(m):
        slot = lax.rem(m, 2)
        g = lax.div(m, 3)
        r = lax.rem(m, 3)
        cols = pl.ds(pl.multiple_of(r * MACRO, 128), MACRO)
        for e in (0, 1):
            w = buf[e]

            @pl.when(g == 1 - e)
            def _():
                if e == 0:
                    @pl.when(r == 0)
                    def _():
                        ready(load(0, "g"))
                for t in range(4):
                    made[slot, t // 2, t % 2] = dot(w["g"][t, :, cols], w["df"][...], 0, 0).astype(bf16)

            @pl.when(g == 3 - e)
            def _():
                @pl.when(r == 0)
                def _():
                    ready(load(e, "hb"))
                for t in range(4):
                    made[slot, t // 2, t % 2] = dot(w["hb"][:, cols], w["d"][t], 0, 0).astype(bf16)

            for rr in range(3):
                @pl.when(m == (5 - e) * 3 + rr)
                def _():
                    if rr == 0:
                        ready(load(e, "o"), load(e, "x"))
                    for t in range(4):
                        at = rr * MACRO
                        while at < (rr + 1) * MACRO:
                            j, off = at // 192, at % 192
                            n = min(192 - off, (rr + 1) * MACRO - at)
                            src = w["qkv"][j * D + t * 192 + off : j * D + t * 192 + off + n, :] if j < 3 else w["o"][t * 192 + off : t * 192 + off + n, :]
                            made[slot, t // 2, t % 2, at - rr * MACRO : at - rr * MACRO + n] = dot(
                                src, w["x"][...] if j < 3 else w["da"][...], 1, 0).astype(bf16)
                            at += n

        @pl.when(m == MACROS)
        def _():
            row = lambda e, i: sums[e, i : i + 1, :]
            shared = [row(e, i + k) for i in (2, 4, 6) for e in (0, 1) for k in (0, 1)]
            for t in range(4):
                v = [row(0, 0), row(0, 1), row(1, 0), row(1, 1), row(0, 8 + t), row(1, 8 + t)] + shared[3 * t : 3 * t + 3]
                v = jnp.concatenate(v + [jnp.zeros((7, D), f32)], axis=0)
                made[slot, t // 2, t % 2, 0:16] = v.astype(bf16)
                made[slot, t // 2, t % 2, 16:R] = jnp.zeros((R - 16, D), bf16)

    def fetch(u):
        @pl.when(lax.rem(u, 4) == 0)
        def _():
            make(lax.div(u, 4))

        c_copy(u).start()

    def step(s, _):
        when(s - lf - da, finished)
        when(s - lf, finish)
        when(s - la, take_z)
        when(s - lz, take_y)
        when(s - ly, take_x)
        when(s - lx, take_c)
        when(s, fetch)
        work(s)
        return _

    lax.fori_loop(0, STEPS + lf + da, step, 0)
    ready(dx_copy(0), dx_copy(1))
    x, c = p["x"], p["c"]
    own = rows_ref.at[pl.ds(0, 16)]
    sends = [remote(own, small_ref.at[x, c], t_ss.at[i], t_rs.at[i], dev) for i, dev in enumerate((sib, xp, diag))]
    for cp in sends:
        cp.start()
    small_ref[x, c] = rows_ref[0:16]
    for i, (a, b) in enumerate(((x, 1 - c), (1 - x, c), (1 - x, 1 - c))):
        sends[i].wait_send()
        remote(own, small_ref.at[a, b], t_ss.at[i], t_rs.at[i], sib).wait_recv()
    got = [small_ref[t // 2, t % 2].astype(f32) for t in range(4)]
    for r in range(12):
        shared_ref[r // 4][(r // 2) % 2, r % 2 : r % 2 + 1] = got[r // 3][6 + r % 3 : 7 + r % 3]


def backward(w_all, dc, vec, kept, sizes, dp, cid=3):
    outer = dp // 8
    dma = pltpu.SemaphoreType.DMA
    lc, lx, ly, lz, la = (LAG[k] for k in "cxyza")
    no = max(outer - 1, 1)
    vm = lambda s, t=bf16: pltpu.VMEM(s, t)
    scratch = []
    for e in (0, 1):
        n = sizes[e][0] * sizes[e][1]
        scratch += [vm(kept[e][k].shape, kept[e][k].dtype) for k in held_names(e)]
        scratch += [vm((n, D)), vm((n, D)), vm((n, D), f32), vm((n, D), f32), vm((D, n))]
    args = [w_all, dc, *vec] + [kept[e][k] for e in (0, 1) for k in KEPT]
    return pl.pallas_call(
        functools.partial(back_kernel, outer, sizes),
        out_shape=(*[SDS((2, D, D), bf16)] * 2, SDS((2, 3 * D // 4, D), bf16), SDS((2, D // 4, D), bf16), SDS((R, D), bf16), SDS((2, 2, 16, D), bf16), *[SDS((2, 2, D), f32)] * 3,
                   SDS(kept[0]["x"].shape, bf16), SDS(kept[1]["x"].shape, bf16)),
        in_specs=[ANY] + [VM] * 4 + [ANY] * 24,
        out_specs=(ANY, ANY, ANY, ANY, VM, VM, VM, VM, VM, ANY, ANY),
        scratch_shapes=scratch + [
            vm(kept[0]["p"].shape), *[vm(s) for s in W_SHAPES], vm((2, 16, D), f32), dma((2, 12)), dma((2,)), dma((24,)),
            vm((2, 2, 2, MACRO, D)), vm((2 * lc, 2, R, D)), vm((2 * lx, 2, R, D)), vm((2 * lx, R, D)),
            vm((2 * ly, R, D)), vm((2 * ly, R, HALF)), vm((2 * lz, R, HALF)), vm((2 * lz, 48, HALF)), vm((3 * la, R, HALF)),
            vm((16, HALF)), vm((no, 16, HALF)),
            dma((2 * lc,)), dma((2 * lc,)), dma((2 * lx,)), dma((2 * lx,)), dma((2 * ly,)), dma((2 * ly,)),
            dma((2 * lz,)), dma((2 * lz,)), dma((3 * la,)), dma((3 * la,)), dma((no,)), dma((no,)),
            dma((3 * la,)), dma((3 * la,)), dma((3 * la,)), dma((3,)), dma((3,)),
        ],
        compiler_params=pltpu.CompilerParams(collective_id=cid, has_side_effects=True, vmem_limit_bytes=VMEM_LIMIT),
    )(*args)


HD = 64
EPS = 1e-12


def dot(a, b, ca, cb):
    return lax.dot_general(a, b, (((ca,), (cb,)), ((), ())), preferred_element_type=f32)


def gelu_pair(u):
    a = jnp.abs(u) * 0.7071067811865476
    t = 1.0 / (1.0 + 0.3275911 * a)
    e = jnp.exp(-(a * a))
    poly = t * (0.254829592 + t * (-0.284496736 + t * (1.421413741 + t * (-1.453152027 + t * 1.061405429))))
    tail = 0.5 * poly * e
    cdf = jnp.where(u >= 0, 1.0 - tail, tail)
    return u * cdf, cdf + u * (e * 0.3989422804014327)


def loop(n, fn):
    def run(i, c):
        fn(i)
        return c

    lax.fori_loop(0, n, run, 0)


def norm(r, gain, shift):
    c = r - jnp.mean(r, axis=-1, keepdims=True)
    inv = lax.rsqrt(jnp.mean(c * c, axis=-1, keepdims=True) + EPS)
    n = c * inv
    return n * gain + shift, n, inv


def spot(seqs, length):
    tokens = seqs * length
    if length % 128 == 0:
        return length, seqs, 1
    return tokens, 1, seqs


W_SHAPES = ((3 * D, D), (D, D), (4, D, D), (4, D, D))


def weight_copies(e, w_ref, refs, sem, kind):
    base, q = 3 * (1 - e), D // 4
    dst = refs[kind]
    pairs = []
    for t in range(4):
        src = w_ref.at[t // 2, t % 2]
        if kind == 0:
            pairs += [(src.at[base, pl.ds(j * q, q)], dst.at[pl.ds(j * D + t * q, q)]) for j in range(3)]
        elif kind == 1:
            pairs.append((src.at[base, pl.ds(3 * q, q)], dst.at[pl.ds(t * q, q)]))
        else:
            pairs.append((src.at[base + kind - 1], dst.at[t]))
    first = (0, 12, 16, 20)[kind]
    return [pltpu.make_async_copy(a, b, sem.at[first + i]) for i, (a, b) in enumerate(pairs)]


def p_at(e, size, g, h):
    group, groups, _ = spot(*size)
    if groups == 1:
        return (h,)
    return (h // 3 if isinstance(h, int) else lax.div(h, 3),
            pl.ds(g * group if isinstance(g, int) else pl.multiple_of(g * group, group), group),
            pl.ds(pl.multiple_of((h % 3 if isinstance(h, int) else lax.rem(h, 3)) * group, 128), group))


def norm_back(dz, n, inv):
    return inv * (dz - jnp.mean(dz, axis=-1, keepdims=True) - n * jnp.mean(dz * n, axis=-1, keepdims=True))


CH = 6
PLAN = ((0, 1), (1, 1), (2, 1), (0, 0), (1, 0), (2, 0))
PIECES = [(h, 0, D) for h in range(CH)]
NP_ = len(PIECES)
MADE = ("y", "qkv", "p", "o", "n1", "i1", "hb", "g", "d", "n2", "i2")


def made_shapes(size):
    t = size[0] * size[1]
    group, groups, _ = spot(*size)
    return dict(y=(t, D), qkv=(3 * D, t), p=(4, t, D) if groups > 1 else (12, group, group), o=(D, t), n1=(t, D), i1=(t, 1),
                hb=(t, D), g=(4, t, D), d=(4, t, D), n2=(t, D), i2=(t, 1))


def front_kernel(n, sizes, io_ref, up_ref, down_ref, b_ref, x0_ref, x1_ref, *refs):
    (*vec_ref, code_ref), refs = refs[:4], refs[4:]
    (out_ref, dc_ref, loss_ref), refs = refs[:3], refs[3:]
    hbm = [dict(zip(MADE, refs[11 * e : 11 * e + 11])) for e in (0, 1)]
    refs = refs[22:]
    buf = [dict(zip(MADE, refs[11 * e : 11 * e + 11])) for e in (0, 1)]
    refs = refs[22:]
    (h0, f0, h1, f1, win, wout, up, down, bias_ref, bias_in, held, cls, full, codes, pay, w_sem, made_sem,
     x_ss, x_rs, y_ss, y_rs, z_ss, z_rs, y2_ss, y2_rs, z2_ss, z2_rs, sib_ss, sib_rs, f_ss, f_rs, b_ss, b_rs, in_sem, back_sem,
     r_ss, r_rs, g_ss, g_rs, x2_ss, x2_rs) = refs
    xin, hs, fs = (x0_ref, x1_ref), (h0, h1), (f0, f1)
    p = place()
    zb = lax.rem(p["z"], 2)
    sib, xp, yp = device(p, c=1 - p["c"]), device(p, x=1 - p["x"]), device(p, y=1 - p["y"])
    zp = device(p, z=p["z"] + 1 - 2 * zb)
    diag = device(p, x=1 - p["x"], c=1 - p["c"])
    ring = [lax.rem(p["dp"] + j, n) for j in range(1, n)]
    group4 = [lax.rem(p["t"] + j, 4) for j in range(1, 4)]
    greet([(q, p["t"]) for q in ring] + [(p["dp"], q) for q in group4])
    x, c, y = p["x"], p["c"], p["y"]
    def rows(i, q):
        _, r, k = PIECES[i]
        return pl.ds(pl.multiple_of(r + q * (k // 4), 16), k // 4)

    def hrows(i, q, j):
        _, r, k = PIECES[i]
        return pl.ds(pl.multiple_of(r + q * (k // 4) + j * (k // 12), 16), k // 12)

    mine, qy, qz, dg = y * 2 + zb, (1 - y) * 2 + zb, y * 2 + 1 - zb, (1 - y) * 2 + 1 - zb
    source = lambda h: (io_ref, up_ref, down_ref)[PLAN[h][0]].at[PLAN[h][1]]
    started = []

    def go(cp):
        cp.start()
        started.append(cp)

    for i, dev in enumerate((sib, xp, diag)):
        go(remote(b_ref, bias_ref.at[x, c], b_ss.at[i], b_rs.at[i], dev))
    for i in range(NP_ + 1):
        if i < NP_:
            h = PIECES[i][0]
            go(remote(source(h).at[rows(i, mine)], out_ref.at[x, c, h, rows(i, mine)], x_ss.at[i], x_rs.at[i], xp))
            if PIECES[i][1] == 0:
                go(remote(source(h), out_ref.at[x, c, h], sib_ss.at[h], sib_rs.at[h], sib))
        if i > 0:
            h, r = PIECES[i - 1][0], hrows(i - 1, dg, 2)
            go(remote(source(h).at[r], out_ref.at[x, c, h, r], x2_ss.at[i - 1], x2_rs.at[i - 1], xp))
    ins = [pltpu.make_async_copy(source(h), held.at[h % 2], in_sem.at[h]) for h in range(CH)]
    backs = [pltpu.make_async_copy(held.at[h % 2], out_ref.at[x, c, h], back_sem.at[h]) for h in range(CH)]
    ins[0].start()
    ins[1].start()
    bias_ref[x, c] = b_ref[...]
    def bounce(h):
        ins[h].wait()
        backs[h].start()
        if h + 2 < CH:
            backs[h].wait()
            ins[h + 2].start()

    def whole(i, q, ss, rs, dev):
        a = out_ref.at[1 - x, c, PIECES[i][0], rows(i, q)]
        return remote(a, a, ss, rs, dev)

    def part(i, q, k, ss, rs, dev):
        a = out_ref.at[1 - x, c, PIECES[i][0], hrows(i, q, k)]
        return remote(a, a, ss.at[i], rs.at[i], dev)

    def first(i):
        whole(i, mine, x_ss.at[i], x_rs.at[i], xp).wait_recv()
        go(whole(i, mine, y_ss.at[i], y_rs.at[i], yp))
        go(whole(i, mine, z_ss.at[i], z_rs.at[i], zp))
        go(whole(i, mine, f_ss.at[i, 0], f_rs.at[i, 0], sib))

    def second(i):
        whole(i, qy, y_ss.at[i], y_rs.at[i], yp).wait_recv()
        go(part(i, qy, 1, z2_ss, z2_rs, zp))
        whole(i, qz, z_ss.at[i], z_rs.at[i], zp).wait_recv()
        go(part(i, qz, 0, y2_ss, y2_rs, yp))
        go(whole(i, qy, f_ss.at[i, 1], f_rs.at[i, 1], sib))
        go(whole(i, qz, f_ss.at[i, 2], f_rs.at[i, 2], sib))

    def third(i):
        part(i, dg, 0, y2_ss, y2_rs, yp).wait_recv()
        part(i, dg, 1, z2_ss, z2_rs, zp).wait_recv()
        part(i, dg, 2, x2_ss, x2_rs, xp).wait_recv()
        go(whole(i, dg, f_ss.at[i, 3], f_rs.at[i, 3], sib))

    def arrived(h):
        a = out_ref.at[x, 1 - c, h]
        remote(a, a, sib_ss.at[h], sib_rs.at[h], sib).wait_recv()
        for i in range(NP_):
            if PIECES[i][0] == h:
                for j, q in enumerate((mine, qy, qz, dg)):
                    a = out_ref.at[1 - x, 1 - c, h, rows(i, q)]
                    remote(a, a, f_ss.at[i, j], f_rs.at[i, j], sib).wait_recv()
        if h >= CH - 2:
            backs[h].wait()

    def weights(e, kind):
        return weight_copies(e, out_ref, (win, wout, up, down), w_sem, kind)

    def begin(*copies):
        for cp in copies:
            cp.start()

    def ready(*copies):
        for cp in copies:
            cp.wait()

    def keep(e, *names):
        for k in names:
            cp = pltpu.make_async_copy(buf[e][k], hbm[e][k], made_sem.at[e, MADE.index(k)])
            cp.start()
            keeps.append(cp)

    keeps = []
    vec = lambda e, i: vec_ref[i // 2][e].astype(f32)[i % 2 : i % 2 + 1]

    def tokens(e, b):
        m = spot(*sizes[e])[0]
        return pl.ds(b * m, m)

    def project(e, i):
        r = pl.ds(pl.multiple_of(i * 256, 256), 256)
        ones = jnp.ones((16, xin[e].shape[0]), bf16)
        bias = bias_in[e, lax.div(i, 3), :, pl.ds(pl.multiple_of(lax.rem(i, 3) * 256, 128), 256)]
        v = (dot(win[r, :], xin[e][...], 1, 1) + dot(bias, ones, 0, 0)).astype(bf16)
        buf[e]["qkv"][r, :] = v * jnp.where(i < 3, 0.125, 1.0).astype(bf16)

    def heads(e, g, i):
        group, groups, per = spot(*sizes[e])
        tok, w = tokens(e, g), buf[e]
        for k in range(2):
            h = i * 2 + k
            at = lambda base: pl.ds(pl.multiple_of(base + h * HD, HD), HD)
            s = dot(w["qkv"][at(D), tok], w["qkv"][at(0), tok], 0, 0)
            if per > 1:
                a = lax.broadcasted_iota(jnp.int32, s.shape, 0) // sizes[e][1]
                b = lax.broadcasted_iota(jnp.int32, s.shape, 1) // sizes[e][1]
                s = jnp.where(a == b, s, -1e30)
            ex = jnp.exp(s - jnp.max(s, axis=0, keepdims=True))
            pr = (ex * (1.0 / jnp.sum(ex, axis=0, keepdims=True))).astype(bf16)
            w["p"][p_at(e, sizes[e], g, h)] = pr
            w["o"][at(0), tok] = dot(w["qkv"][at(2 * D), tok], pr, 1, 0).astype(bf16)

    def out_norm(e, b):
        tok, w = tokens(e, b), buf[e]
        r = dot(w["o"][:, tok], wout[...], 0, 0) + xin[e][tok, :].astype(f32) + vec(e, 4)
        h, m, inv = norm(r, vec(e, 0), vec(e, 2))
        hs[e][tok, :] = h
        w["hb"][tok, :] = h.astype(bf16)
        w["n1"][tok, :] = m.astype(bf16)
        w["i1"][tok, :] = inv

    def hidden(e, i, b):
        tok, w = tokens(e, b), buf[e]
        ub = bias_ref[i // 2, i % 2, 0:16, :].astype(f32)[4 + e : 5 + e]
        for k in range(3):
            cc = slice(k * 256, (k + 1) * 256)
            u = dot(w["hb"][tok, :], up[i, :, cc], 1, 0) + ub[:, cc]
            g, d = gelu_pair(u)
            w["g"][i, tok, cc] = g.astype(bf16)
            w["d"][i, tok, cc] = d.astype(bf16)

    def shrink(e, i, b):
        tok, w = tokens(e, b), buf[e]
        part_ = dot(w["g"][i, tok, :], down[i], 1, 0)
        fs[e][tok, :] = part_ if i == 0 else fs[e][tok, :] + part_

    def norm2(e, b):
        tok, w = tokens(e, b), buf[e]
        v, m, inv = norm(hs[e][tok, :] + (fs[e][tok, :] + vec(e, 5)), vec(e, 1), vec(e, 3))
        w["y"][tok, :] = v.astype(bf16)
        w["n2"][tok, :] = m.astype(bf16)
        w["i2"][tok, :] = inv

    def projects(e, a, b):
        lax.fori_loop(a, b, lambda i, cc: (project(e, i), cc)[1], 0)

    def biases():
        for i, (a, b) in enumerate(((x, 1 - c), (1 - x, c), (1 - x, 1 - c))):
            remote(b_ref, bias_ref.at[a, b], b_ss.at[i], b_rs.at[i], sib).wait_recv()
        for e in (0, 1):
            for j in range(3):
                if j == 1:
                    bias_in[e, j] = jnp.zeros((16, D), bf16)
                else:
                    r = 2 * e + j // 2
                    got = [bias_ref[t // 2, t % 2].astype(f32)[r : r + 1] for t in range(4)]
                    bias_in[e, j] = jnp.concatenate(got + [jnp.zeros((12, D), f32)], axis=0).astype(bf16)

    def attend(e, g, lo, hi):
        lax.fori_loop(lo, hi, lambda i, cc: (heads(e, g, i), cc)[1], 0)

    tasks = []

    def task(name, us, needs, fn):
        tasks.append((name, us, tuple(needs), fn))

    for h in range(2):
        task(f"bounce{h}", 1.0, (), functools.partial(bounce, h))
    task("biases", 0.3, (), biases)
    for h in range(2, CH):
        task(f"bounce{h}", 1.0, (f"bounce{h - 2}",), functools.partial(bounce, h))
    for e in (1, 0):
        base = 0 if e else 3
        k, blocks, groups = (1.0, 3, 3) if e else (0.45, 1, 1)
        free = lambda *names: () if e else names
        task(f"w0{e}", 0.3, (f"arrived{base}", *free("project1")), lambda e=e: begin(*weights(e, 0)))
        task(f"w1{e}", 0.1, (f"arrived{base}", *free("out1")), lambda e=e: begin(*weights(e, 1)))
        task(f"w2{e}", 0.1, (f"arrived{base + 1}", *free("hidden1")), lambda e=e: begin(*weights(e, 2)))
        task(f"w3{e}", 0.1, (f"arrived{base + 2}", *free("shrink1")), lambda e=e: begin(*weights(e, 3)))
        task(f"r0{e}", 0.8, (f"w0{e}", "biases"), lambda e=e: ready(*weights(e, 0)))
        for i in range(3):
            last = "project%d" % e if i == 2 else "project%d_%d" % (e, i)
            task(last, 2.2 * k, (f"r0{e}",), lambda e=e, i=i: projects(e, 3 * i, 3 * i + 3))
        for g in range(groups):
            for half_ in (0, 1):
                task(f"att{e}_{g}_{half_}", 2.6, (f"project{e}",), lambda e=e, g=g, q=half_: attend(e, g, 3 * q, 3 * q + 3))
        every = [f"att{e}_{g}_{q}" for g in range(groups) for q in (0, 1)]
        task(f"keepa{e}", 0.1, every, lambda e=e: keep(e, "qkv", "p", "o"))
        task(f"r1{e}", 0.3, (f"w1{e}", *every), lambda e=e: ready(*weights(e, 1)))
        for b in range(blocks):
            task(f"out{e}" if b == blocks - 1 else f"out{e}_{b}", 1.4, (f"r1{e}",), lambda e=e, b=b: out_norm(e, b))
        task(f"keepb{e}", 0.1, (f"out{e}",), lambda e=e: keep(e, "n1", "i1", "hb"))
        task(f"r2{e}", 0.6, (f"w2{e}", f"out{e}"), lambda e=e: ready(*weights(e, 2)))
        task(f"r3{e}", 0.6, (f"w3{e}", f"out{e}"), lambda e=e: ready(*weights(e, 3)))
        for i in range(4):
            for b in range(blocks):
                end = i == 3 and b == blocks - 1
                task(f"hidden{e}" if end else f"hidden{e}_{i}_{b}", 1.2, (f"r2{e}",), lambda e=e, i=i, b=b: hidden(e, i, b))
        for i in range(4):
            for b in range(blocks):
                end = i == 3 and b == blocks - 1
                task(f"shrink{e}" if end else f"shrink{e}_{i}_{b}", 0.6,
                     (f"r3{e}", "hidden%d" % e if i == 3 and b == blocks - 1 else f"hidden{e}_{i}_{b}"),
                     lambda e=e, i=i, b=b: shrink(e, i, b))
        task(f"keepc{e}", 0.1, (f"hidden{e}",), lambda e=e: keep(e, "g", "d"))
        for b in range(blocks):
            task(f"norm{e}" if b == blocks - 1 else f"norm{e}_{b}", 0.8, (f"shrink{e}",), lambda e=e, b=b: norm2(e, b))
        task(f"keepd{e}", 0.1, (f"norm{e}",), lambda e=e: keep(e, "y", "n2", "i2"))

    span_ = [k * 2 * D * 2 / 4 / 75e3 for _, _, k in PIECES]
    at_x, at_x2, t_ = {}, {}, 3.0
    for i in range(NP_ + 1):
        if i < NP_:
            t_ += span_[i]
            at_x[i] = t_ + 1.5
        if i > 0:
            t_ += span_[i - 1] / 3
            at_x2[i - 1] = t_ + 1.5
    order = [("f", 0)]
    for i in range(NP_ + 2):
        order += [("f", i + 1)] if i + 1 < NP_ else []
        order += [("s", i)] if i < NP_ else []
        order += [("t", i - 1)] if 0 <= i - 1 < NP_ else []
    line, landed, done, now = 3.0, {}, set(), 3.0
    comm = {"f": first, "s": second, "t": third}
    while order or tasks:
        kind, i = order[0] if order else (None, None)
        due = {"f": lambda: at_x[i], "s": lambda: landed["f", i], "t": lambda: max(landed["s", i], at_x2[i])}[kind]() if kind else 1e9
        pick = next((k for k in tasks if all(d in done for d in k[2])), None)
        if due <= now or pick is None:
            now = max(now, due) + 0.25
            comm[kind](i)
            order.pop(0)
            if kind in "fs":
                line = max(line, now) + span_[i] / (1 if kind == "f" else 3)
                landed[kind, i] = line + 1.5
            elif i + 1 == NP_ or PIECES[i + 1][0] != PIECES[i][0]:
                arrived(PIECES[i][0])
                now += 0.8
                done.add(f"arrived{PIECES[i][0]}")
        else:
            pick[3]()
            now += pick[1]
            done.add(pick[0])
            tasks.remove(pick)
    nq, np_ = sizes[0][0], sizes[1][0]
    got = [buf[e]["y"][i * sizes[e][1] : i * sizes[e][1] + 16, :].astype(f32)[0:1] for e in (0, 1) for i in range(sizes[e][0])]
    blank = jnp.zeros((16 - 2 * (nq + np_), HALF), f32)
    pay[...] = (jnp.concatenate([v[:, :HALF] for v in got] + [v[:, HALF:] for v in got] + [blank], axis=0) + code_ref[...]).astype(bf16)
    place_of = lambda t, d: pl.ds(pl.multiple_of((t * n + d) * 16, 16), 16)
    here = cls.at[place_of(p["t"], p["dp"])]
    cls[place_of(p["t"], p["dp"]), :] = pay[...]
    for j, q in enumerate(ring):
        go(remote(pay, here, r_ss.at[j], r_rs.at[n - 2 - j], (q, p["t"])))
    for j, q in enumerate(ring):
        remote(pay, cls.at[place_of(p["t"], q)], r_ss.at[j], r_rs.at[j], (q, p["t"])).wait_recv()
    band = lambda x_, c_: cls.at[pl.ds(pl.multiple_of((x_ * 2 + c_) * n * 16, 16), n * 16)]
    go(remote(band(x, c), band(x, c), g_ss.at[0], g_rs.at[0], xp))
    go(remote(band(x, c), band(x, c), g_ss.at[1], g_rs.at[1], sib))
    remote(band(1 - x, c), band(1 - x, c), g_ss.at[0], g_rs.at[0], xp).wait_recv()
    go(remote(band(1 - x, c), band(1 - x, c), g_ss.at[2], g_rs.at[2], sib))
    remote(band(x, 1 - c), band(x, 1 - c), g_ss.at[1], g_rs.at[1], sib).wait_recv()
    remote(band(1 - x, 1 - c), band(1 - x, 1 - c), g_ss.at[2], g_rs.at[2], sib).wait_recv()

    total = 4 * n * 16
    scale = 2.7 * D**-0.5
    count = nq + np_

    def unfold(v):
        v = v.astype(f32)
        k = v.shape[0]
        return jnp.concatenate([v, pltpu.roll(v, k - count, 0), pltpu.roll(v[:, 0:128], k - 2 * count, 0)], axis=1)

    own = unfold(pay[...])
    own_code, own = own[:, D:], own[:, :D].astype(bf16)
    wide = unfold(cls[...])
    full[...] = wide[:, :D].astype(bf16)
    codes[...] = wide[:, D:]
    at = lax.broadcasted_iota(jnp.int32, (1, total), 1)
    block, pos = at // 16, at % 16
    name = (((block % n) * 4 + block // n) * np_ + (pos - nq)).astype(f32)
    live = jnp.logical_and(pos >= nq, pos < nq + np_)

    def marks(code, names):
        m = jnp.zeros((code.shape[0], names.shape[1]), f32)
        for k in range(4):
            m = m + (code[:, k : k + 1] * 16.0 + code[:, 4 + k : 5 + k] == names).astype(f32)
        return m

    def spread(block_rows, code):
        s = jnp.where(live, dot(block_rows, full[...], 1, 1) * scale, -1e30)
        top = jnp.max(s, axis=1, keepdims=True)
        ex = jnp.exp(s - top)
        m = jnp.where(live, marks(code, name), 0.0)
        return top, ex, jnp.sum(ex, axis=1, keepdims=True), m, jnp.sum(m * ex, axis=1, keepdims=True)

    row = lax.broadcasted_iota(jnp.int32, (16, 1), 0)
    top, ex, z, m, pz = spread(own, own_code)
    loss_ref[...] = jnp.broadcast_to(jnp.log(z) - jnp.log(pz), loss_ref.shape)
    ds = jnp.where(row < nq, ex / z - m * ex / pz, 0.0).astype(bf16)
    dc_ref[0] = dot(ds, full[...], 1, 0) * scale
    own_pos = lax.broadcasted_iota(jnp.int32, (1, 16), 1)
    own_name = ((p["dp"] * 4 + p["t"]) * np_ + (own_pos - nq)).astype(f32)
    own_live = jnp.logical_and(own_pos >= nq, own_pos < nq + np_)
    step = min(total, max(16, 131072 // total))
    dc_ref[1] = jnp.zeros((16, D), f32)

    def block_of(i):
        r = pl.ds(pl.multiple_of(i * step, 16), step)
        rows_ = full[r, :]
        code = codes[r, :]
        top, _, z, _, pz = spread(rows_, code)
        e_ = jnp.exp(dot(rows_, own, 1, 1) * scale - top)
        real = lax.broadcasted_iota(jnp.int32, (step, 1), 0) % 16 < nq
        ds = jnp.where(jnp.logical_and(real, own_live), e_ / z - marks(code, own_name) * e_ / pz, 0.0).astype(bf16)
        dc_ref[1] += dot(ds, rows_, 0, 0) * scale

    loop(total // step, block_of)
    for cp in keeps:
        cp.wait()
    for cp in started:
        cp.wait_send()


def forward(io, up, down, bias_rows, xs_, vec, code, sizes, n, cid=1):
    dma = pltpu.SemaphoreType.DMA
    vm = lambda s, t=bf16: pltpu.VMEM(s, t)
    shapes = [made_shapes(z) for z in sizes]
    kind = lambda k: f32 if k in ("i1", "i2") else bf16
    tok = [a * b for a, b in sizes]
    outs = [SDS(shapes[e][k], kind(k)) for e in (0, 1) for k in MADE]
    scratch = [vm(shapes[e][k], kind(k)) for e in (0, 1) for k in MADE]
    for t in tok:
        scratch += [vm((t, D), f32), vm((t, D), f32)]
    return pl.pallas_call(
        functools.partial(front_kernel, n, sizes),
        out_shape=[SDS((2, 2, CH, D, D), bf16), SDS((2, 16, D), f32), SDS((16, 128), f32)] + outs,
        in_specs=[ANY] * 3 + [VM] * 7,
        out_specs=[ANY, VM, VM] + [ANY] * 22,
        scratch_shapes=scratch + [vm(s) for s in W_SHAPES] + [
            vm((2, 2, 16, D)), vm((2, 3, 16, D)), vm((2, D, D)), vm((4 * n * 16, HALF)), vm((4 * n * 16, D)), vm((4 * n * 16, 128), f32), vm((16, HALF)), dma((24,)), dma((2, 11))]
        + [dma((NP_,))] * 10 + [dma((CH,))] * 2 + [dma((NP_, 4))] * 2 + [dma((3,))] * 2 + [dma((CH,))] * 2 + [dma((n - 1,))] * 2 + [dma((3,))] * 2 + [dma((NP_,))] * 2,
        compiler_params=pltpu.CompilerParams(collective_id=cid, has_side_effects=True, vmem_limit_bytes=VMEM_LIMIT),
    )(io, up, down, bias_rows, *xs_, *vec, code)


def body(n_dp, questions, passages, question_cotangent, passage_cotangent, positives, positive_counts,
         attention_in, attention_bias, attention_out, branch_biases, norm_gains, norm_shifts, up_weight, up_bias, down_weight):
    q4 = D // 4
    nq = questions.shape[0]
    sizes = (questions.shape[:2], passages.shape[:2])
    io = jnp.concatenate([attention_in.transpose(0, 1, 3, 2).reshape(2, 3 * q4, D), attention_out], axis=1)
    own_columns = jnp.arange(D, dtype=jnp.int32)[None, :] // q4 == lax.axis_index("tensor")
    att_rows = jnp.where(own_columns, jnp.tile(attention_bias.reshape(4, q4), (1, 4)), 0.0)
    bias_rows = jnp.concatenate([att_rows.astype(bf16), up_bias, jnp.zeros((10, D), bf16)])
    vec = (norm_gains, norm_shifts, branch_biases)
    slots = positives.shape[1]
    live = jnp.arange(slots, dtype=jnp.int32)[None, :] < positive_counts[:, None]
    named = jnp.where(live, positives, -16)
    code = jnp.concatenate([named // 16, named % 16], axis=1)
    code = jnp.pad(code, ((2 * (nq + passages.shape[0]), 16 - 3 * nq - 2 * passages.shape[0]), (0, HALF - 2 * slots))).astype(f32)
    xs_ = (questions.reshape(-1, D), passages.reshape(-1, D))
    weights, dc, losses, *made = forward(io, up_weight, down_weight, bias_rows, xs_, vec, code, sizes, n_dp)
    kept = []
    for e, cot in enumerate((question_cotangent, passage_cotangent)):
        kept.append(dict(zip(MADE, made[11 * e : 11 * e + 11]), cot=cot.reshape(-1, D), x=xs_[e]))
    down_g, up_g, in_g, wo_g, own_rows, _, branch_g, gains_g, shifts_g, *dxs = backward(weights, dc, vec, kept, sizes, n_dp)
    own_small = own_rows[:16].astype(f32)
    att = lax.dynamic_slice_in_dim(own_small[0:4], lax.axis_index("tensor") * q4, q4, 1)
    return (
        kept[0]["y"].reshape(questions.shape), kept[1]["y"].reshape(passages.shape), losses[:nq, 0],
        dxs[0].reshape(questions.shape), dxs[1].reshape(passages.shape),
        in_g.reshape(2, 3, q4, D).transpose(0, 1, 3, 2).astype(f32), att.reshape(2, 2, q4),
        wo_g.astype(f32), branch_g, gains_g, shifts_g,
        up_g.astype(f32), own_small[4:6], down_g.astype(f32))


def solution(mesh):
    both = ("dp", "tensor")
    seq, rep = P(both, None, None), P()
    w4, w3, o3 = P(None, None, None, "tensor"), P(None, None, "tensor"), P(None, "tensor", None)
    in_specs = (seq, seq, seq, seq, P(both, None), P(both), w4, w3, o3, rep, rep, rep, w3, P(None, "tensor"), o3)
    out_specs = (seq, seq, P(both), seq, seq, w4, w3, o3, rep, rep, rep, w3, P(None, "tensor"), o3)
    return jax.shard_map(functools.partial(body, mesh.shape["dp"]), mesh=mesh, in_specs=in_specs, out_specs=out_specs, check_vma=False)
```
